256 devices in a mesh: seq: 8 (over z), grp: 32 (over y, x, core).
Axes of the slice: x: 4, y: 4, z: 8, core: 2. Of those that a mesh axis runs over, the one named last changes fastest.
Arguments:
- history: bfloat16 [32, 1024, 512], P('grp', 'seq'), may hold values from -6 to 6
- lengths: int32 [32], P('grp'), may hold values from 256 to 1024, as said below
- next_items: int32 [32, 1024], P('grp', 'seq'), may hold values from 0 to 2047
- negatives: int32 [32, 512], P('grp'), may hold values from 0 to 2047
- input_weight: bfloat16 [512, 2048], replicated, may hold values from -0.25 to 0.25
- output_weight: bfloat16 [512, 512], replicated, may hold values from -0.25 to 0.25
- pool_features: bfloat16 [2048, 1024], P('grp'), may hold values from -6 to 6
- tower_first: bfloat16 [1024, 1024], P('grp'), may hold values from -0.1875 to 0.1875
- tower_middle: bfloat16 [1024, 1024], P('grp'), may hold values from -0.1875 to 0.1875
- tower_last: bfloat16 [1024, 512], P('grp'), may hold values from -0.1875 to 0.1875
Outputs:
- layer_out: bfloat16 [32, 1024, 512], P('grp', 'seq')
- loss: float32 [], replicated
- user_grad: float32 [32, 1024, 512], P('grp', 'seq')
- grad_first: float32 [1024, 1024], P('grp')
- grad_middle: float32 [1024, 1024], P('grp')
- grad_last: float32 [1024, 512], P('grp')
The draws below stay inside these ranges and needn't reach their ends.
Inputs may be any that keep to these rules, and one draw needn't show every extreme that they name: `lengths`: each user's history holds 256 to 1024 events; in every draw one user has exactly 1024 and another exactly 256.
All inputs are finite; a program needn't handle non-finite values.
Results may differ from the reference program's by a relative error of at most 0.017.
Values may be sent and summed in bfloat16 or wider, within the bound.
A program may use at most 64 MiB of HBM per device.

```python
import math
import jax
import jax.numpy as jnp
import numpy as np
from jax import lax

D = 512
H = 8
DH = 64
F = 1024
DI = 1024
NEG = 512
POOL = 2048
L = 1024
USERS = 32
HD = 512


def draw_lengths(key, part):
    key = jax.random.fold_in(key, 7)
    draw_key, pick_key = jax.random.split(key)
    sampled = jax.random.randint(draw_key, (USERS,), L // 4, L + 1, dtype=jnp.int32)
    ranking = jax.random.permutation(pick_key, USERS)
    sampled = sampled.at[ranking[0]].set(L)
    return sampled.at[ranking[1]].set(L // 4)


def plant(drawn, key, low, top_value):
    longest = drawn.shape.index(max(drawn.shape))
    spots = []
    for shift in (0, 1):
        where = [jax.random.randint(jax.random.fold_in(key, axis), (), 0, length) for axis, length in enumerate(drawn.shape)]
        where[longest] = (where[longest] + shift) % drawn.shape[longest]
        spots.append(tuple(where))
    return drawn.at[spots[0]].set(low).at[spots[1]].set(top_value)


def levels(rng, dims, cuts, low, largest):
    factor_of = 1.0
    for axis_at, shards_of in cuts:
        draws = jax.random.uniform(jax.random.fold_in(jax.random.fold_in(rng, 6), axis_at), (shards_of,), jnp.float32, low / len(cuts), largest / len(cuts))
        factor_of = factor_of * jnp.repeat(jnp.exp(draws), dims[axis_at] // shards_of).reshape((-1,) + (1,) * (len(dims) - 1 - axis_at))
    return factor_of


def rank_bounds(number_of, lean):
    weights = [(1 << 20) // math.isqrt(standing ** lean) + 1 for standing in range(1, number_of + 1)]
    deviation = 1 + sum(weights) // (1 << 30)
    return np.cumsum(np.array([max(1, weight // deviation) for weight in weights]))


def ranked_ids(key, shape, count, lean):
    listing = rank_bounds(count, lean)
    lot = jax.random.randint(jax.random.fold_in(key, 1), shape, 0, int(listing[count - 1]))
    standing = jnp.searchsorted(jnp.asarray(listing, jnp.int32), lot, side="right")
    return jax.random.permutation(jax.random.fold_in(key, 2), count)[standing].astype(jnp.int32)


def noise(key, dims, deviation, most, shards=(), held_as=jnp.bfloat16):
    drawn = jax.random.normal(key, dims, jnp.float32) * deviation
    if len(shards) > 0:
        drawn = levels(key, dims, shards, -0.22, 0.18) * drawn
    return jnp.clip(drawn, min=-most, max=most).astype(held_as)


def setup_inputs(seed: int = 0) -> dict:
    arg_keys = jax.random.split(jax.random.key(seed), 11)
    return {
        "history": noise(arg_keys[0], (USERS, L, D), 1.0, 6.0, ((0, 32), (1, 8))),
        "lengths": draw_lengths(jax.random.fold_in(arg_keys[10], 71), 0),
        "next_items": plant(ranked_ids(arg_keys[2], (USERS, L), POOL, 2), jax.random.fold_in(arg_keys[2], 3), 0, POOL - 1).astype(jnp.int32),
        "negatives": plant(jax.random.randint(arg_keys[3], (USERS, NEG), 0, POOL), jax.random.fold_in(arg_keys[3], 1), 0, POOL - 1).astype(jnp.int32),
        "input_weight": noise(arg_keys[4], (D, 4 * HD), D ** -0.5, 0.25),
        "output_weight": noise(arg_keys[5], (HD, D), HD ** -0.5, 0.25),
        "pool_features": noise(arg_keys[6], (POOL, DI), 1.0, 6.0, ((0, 32),)),
        "tower_first": noise(arg_keys[7], (DI, F), DI ** -0.5, 0.1875, ((0, 32),)),
        "tower_middle": noise(arg_keys[8], (F, F), F ** -0.5, 0.1875, ((0, 32),)),
        "tower_last": noise(arg_keys[9], (F, D), F ** -0.5, 0.1875, ((0, 32),)),
    }


epsilon_norm = 1e-05
epsilon_unit = 1e-06
inverse_temp = 20.0

def layer_norm(values):
    center = values - lax.optimization_barrier(jnp.mean(values, axis=-1, keepdims=True))
    spread = lax.optimization_barrier(jnp.mean(center * center, axis=-1, keepdims=True))
    return center * lax.rsqrt(spread + epsilon_norm)

def silu_slope(preact):
    sigma = jax.nn.sigmoid(preact)
    return sigma * (1.0 + preact * (1.0 - sigma))

def tower_forward(features, first_weight, middle_weight, last_weight):
    pre_first = jnp.dot(features, first_weight, preferred_element_type=jnp.float32)
    hidden_first = jax.nn.silu(pre_first).astype(jnp.bfloat16)
    pre_second = jnp.dot(hidden_first, middle_weight, preferred_element_type=jnp.float32)
    hidden_second = jax.nn.silu(pre_second).astype(jnp.bfloat16)
    raw_item = jnp.dot(hidden_second, last_weight, preferred_element_type=jnp.float32)
    item_inverse = lax.rsqrt(lax.optimization_barrier(jnp.sum(raw_item * raw_item, axis=-1, keepdims=True)) + epsilon_unit)
    return (pre_first, hidden_first, pre_second, hidden_second, raw_item * item_inverse, item_inverse)

def sample_loss(layer_out, length, items, negative_row, pool_emb, positions):
    outward = layer_out.astype(jnp.float32)
    user_inverse = lax.rsqrt(lax.optimization_barrier(jnp.sum(outward * outward, axis=-1, keepdims=True)) + epsilon_unit)
    unit_user = outward * user_inverse
    unit_low = unit_user.astype(jnp.bfloat16)
    positive_rows = jnp.take(pool_emb, items, axis=0)
    negative_rows = jnp.take(pool_emb, negative_row, axis=0)
    positive_logit = inverse_temp * lax.optimization_barrier(jnp.sum(unit_low.astype(jnp.float32) * positive_rows.astype(jnp.float32), axis=-1))
    negative_logit = inverse_temp * jnp.dot(unit_low, negative_rows.T, preferred_element_type=jnp.float32)
    kept = (negative_row[None, :] != items[:, None]).astype(jnp.float32)
    positive_exp = jnp.exp(positive_logit)
    negative_exp = jnp.exp(negative_logit) * kept
    denominator = positive_exp + lax.optimization_barrier(jnp.sum(negative_exp, axis=-1))
    valid = (positions < length - 1).astype(jnp.float32)
    token_loss = jnp.log(denominator) - positive_logit
    loss_sum = jnp.sum(valid * token_loss)
    positive_slope = valid * (positive_exp / denominator - 1.0)
    negative_slope = (valid[:, None] * negative_exp / denominator[:, None]).astype(jnp.bfloat16)
    user_dir = inverse_temp * (positive_slope[:, None] * positive_rows.astype(jnp.float32) + jnp.dot(negative_slope, negative_rows, preferred_element_type=jnp.float32))
    user_grad = user_inverse * (user_dir - unit_user * lax.optimization_barrier(jnp.sum(unit_user * user_dir, axis=-1, keepdims=True)))
    pool_term = jnp.zeros((pool_emb.shape[0], pool_emb.shape[1]), jnp.float32)
    pool_term = pool_term.at[items].add(inverse_temp * positive_slope[:, None] * unit_low.astype(jnp.float32))
    negative_part = lax.dot_general(negative_slope, unit_low, (((0,), (0,)), ((), ())), preferred_element_type=jnp.float32)
    pool_term = pool_term.at[negative_row].add(inverse_temp * negative_part)
    return (loss_sum, user_grad, pool_term)

def outer_product(left, right):
    return lax.dot_general(left, right, (((0,), (0,)), ((), ())), preferred_element_type=jnp.float32)

def reference(history, lengths, next_items, negatives, input_weight, output_weight, pool_features, tower_first, tower_middle, tower_last):
    pre_first, hidden_first, pre_second, hidden_second, unit_item, item_inverse = tower_forward(pool_features, tower_first, tower_middle, tower_last)
    pool_emb = unit_item.astype(jnp.bfloat16)
    positions = jnp.arange(L, dtype=jnp.int32)
    score_scale = DH ** (-0.5)

    def user_step(carry, inputs):
        pool_sum, loss_acc = carry
        history_row, length, items, negative_row = inputs
        normed = layer_norm(history_row.astype(jnp.float32)).astype(jnp.bfloat16)
        projected = jax.nn.silu(jnp.dot(normed, input_weight, preferred_element_type=jnp.float32)).astype(jnp.bfloat16)
        gate = projected[:, :HD]
        head_major = jnp.transpose(projected[:, HD:].reshape(L, H, 3 * DH), (1, 0, 2))
        allowed = (positions[None, :] <= positions[:, None]) & (positions[None, :] < length) & (positions[:, None] < length)

        def one_head(head_block):
            queries = head_block[:, :DH].astype(jnp.float32)
            keys_all = head_block[:, DH:2 * DH].astype(jnp.float32)
            values_all = head_block[:, 2 * DH:].astype(jnp.float32)
            scores = jnp.dot(queries, keys_all.T, preferred_element_type=jnp.float32) * score_scale
            weights = jnp.where(allowed, jax.nn.silu(scores), 0.0) / length.astype(jnp.float32)
            weights = weights.astype(jnp.bfloat16).astype(jnp.float32)
            return jnp.dot(weights, values_all, preferred_element_type=jnp.float32).astype(jnp.bfloat16)
        attended = jnp.transpose(lax.map(one_head, head_major), (1, 0, 2)).reshape(L, HD)
        branch = (layer_norm(attended.astype(jnp.float32)) * gate.astype(jnp.float32)).astype(jnp.bfloat16)
        layer_out = (history_row.astype(jnp.float32) + jnp.dot(branch, output_weight, preferred_element_type=jnp.float32)).astype(jnp.bfloat16)
        loss_sum, user_grad, pool_term = sample_loss(layer_out, length, items, negative_row, pool_emb, positions)
        return ((pool_sum + pool_term, loss_acc + loss_sum), (layer_out, user_grad))
    start_carry = (jnp.zeros((POOL, D), jnp.float32), jnp.zeros((), jnp.float32))
    (pool_grad, loss_total), (layer_out, user_grad) = lax.scan(user_step, start_carry, (history, lengths, next_items, negatives))
    count = jnp.sum(lengths - 1).astype(jnp.float32)
    loss = loss_total / count
    raw_grad = (item_inverse * (pool_grad - unit_item * lax.optimization_barrier(jnp.sum(unit_item * pool_grad, axis=-1, keepdims=True)))).astype(jnp.bfloat16)
    grad_last = outer_product(hidden_second, raw_grad)
    second_grad = (jnp.dot(raw_grad, tower_last.T, preferred_element_type=jnp.float32) * silu_slope(pre_second)).astype(jnp.bfloat16)
    grad_middle = outer_product(hidden_first, second_grad)
    first_grad = (jnp.dot(second_grad, tower_middle.T, preferred_element_type=jnp.float32) * silu_slope(pre_first)).astype(jnp.bfloat16)
    grad_first = outer_product(pool_features, first_grad)
    return (layer_out, loss, user_grad, grad_first, grad_middle, grad_last)
```

```python
import functools

import jax
import jax.numpy as jnp
from jax import lax
from jax.experimental import pallas as pl
from jax.experimental.pallas import tpu as pltpu
from jax.sharding import PartitionSpec as P

DH = 64
EPS_NORM = 1e-05
EPS_UNIT = 1e-06
TEMP = 20.0

MESH = pl.DeviceIdType.MESH
BF = jnp.bfloat16
F32 = jnp.float32

A, B, AS, BS, QKV, ATT, H1, H2, PES, ZR, ZG, PP, G1, G2, F1, F2, RS = range(17)
PE, PAIR = 17, 20
N_SEM = 24


def silu(x):
    half = 0.5 * x
    return half * (1.0 + jnp.tanh(half))


def silu_slope(z):
    sigma = 0.5 * (1.0 + jnp.tanh(0.5 * z))
    return sigma * (1.0 + z * (1.0 - sigma))


def layer_norm(values):
    center = values - jnp.mean(values, axis=-1, keepdims=True)
    spread = jnp.mean(center * center, axis=-1, keepdims=True)
    return center * lax.rsqrt(spread + EPS_NORM)


def dot(a, b):
    return jnp.dot(a, b, preferred_element_type=F32)


def dot_t(a, b):
    return lax.dot_general(a, b, (((1,), (1,)), ((), ())), preferred_element_type=F32)


def t_dot(a, b):
    return lax.dot_general(a, b, (((0,), (0,)), ((), ())), preferred_element_type=F32)


def wait(ref, sem):
    pltpu.make_async_copy(ref, ref, sem).wait()


def kernel(
    S, G,
    len_ref, hist, nxt, neg, win, wout, xf, w1, w2, w3,
    lo_ref, loss_ref, ug_ref, gf_ref, gm_ref, gl_ref,
    send, recv,
    a_buf, b_buf, qs_buf, qr_buf, gate, k_scr, q_scr, v_scr, at_send, at_recv,
    h1_buf, h2_buf, pre1, pre2, ui, inv, pe_buf, em, sl, pt_send, pair_recv, rs_send, rs_recv,
    zs_send, zs_recv, zg_buf, rg, p_send, p_recv, gl_scr, g1_send, g1_recv, g2_send, g2_recv,
    f1_buf, f2_buf, cnt, uu, uinv,
):
    C = G // 2
    s = lax.axis_index("seq")
    g = lax.axis_index("grp")
    p = g // 2
    c = g % 2
    tok = hist.shape[0]
    length = len_ref[0]

    def z_partner(k):
        return lax.rem(s + k, S)

    def copy(src, dst, i, dev, j=None):
        return pltpu.make_async_remote_copy(
            src_ref=src, dst_ref=dst, send_sem=send.at[i if j is None else j],
            recv_sem=recv.at[i if j is None else j], device_id=dev, device_id_type=MESH)

    def z_bcast(buf, i):
        def step(k, _):
            copy(buf.at[s], buf.at[s], i, (z_partner(k), g)).start()
            return 0
        lax.fori_loop(1, S, step, 0)

    def z_scatter(src, dst, i):
        def step(k, _):
            t = z_partner(k)
            copy(src.at[t], dst.at[s], i, (t, g)).start()
            return 0
        lax.fori_loop(1, S, step, 0)

    def grp_scatter(src, dst, i):
        def step(k, _):
            t = lax.rem(g + k, G)
            copy(src.at[t], dst.at[g], i, (s, t)).start()
            return 0
        lax.fori_loop(1, G, step, 0)

    barrier = pltpu.get_barrier_semaphore()

    def greet_grp(k, _):
        pl.semaphore_signal(barrier, inc=1, device_id=(s, lax.rem(g + k, G)), device_id_type=MESH)
        return 0

    def greet_seq(k, _):
        pl.semaphore_signal(barrier, inc=1, device_id=(z_partner(k), g), device_id_type=MESH)
        return 0

    lax.fori_loop(1, G, greet_grp, 0)
    lax.fori_loop(1, S, greet_seq, 0)

    cols = pl.ds(pl.multiple_of(s * 128, 128), 128)
    rows = w1.shape[0]
    a_buf[p, c, :rows] = w1[:, cols]
    a_buf[p, c, rows:] = w2[:, cols]
    b_buf[p, c] = w3[...]
    pl.semaphore_wait(barrier, (G - 1) + (S - 1))

    def a_step(k, _):
        t = lax.rem(p + k, C)
        copy(a_buf.at[p, c], a_buf.at[p, c], A, (s, 2 * t + c)).start()
        return 0

    lax.fori_loop(1, C, a_step, 0)

    events = hist[...].astype(F32)
    normed = layer_norm(events).astype(BF)
    gate[...] = silu(dot(normed, win[:, :512])).astype(BF)
    for j in range(4):
        x = silu(dot(normed, win[:, 512 + 384 * j : 512 + 384 * (j + 1)])).astype(BF)
        for e in (0, 1):
            o = 192 * e
            qs_buf[2 * j + e, :tok] = x[:, o : o + 128]
            v = x[:, o + 128 : o + 192]
            qs_buf[2 * j + e, tok:] = jnp.concatenate([v[: tok // 2], v[tok // 2 :]], axis=1)
    z_scatter(qs_buf, qr_buf, QKV)
    qr_buf[s] = qs_buf[s]

    def b_step(k, _):
        t = lax.rem(p + k, C)
        copy(b_buf.at[p, c], b_buf.at[p, c], B, (s, 2 * t + c)).start()
        return 0

    lax.fori_loop(1, C, b_step, 0)

    sib = (s, 2 * p + 1 - c)
    wait(a_buf.at[pl.ds(0, C - 1), 0], recv.at[A])
    copy(a_buf.at[:, c], a_buf.at[:, c], AS, sib).start()

    ids = neg[...]
    n_hi = cnt.shape[0]
    oh_hi = (lax.broadcasted_iota(jnp.int32, (n_hi, ids.shape[1]), 0) == (ids >> 7)).astype(F32).astype(BF)
    oh_lo = (lax.broadcasted_iota(jnp.int32, (128, ids.shape[1]), 0) == (ids & 127)).astype(F32).astype(BF)
    cnt[...] = dot_t(oh_hi, oh_lo)

    wait(a_buf.at[:, 0], recv.at[AS])
    x_own = xf[...]
    z1 = dot(x_own, a_buf[:, :, :rows].reshape(2 * C * rows, 128))
    pre1[...] = z1
    h1_buf[s] = silu(z1).astype(BF)
    z_bcast(h1_buf, H1)

    wait(qr_buf.at[pl.ds(0, S - 1)], recv.at[QKV])
    for j in range(S):
        x = qr_buf[j]
        q_scr[tok * j : tok * (j + 1)] = x[:tok, :DH]
        k_scr[tok * j : tok * (j + 1)] = x[:tok, DH:]
        v_scr[tok * j : tok * (j + 1)] = jnp.concatenate([x[tok:, :DH], x[tok:, DH:]], axis=0)

    inv_len = 1.0 / jnp.full((1, 1), length, jnp.int32).astype(F32)
    W = 256

    def attend(b):
        q = q_scr[W * b : W * (b + 1)]
        acc = jnp.zeros((W, DH), F32)
        for kb in range(b + 1):
            half = dot_t(q, k_scr[W * kb : W * (kb + 1)]) * (0.5 * DH ** (-0.5))
            w = (half * inv_len) * (1.0 + jnp.tanh(half))
            if kb == b:
                r = lax.broadcasted_iota(jnp.int32, (W, W), 0)
                cc = lax.broadcasted_iota(jnp.int32, (W, W), 1)
                w = jnp.where(cc <= r, w, 0.0)
            acc = acc + dot(w.astype(BF), v_scr[W * kb : W * (kb + 1)])
        pos = W * b + lax.broadcasted_iota(jnp.int32, (W, 1), 0)
        acc = jnp.where(pos < length, acc, 0.0).astype(BF)
        for i in range(W // tok):
            o = acc[tok * i : tok * (i + 1)]
            at_send[(W // tok) * b + i] = jnp.concatenate([o[: tok // 2], o[tok // 2 :]], axis=1)

    n_blocks = S * tok // W
    for b in range(n_blocks // 2, n_blocks):
        attend(b)

    wait(h1_buf.at[pl.ds(0, S - 1)], recv.at[H1])
    h1 = jnp.concatenate([h1_buf[j] for j in range(S)], axis=1)
    z2 = dot(h1, a_buf[:, :, rows:].reshape(2 * C * rows, 128))
    pre2[...] = z2
    h2_buf[s] = silu(z2).astype(BF)
    z_bcast(h2_buf, H2)

    for b in range(n_blocks // 2):
        attend(b)
    z_scatter(at_send, at_recv, ATT)
    at_recv[s] = at_send[s]

    wait(b_buf.at[pl.ds(0, C - 1), 0], recv.at[B])
    copy(b_buf.at[:, c], b_buf.at[:, c], BS, sib).start()

    wait(h2_buf.at[pl.ds(0, S - 1)], recv.at[H2])
    wait(b_buf.at[:, 0], recv.at[BS])
    h2 = jnp.concatenate([h2_buf[j] for j in range(S)], axis=1)
    raw = dot(h2, b_buf[...].reshape(2 * C * rows, 512))
    item_inverse = lax.rsqrt(jnp.sum(raw * raw, axis=-1, keepdims=True) + EPS_UNIT)
    unit_item = raw * item_inverse
    ui[...] = unit_item
    inv[...] = jnp.broadcast_to(item_inverse, inv.shape)
    pe_buf[p, c] = unit_item.astype(BF)

    copy(pe_buf.at[p, c], pe_buf.at[p, c], PES, sib).start()
    per = (C - 1) // 3

    def pe_step(k, _):
        t = lax.rem(p + k, C)
        grp = (k - 1) // per
        copy(pe_buf.at[p, c], pe_buf.at[p, c], 0, (s, 2 * t + c), PE + grp).start()
        return 0

    lax.fori_loop(1, C, pe_step, 0)

    wait(at_recv.at[pl.ds(0, S - 1)], recv.at[ATT])
    tops, bottoms = [], []
    for h in range(S):
        x = at_recv[h]
        tops.append(x[:, :DH])
        bottoms.append(x[:, DH:])
    merged = jnp.concatenate(
        [jnp.concatenate(tops, axis=1), jnp.concatenate(bottoms, axis=1)], axis=0).astype(F32)
    branch = (layer_norm(merged) * gate[...].astype(F32)).astype(BF)
    layer_out = (hist[...].astype(F32) + dot(branch, wout[...])).astype(BF)
    lo_ref[...] = layer_out
    outward = layer_out.astype(F32)
    user_inverse = lax.rsqrt(jnp.sum(outward * outward, axis=-1, keepdims=True) + EPS_UNIT)
    unit_user = outward * user_inverse
    unit_low = unit_user.astype(BF)
    uu[...] = unit_user
    uinv[...] = jnp.broadcast_to(user_inverse, uinv.shape)

    for j in range(3):
        wait(pe_buf.at[pl.ds(0, per), 0], recv.at[PE + j])

        def fwd(k, _):
            t = lax.rem(p + C - k, C)
            copy(pe_buf.at[t, c], pe_buf.at[t, c], PES, sib).start()
            return 0

        lax.fori_loop(1 + per * j, 1 + per * (j + 1), fwd, 0)

    eye = lax.broadcasted_iota(jnp.int32, (tok, tok), 0) == lax.broadcasted_iota(jnp.int32, (tok, tok), 1)
    items = jnp.sum(
        jnp.where(eye, jnp.broadcast_to(nxt[...].astype(F32), (tok, tok)), 0.0), axis=1, keepdims=True
    ).astype(jnp.int32)
    positions = s * tok + lax.broadcasted_iota(jnp.int32, (tok, 1), 0)
    valid = (positions < length - 1).astype(F32)

    wait(pe_buf.at[:, 0], recv.at[PES])

    Q = 4
    CQ = C // Q
    width = pe_buf.shape[0] * 2 * pe_buf.shape[2] // Q
    den = jnp.zeros((tok, 1), F32)
    positive = jnp.zeros((tok, 1), F32)
    for q in range(Q):
        rows_q = pe_buf[CQ * q : CQ * (q + 1)].reshape(width, 512)
        logit = TEMP * dot_t(unit_low, rows_q)
        r_id = width * q + lax.broadcasted_iota(jnp.int32, (tok, width), 1)
        own = r_id == items
        times = jnp.concatenate(
            [cnt[i : i + 1] for i in range(q * width // 128, (q + 1) * width // 128)], axis=1)
        e = jnp.where(own, 0.0, jnp.exp(logit) * times)
        em[q] = e
        den = den + jnp.sum(e, axis=1, keepdims=True)
        positive = positive + jnp.sum(jnp.where(own, logit, 0.0), axis=1, keepdims=True)
    positive_exp = jnp.exp(positive)
    den = den + positive_exp
    slope = valid * (positive_exp / den - 1.0)
    scale = valid / den
    loss_sum = jnp.sum(valid * (jnp.log(den) - positive))

    for q in range(Q):
        gq = lax.rem(p // CQ + q, Q)
        r_id = width * gq + lax.broadcasted_iota(jnp.int32, (tok, width), 1)
        sm = jnp.where(r_id == items, slope, scale * em[gq]).astype(BF)
        sl[gq] = sm
        term = (TEMP * t_dot(sm, unit_low)).astype(BF)
        pt_send[pl.ds(CQ * gq, CQ)] = term.reshape(CQ, 2, pe_buf.shape[2], 512)
        copy(pt_send.at[pl.ds(CQ * gq, CQ), 1 - c], pair_recv.at[pl.ds(CQ * gq, CQ)], 0, sib, PAIR + q).start()

    for q in range(Q):
        gq = lax.rem(p // CQ + q, Q)
        wait(pair_recv.at[pl.ds(CQ * gq, CQ)], recv.at[PAIR + q])
        both = pt_send[pl.ds(CQ * gq, CQ), c].astype(F32) + pair_recv[pl.ds(CQ * gq, CQ)].astype(F32)
        rs_send[pl.ds(CQ * gq, CQ)] = both.astype(BF)

        def rs_step(i, _):
            t = CQ * gq + lax.rem(p + i, CQ)

            @pl.when(t != p)
            def _():
                copy(rs_send.at[t], rs_recv.at[p], RS, (s, 2 * t + c)).start()
            return 0

        lax.fori_loop(0, CQ, rs_step, 0)

    user_dir = jnp.zeros((tok, 512), F32)
    for q in range(Q):
        user_dir = user_dir + dot(sl[q], pe_buf[CQ * q : CQ * (q + 1)].reshape(width, 512))
    user_dir = TEMP * user_dir
    uun = uu[...]
    ug_ref[...] = uinv[:, :1] * (user_dir - uun * jnp.sum(uun * user_dir, axis=-1, keepdims=True))

    wait(rs_recv.at[pl.ds(0, C - 1)], recv.at[RS])
    rs_recv[p] = rs_send[p]
    part = jnp.sum(rs_recv[...].astype(F32), axis=0)
    lane = lax.broadcasted_iota(jnp.int32, (8, 128), 1)
    count = jnp.full((8, 128), length - 1, jnp.int32).astype(F32)
    tail = jnp.where(lane == 0, loss_sum, jnp.where(lane == 1, count, 0.0))
    for t in range(S):
        zs_send[t, :, :512] = part[8 * t : 8 * (t + 1)]
        zs_send[t, :, 512:] = tail
    z_scatter(zs_send, zs_recv, ZR)
    wait(zs_recv.at[pl.ds(0, S - 1)], recv.at[ZR])
    zs_recv[s] = zs_send[s]
    total = zs_recv[0]
    for t in range(1, S):
        total = total + zs_recv[t]
    own_grad = total[:, :512]
    own_rows = pl.ds(pl.multiple_of(s * 8, 8), 8)
    ui8 = ui[own_rows]
    raw8 = inv[own_rows][:, :1] * (own_grad - ui8 * jnp.sum(ui8 * own_grad, axis=-1, keepdims=True))
    zg_buf[s] = raw8.astype(BF).astype(F32)
    z_bcast(zg_buf, ZG)
    loss_row = total[0:1, 512:]
    loss_hi = loss_row.astype(BF).astype(F32)
    loss_lo = loss_row - loss_hi
    row16 = lax.broadcasted_iota(jnp.int32, (16, 128), 0)
    loss16 = jnp.where(row16 == 0, loss_hi, jnp.where(row16 == 1, loss_lo, 0.0)).astype(BF)
    wait(zg_buf.at[pl.ds(0, S - 1)], recv.at[ZG])
    raw_grad = zg_buf[...].reshape(8 * S, 512).astype(BF)
    rg[...] = raw_grad

    w3_rows = b_buf[pl.ds(128 // (2 * rows) * s, 128 // (2 * rows))].reshape(128, 512)
    sg = (dot_t(raw_grad, w3_rows) * silu_slope(pre2[...])).astype(BF)
    back = dot_t(sg, a_buf[:, :, rows:].reshape(2 * C * rows, 128)).astype(BF)
    for t in range(S):
        p_send[t] = back[:, 128 * t : 128 * (t + 1)]
    z_scatter(p_send, p_recv, PP)
    p_recv[s] = p_send[s]

    h1 = jnp.concatenate([h1_buf[j] for j in range(S)], axis=1)
    h2 = jnp.concatenate([h2_buf[j] for j in range(S)], axis=1)
    q_cols = pl.ds(pl.multiple_of(lax.rem(s, 4) * 128, 128), 128)
    half = rows // 2
    gl_scr[...] = t_dot(h2, rg[:, q_cols]).astype(BF).reshape(G, 2, half, 128)
    g1_send[:, :rows] = t_dot(h1, sg).astype(BF).reshape(G, rows, 128)
    g1_send[:, rows : rows + half] = gl_scr[:, s // 4]
    g1_send[:, rows + half :] = jnp.broadcast_to(loss16[None], (G, 16, 128))
    grp_scatter(g1_send, g1_recv, G1)
    g1_recv[g] = g1_send[g]

    wait(p_recv.at[pl.ds(0, S - 1)], recv.at[PP])
    back1 = p_recv[0].astype(F32)
    for t in range(1, S):
        back1 = back1 + p_recv[t].astype(F32)
    fg = (back1 * silu_slope(pre1[...])).astype(BF)
    g2_send[...] = t_dot(xf[...], fg).astype(BF).reshape(G, rows, 128)
    grp_scatter(g2_send, g2_recv, G2)
    g2_recv[g] = g2_send[g]

    wait(g1_recv.at[pl.ds(0, G - 1)], recv.at[G1])
    sum1 = jnp.sum(g1_recv[...].astype(F32), axis=0)
    f1_buf[s] = sum1[: rows + half].astype(BF)
    z_bcast(f1_buf, F1)
    both = sum1[rows + half : rows + half + 1] + sum1[rows + half + 1 : rows + half + 2]
    lane1 = lax.broadcasted_iota(jnp.int32, (1, 128), 1)
    numer = jnp.sum(jnp.where(lane1 == 0, both, 0.0), axis=1, keepdims=True)
    denom = jnp.sum(jnp.where(lane1 == 1, both, 0.0), axis=1, keepdims=True)
    loss_ref[...] = jnp.broadcast_to(numer * S / denom, loss_ref.shape)

    wait(g2_recv.at[pl.ds(0, G - 1)], recv.at[G2])
    f2_buf[s] = jnp.sum(g2_recv[...].astype(F32), axis=0).astype(BF)
    z_bcast(f2_buf, F2)

    wait(f1_buf.at[pl.ds(0, S - 1)], recv.at[F1])
    for t in range(S):
        gm_ref[:, 128 * t : 128 * (t + 1)] = f1_buf[t, :rows].astype(F32)
        gl_ref[half * (t // 4) : half * (t // 4 + 1), 128 * (t % 4) : 128 * (t % 4 + 1)] = f1_buf[t, rows:].astype(F32)

    wait(a_buf.at[pl.ds(0, C - 1), 0], send.at[A])
    wait(b_buf.at[pl.ds(0, C - 1), 0], send.at[B])
    wait(a_buf.at[:, 0], send.at[AS])
    wait(b_buf.at[:, 0], send.at[BS])
    wait(pe_buf.at[:, 0], send.at[PES])
    for j in range(3):
        wait(pe_buf.at[pl.ds(0, per), 0], send.at[PE + j])
    for q in range(Q):
        wait(pair_recv.at[pl.ds(0, CQ)], send.at[PAIR + q])
    wait(rs_recv.at[pl.ds(0, C - 1)], send.at[RS])
    for buf, i in ((qr_buf, QKV), (at_recv, ATT), (h1_buf, H1), (h2_buf, H2), (zs_recv, ZR), (zg_buf, ZG),
                   (p_recv, PP), (f1_buf, F1)):
        wait(buf.at[pl.ds(0, S - 1)], send.at[i])
    wait(g1_recv.at[pl.ds(0, G - 1)], send.at[G1])
    wait(g2_recv.at[pl.ds(0, G - 1)], send.at[G2])

    wait(f2_buf.at[pl.ds(0, S - 1)], recv.at[F2])
    for t in range(S):
        gf_ref[:, 128 * t : 128 * (t + 1)] = f2_buf[t].astype(F32)
    wait(f2_buf.at[pl.ds(0, S - 1)], send.at[F2])


def local(history, lengths, next_items, negatives, input_weight, output_weight, pool_features,
          tower_first, tower_middle, tower_last, S, G):
    events = history[0]
    tok = events.shape[0]
    C = G // 2
    R = pool_features.shape[0]
    rows = tower_first.shape[0]
    V = pltpu.VMEM
    vmem = pl.BlockSpec(memory_space=pltpu.VMEM)
    width = 2 * C * R // 4
    scratch = [
        pltpu.SemaphoreType.DMA((N_SEM,)),
        pltpu.SemaphoreType.DMA((N_SEM,)),
        V((C, 2, 2 * rows, 128), BF),
        V((C, 2, rows, 512), BF),
        V((S, tok + tok // 2, 128), BF),
        V((S, tok + tok // 2, 128), BF),
        V((tok, 512), BF),
        V((S * tok, DH), BF),
        V((S * tok, DH), BF),
        V((S * tok, DH), BF),
        V((S, tok // 2, 128), BF),
        V((S, tok // 2, 128), BF),
        V((S, R, 128), BF),
        V((S, R, 128), BF),
        V((R, 128), F32),
        V((R, 128), F32),
        V((R, 512), F32),
        V((R, 128), F32),
        V((C, 2, R, 512), BF),
        V((4, tok, width), F32),
        V((4, tok, width), BF),
        V((C, 2, R, 512), BF),
        V((C, R, 512), BF),
        V((C, R, 512), BF),
        V((C, R, 512), BF),
        V((S, 8, 640), F32),
        V((S, 8, 640), F32),
        V((S, 8, 512), F32),
        V((R, 512), BF),
        V((S, R, 128), BF),
        V((S, R, 128), BF),
        V((G, 2, rows // 2, 128), BF),
        V((G, rows + rows // 2 + 16, 128), BF),
        V((G, rows + rows // 2 + 16, 128), BF),
        V((G, rows, 128), BF),
        V((G, rows, 128), BF),
        V((S, rows + rows // 2, 128), BF),
        V((S, rows, 128), BF),
        V((2 * C * R // 128, 128), F32),
        V((tok, 512), F32),
        V((tok, 128), F32),
    ]
    lo, loss, ug, gf, gm, gl = pl.pallas_call(
        functools.partial(kernel, S, G),
        out_shape=[
            jax.ShapeDtypeStruct((tok, 512), BF),
            jax.ShapeDtypeStruct((8, 128), F32),
            jax.ShapeDtypeStruct((tok, 512), F32),
            jax.ShapeDtypeStruct((rows, 1024), F32),
            jax.ShapeDtypeStruct((rows, 1024), F32),
            jax.ShapeDtypeStruct((rows, 512), F32),
        ],
        in_specs=[pl.BlockSpec(memory_space=pltpu.SMEM)] + [vmem] * 9,
        out_specs=[vmem] * 6,
        scratch_shapes=scratch,
        compiler_params=pltpu.CompilerParams(
            collective_id=0, has_side_effects=True, vmem_limit_bytes=48 * 1024 * 1024),
    )(lengths, events, next_items, negatives, input_weight, output_weight, pool_features,
      tower_first, tower_middle, tower_last)
    return lo[None], loss[0, 0], ug[None], gf, gm, gl


def solution(mesh):
    placed = (
        P("grp", "seq", None), P("grp"), P("grp", "seq"), P("grp", None), P(), P(),
        P("grp", None), P("grp", None), P("grp", None), P("grp", None),
    )
    return jax.shard_map(
        functools.partial(local, S=mesh.shape["seq"], G=mesh.shape["grp"]),
        mesh=mesh,
        in_specs=placed,
        out_specs=(
            P("grp", "seq", None), P(), P("grp", "seq", None),
            P("grp", None), P("grp", None), P("grp", None),
        ),
        check_vma=False,
    )
```

```python
import functools

import jax
import jax.numpy as jnp
from jax import lax
from jax.experimental import pallas as pl
from jax.experimental.pallas import tpu as pltpu
from jax.sharding import PartitionSpec as P

DH = 64
EPS_NORM = 1e-05
EPS_UNIT = 1e-06
TEMP = 20.0

MESH = pl.DeviceIdType.MESH
BF = jnp.bfloat16
F32 = jnp.float32

(A, A2, B, AS, AS2, BS, QKV, ATT, H1, H2, SL2, PES, HX, NX, DN, UD, ZA, ZL, GL, G1, G2, F1, F2, RS, W2, W2S) = range(26)
PE, PAIR = 26, 29
N_SEM = 34

(I_W3, I_H, I_WIN, I_WOUT, I_X, I_NEG, I_NXT, I_W2R, O_LO, O_UG) = range(10)
I_W1, I_W2 = 10, 11
N_HERE = 15


def silu(x):
    half = 0.5 * x
    return half * (1.0 + jnp.tanh(half))


def silu_slope(z):
    sigma = 0.5 * (1.0 + jnp.tanh(0.5 * z))
    return sigma * (1.0 + z * (1.0 - sigma))


def layer_norm(values):
    center = values - jnp.mean(values, axis=-1, keepdims=True)
    spread = jnp.mean(center * center, axis=-1, keepdims=True)
    return center * lax.rsqrt(spread + EPS_NORM)


def dot(a, b):
    return jnp.dot(a, b, preferred_element_type=F32)


def dot_t(a, b):
    return lax.dot_general(a, b, (((1,), (1,)), ((), ())), preferred_element_type=F32)


def t_dot(a, b):
    return lax.dot_general(a, b, (((0,), (0,)), ((), ())), preferred_element_type=F32)


def wait(ref, sem):
    pltpu.make_async_copy(ref, ref, sem).wait()


def kernel(
    S, G,
    len_ref, hist, nxt, neg, win, wout, xf, w1, w2, w3,
    lo_ref, loss_ref, ug_ref, gf_ref, gm_ref, gl_ref,
    send, recv, here,
    h256, nx_buf, neg_v, win_v, wout_v, xf_v,
    a_buf, a2_buf, b_buf, w2r_buf, qs_buf, qr_buf, gate, k_scr, q_scr, v_scr, at_send, at_recv,
    h1_buf, h2_buf, sl2_buf, pre1, ui, inv, pe_buf, em, st, pt_send, pair_recv, rs_send, rs_recv,
    dn_send, dn_recv, ud, ud_send, ud_recv, lo_scr, zl_buf, lg_buf, za_buf, rg, sg_scr,
    gl_scr, g1_send, g1_recv, g2_send, g2_recv, f1_buf, f2_buf, cnt, uu, uinv,
):
    C = G // 2
    s = lax.axis_index("seq")
    g = lax.axis_index("grp")
    p = g // 2
    c = g % 2
    par = s % 2
    tok = h256.shape[1]
    rows = b_buf.shape[2]
    NB = a2_buf.shape[2]
    half = rows // 2
    R = xf_v.shape[0]
    RH = R // 2
    length = len_ref[0]
    pair = (s + 1 - 2 * par, g)
    sib = (s, 2 * p + 1 - c)
    cols = pl.ds(pl.multiple_of(s * 128, 128), 128)

    def copy(src, dst, i, dev):
        return pltpu.make_async_remote_copy(
            src_ref=src, dst_ref=dst, send_sem=send.at[i], recv_sem=recv.at[i],
            device_id=dev, device_id_type=MESH)

    def fetch(src, dst, i):
        pltpu.make_async_copy(src, dst, here.at[i]).start()

    def z_bcast(buf, i):
        def step(k, _):
            copy(buf.at[s], buf.at[s], i, (lax.rem(s + k, S), g)).start()
            return 0
        lax.fori_loop(1, S, step, 0)

    def chips(src, dst, i):
        def step(k, _):
            copy(src, dst, i, (s, 2 * lax.rem(p + k, C) + c)).start()
            return 0
        lax.fori_loop(1, C, step, 0)

    def grp_scatter(src, dst, i):
        def step(k, _):
            t = lax.rem(g + k, G)
            copy(src.at[t], dst.at[g], i, (s, t)).start()
            return 0
        lax.fori_loop(1, G, step, 0)

    barrier = pltpu.get_barrier_semaphore()

    def greet_grp(k, _):
        pl.semaphore_signal(barrier, inc=1, device_id=(s, lax.rem(g + k, G)), device_id_type=MESH)
        return 0

    def greet_seq(k, _):
        pl.semaphore_signal(barrier, inc=1, device_id=(lax.rem(s + k, S), g), device_id_type=MESH)
        return 0

    lax.fori_loop(1, G, greet_grp, 0)
    lax.fori_loop(1, S, greet_seq, 0)

    fetch(hist, h256.at[par], I_H)
    fetch(w1.at[:, cols], a_buf.at[p, c], I_W1)
    for j in range(NB):
        block = pl.ds(pl.multiple_of((2 * j + par) * 128, 128), 128)
        fetch(w2.at[:, block], a2_buf.at[p, c, j], I_W2 + j)
    fetch(win, win_v, I_WIN)
    fetch(nxt, nx_buf.at[par], I_NXT)
    fetch(w3, b_buf.at[p, c], I_W3)
    fetch(xf, xf_v, I_X)
    fetch(neg, neg_v, I_NEG)
    fetch(wout, wout_v, I_WOUT)
    source = p // 2 == s

    @pl.when(source)
    def _():
        fetch(w2, w2r_buf.at[p % 2, c], I_W2R)

    wait(h256.at[par], here.at[I_H])
    normed = layer_norm(h256[par].astype(F32)).astype(BF)
    wait(win_v, here.at[I_WIN])
    for j in range(4):
        x = silu(dot(normed, win_v[:, 512 + 384 * j : 512 + 384 * (j + 1)])).astype(BF)
        for e in (0, 1):
            o = 192 * e
            qs_buf[2 * j + e, :tok] = x[:, o : o + 128]
            v = x[:, o + 128 : o + 192]
            qs_buf[2 * j + e, tok:] = jnp.concatenate([v[: tok // 2], v[tok // 2 :]], axis=1)
    wait(a_buf.at[p, c], here.at[I_W1])
    for j in range(NB):
        wait(a2_buf.at[p, c, j], here.at[I_W2 + j])
    wait(nx_buf.at[par], here.at[I_NXT])
    wait(b_buf.at[p, c], here.at[I_W3])
    pl.semaphore_wait(barrier, (G - 1) + (S - 1))

    chips(a_buf.at[p, c], a_buf.at[p, c], A)

    def qkv_step(k, _):
        t = lax.rem(s + k, S)
        copy(qs_buf.at[t], qr_buf.at[s], QKV, (t, g)).start()
        return 0

    lax.fori_loop(1, S, qkv_step, 0)
    qr_buf[s] = qs_buf[s]

    def local_row(ids):
        mine = (ids // RH) % 2 == par
        return jnp.where(mine, (ids // R) * RH + ids % RH, -1)

    wait(neg_v, here.at[I_NEG])
    n_rows = G * RH
    ids = local_row(neg_v[...])
    hot = (lax.broadcasted_iota(jnp.int32, (n_rows, ids.shape[1]), 0) == ids).astype(F32).astype(BF)
    cnt[...] = dot(hot, jnp.ones((ids.shape[1], 128), BF))

    chips(a2_buf.at[p, c], a2_buf.at[p, c], A2)
    wait(xf_v, here.at[I_X])
    wait(a_buf.at[pl.ds(0, C - 1), 0], recv.at[A])
    copy(a_buf.at[:, c], a_buf.at[:, c], AS, sib).start()
    wait(a_buf.at[:, 0], recv.at[AS])
    z1 = dot(xf_v[...], a_buf[...].reshape(G * rows, 128))
    pre1[...] = z1
    h1_buf[s] = silu(z1).astype(BF)
    z_bcast(h1_buf, H1)
    def whole(buf):
        return jnp.concatenate([buf[j % 2, j // 2] for j in range(2 * NB)], axis=1)

    wait(a2_buf.at[pl.ds(0, C - 1), 0], recv.at[A2])
    copy(a2_buf.at[:, c], a2_buf.at[:, c], AS2, sib).start()
    chips(b_buf.at[p, c], b_buf.at[p, c], B)
    wait(qr_buf.at[pl.ds(0, S - 1)], recv.at[QKV])
    copy(h256.at[par], h256.at[par], HX, pair).start()
    copy(nx_buf.at[par], nx_buf.at[par], NX, pair).start()
    for j in range(S):
        x = qr_buf[j]
        q_scr[tok * j : tok * (j + 1)] = x[:tok, :DH]
        k_scr[tok * j : tok * (j + 1)] = x[:tok, DH:]
        v_scr[tok * j : tok * (j + 1)] = jnp.concatenate([x[tok:, :DH], x[tok:, DH:]], axis=0)

    inv_len = 1.0 / jnp.full((1, 1), length, jnp.int32).astype(F32)
    W = 2 * tok

    def attend(b):
        q = q_scr[W * b : W * (b + 1)]
        acc = jnp.zeros((W, DH), F32)
        for kb in range(b + 1):
            hs = dot_t(q, k_scr[W * kb : W * (kb + 1)]) * (0.5 * DH ** (-0.5))
            w = (hs * inv_len) * (1.0 + jnp.tanh(hs))
            if kb == b:
                r = lax.broadcasted_iota(jnp.int32, (W, W), 0)
                cc = lax.broadcasted_iota(jnp.int32, (W, W), 1)
                w = jnp.where(cc <= r, w, 0.0)
            acc = acc + dot(w.astype(BF), v_scr[W * kb : W * (kb + 1)])
        pos = W * b + lax.broadcasted_iota(jnp.int32, (W, 1), 0)
        acc = jnp.where(pos < length, acc, 0.0).astype(BF)
        at_send[b] = jnp.concatenate([acc[:tok], acc[tok:]], axis=1)

    for b in reversed(range(S // 2)):
        attend(b)
    at_recv[s] = at_send[s // 2]

    wait(h1_buf.at[pl.ds(0, S - 1)], recv.at[H1])
    wait(a2_buf.at[:, 0], recv.at[AS2])
    h1 = jnp.concatenate([h1_buf[j] for j in range(S)], axis=1)
    for j in range(NB):
        z2 = dot(h1, a2_buf[:, :, j].reshape(G * rows, 128))
        h2_buf[par, j] = silu(z2).astype(BF)
        sl2_buf[par, j] = silu_slope(z2).astype(BF)
    copy(h2_buf.at[par], h2_buf.at[par], H2, pair).start()

    def at_step(k, _):
        t = lax.rem(s + k, S)
        copy(at_send.at[t // 2], at_recv.at[s], ATT, (t, g)).start()
        return 0

    lax.fori_loop(1, S, at_step, 0)
    wait(h256.at[0], recv.at[HX])
    copy(sl2_buf.at[par], sl2_buf.at[par], SL2, pair).start()
    both = h256[...].reshape(2 * tok, 512)
    gate[...] = silu(dot(layer_norm(both.astype(F32)).astype(BF), win_v[:, :512])).astype(BF)

    wait(b_buf.at[pl.ds(0, C - 1), 0], recv.at[B])
    copy(b_buf.at[:, c], b_buf.at[:, c], BS, sib).start()

    wait(h2_buf.at[0], recv.at[H2])
    wait(b_buf.at[:, 0], recv.at[BS])
    h2 = whole(h2_buf)
    raw = dot(h2, b_buf[...].reshape(G * rows, 512))
    item_inverse = lax.rsqrt(jnp.sum(raw * raw, axis=-1, keepdims=True) + EPS_UNIT)
    unit_item = raw * item_inverse
    ui[...] = unit_item
    inv[...] = jnp.broadcast_to(item_inverse, inv.shape)
    pe_buf[p, c] = ui[pl.ds(pl.multiple_of(par * RH, RH), RH)].astype(BF)

    copy(pe_buf.at[p, c], pe_buf.at[p, c], PES, sib).start()
    per = (C - 1) // 3

    def pe_step(k, _):
        t = lax.rem(p + k, C)
        copy(pe_buf.at[p, c], pe_buf.at[p, c], PE + (k - 1) // per, (s, 2 * t + c)).start()
        return 0

    lax.fori_loop(1, C, pe_step, 0)

    @pl.when(source)
    def _():
        wait(w2r_buf.at[p % 2, c], here.at[I_W2R])
        chips(w2r_buf.at[p % 2, c], w2r_buf.at[p % 2, c], W2)

    wait(wout_v, here.at[I_WOUT])
    wait(at_recv.at[pl.ds(0, S - 1)], recv.at[ATT])
    tops, bottoms = [], []
    for h in range(S):
        x = at_recv[h]
        tops.append(x[:, :DH])
        bottoms.append(x[:, DH:])
    merged = jnp.concatenate(
        [jnp.concatenate(tops, axis=1), jnp.concatenate(bottoms, axis=1)], axis=0).astype(F32)
    branch = (layer_norm(merged) * gate[...].astype(F32)).astype(BF)
    layer_out = (h256[...].reshape(2 * tok, 512).astype(F32) + dot(branch, wout_v[...])).astype(BF)
    lo_scr[...] = layer_out.reshape(2, tok, 512)
    pltpu.make_async_copy(lo_scr.at[par], lo_ref, here.at[O_LO]).start()
    outward = layer_out.astype(F32)
    user_inverse = lax.rsqrt(jnp.sum(outward * outward, axis=-1, keepdims=True) + EPS_UNIT)
    unit_user = outward * user_inverse
    unit_low = unit_user.astype(BF)
    uu[...] = unit_user.reshape(2, tok, 512)
    uinv[...] = jnp.broadcast_to(user_inverse, (2 * tok, 128)).reshape(2, tok, 128)

    wait(nx_buf.at[0], recv.at[NX])
    items = local_row(jnp.concatenate([nx_buf[0], nx_buf[1]], axis=1))
    pair_pos = lax.broadcasted_iota(jnp.int32, (1, W), 1)
    positions = (s // 2) * W + pair_pos
    valid = (positions < length - 1).astype(F32)

    for j in range(3):
        wait(pe_buf.at[pl.ds(0, per), 0], recv.at[PE + j])

        def fwd(k, _):
            t = lax.rem(p + C - k, C)
            copy(pe_buf.at[t, c], pe_buf.at[t, c], PES, sib).start()
            return 0

        lax.fori_loop(1 + per * j, 1 + per * (j + 1), fwd, 0)

    wait(pe_buf.at[:, 0], recv.at[PES])

    Q = 4
    CQ = C // Q
    width = n_rows // Q
    row_id = lax.broadcasted_iota(jnp.int32, (width, W), 0)
    den = jnp.zeros((1, W), F32)
    positive = jnp.zeros((1, W), F32)
    for q in range(Q):
        logit = TEMP * dot_t(pe_buf[CQ * q : CQ * (q + 1)].reshape(width, 512), unit_low)
        own = row_id + width * q == items
        times = cnt[width * q : width * (q + 1)]
        e = jnp.where(own, 0.0, jnp.exp(logit) * jnp.concatenate([times] * (W // 128), axis=1))
        em[q] = e
        den = den + jnp.sum(e, axis=0, keepdims=True)
        positive = positive + jnp.sum(jnp.where(own, logit, 0.0), axis=0, keepdims=True)
    row8 = lax.broadcasted_iota(jnp.int32, (8, W), 0)
    dn_send[...] = jnp.where(row8 == 0, den, positive)
    copy(dn_send, dn_recv, DN, pair).start()
    wait(dn_recv, recv.at[DN])
    den = den + dn_recv[0:1]
    positive = positive + dn_recv[1:2]
    positive_exp = jnp.exp(positive)
    den = den + positive_exp
    slope = valid * (positive_exp / den - 1.0)
    scale = valid / den

    for q in range(Q):
        gq = lax.rem(p // CQ + q, Q)
        sm = jnp.where(row_id + width * gq == items, slope, scale * em[gq]).astype(BF)
        st[gq] = sm
        pt_send[pl.ds(CQ * gq, CQ)] = (TEMP * dot(sm, unit_low)).astype(BF).reshape(CQ, 2, RH, 512)
        copy(pt_send.at[pl.ds(CQ * gq, CQ), 1 - c], pair_recv.at[pl.ds(CQ * gq, CQ)], PAIR + q, sib).start()

    for q in range(Q):
        gq = lax.rem(p // CQ + q, Q)
        wait(pair_recv.at[pl.ds(CQ * gq, CQ)], recv.at[PAIR + q])
        chip_sum = pt_send[pl.ds(CQ * gq, CQ), c].astype(F32) + pair_recv[pl.ds(CQ * gq, CQ)].astype(F32)
        rs_send[pl.ds(CQ * gq, CQ)] = chip_sum.astype(BF)

        def rs_step(i, _):
            t = CQ * gq + lax.rem(p + i, CQ)

            @pl.when(t != p)
            def _():
                copy(rs_send.at[t], rs_recv.at[p], RS, (s, 2 * t + c)).start()
            return 0

        lax.fori_loop(0, CQ, rs_step, 0)

    mine = pair_pos // tok == par
    loss_sum = jnp.sum(jnp.where(mine, valid * (jnp.log(den) - positive), 0.0))
    lane = lax.broadcasted_iota(jnp.int32, (8, 128), 1)
    count = jnp.full((8, 128), length - 1, jnp.int32).astype(F32)
    zl_buf[s] = jnp.where(lane == 0, loss_sum, jnp.where(lane == 1, count, 0.0))
    z_bcast(zl_buf, ZL)

    user_dir = t_dot(st[...].reshape(n_rows, W), pe_buf[...].reshape(n_rows, 512))
    ud[...] = user_dir.reshape(2, tok, 512)
    ud_send[...] = ud[1 - par].astype(BF)
    copy(ud_send, ud_recv, UD, pair).start()

    @pl.when(source)
    def _():
        wait(w2r_buf.at[0, 0], recv.at[W2])

    @pl.when(jnp.logical_not(source))
    def _():
        wait(w2r_buf.at[:, 0], recv.at[W2])

    copy(w2r_buf.at[:, c], w2r_buf.at[:, c], W2S, sib).start()

    wait(rs_recv.at[pl.ds(0, C - 1)], recv.at[RS])
    rs_recv[p] = rs_send[p]
    za_buf[s] = jnp.sum(rs_recv[...].astype(F32), axis=0).astype(BF)
    z_bcast(za_buf, ZA)

    wait(zl_buf.at[pl.ds(0, S - 1)], recv.at[ZL])
    lg_buf[g] = jnp.sum(zl_buf[...], axis=0)

    def lg_step(k, _):
        copy(lg_buf.at[g], lg_buf.at[g], GL, (s, lax.rem(g + k, G))).start()
        return 0

    lax.fori_loop(1, G, lg_step, 0)
    wait(ud_recv, recv.at[UD])
    user_dir = TEMP * (ud[par] + ud_recv[...].astype(F32))
    uun = uu[par]
    ud[par] = uinv[par][:, :1] * (user_dir - uun * jnp.sum(uun * user_dir, axis=-1, keepdims=True))
    pltpu.make_async_copy(ud.at[par], ug_ref, here.at[O_UG]).start()
    wait(w2r_buf.at[:, 0], recv.at[W2S])
    wait(sl2_buf.at[0], recv.at[SL2])
    h1 = jnp.concatenate([h1_buf[j] for j in range(S)], axis=1)
    h2 = whole(h2_buf)
    slope2 = whole(sl2_buf).astype(F32)
    slope1 = silu_slope(pre1[...])

    wait(za_buf.at[pl.ds(0, S - 1)], recv.at[ZA])
    sums = []
    for e in (0, 1):
        part = za_buf[e].astype(F32)
        for t in range(e + 2, S, 2):
            part = part + za_buf[t].astype(F32)
        sums.append(part)
    own_grad = jnp.concatenate(sums, axis=0)
    uin = ui[...]
    raw_grad = (inv[:, :1] * (own_grad - uin * jnp.sum(uin * own_grad, axis=-1, keepdims=True))).astype(BF)
    rg[...] = raw_grad
    sg = (dot_t(raw_grad, b_buf[...].reshape(G * rows, 512)) * slope2).astype(BF)
    sg_scr[...] = sg
    fg = (dot_t(sg, w2r_buf[...].reshape(4 * rows, 1024)) * slope1).astype(BF)
    g2_send[...] = t_dot(xf_v[...], fg).astype(BF).reshape(G, rows, 128)
    grp_scatter(g2_send, g2_recv, G2)
    g2_recv[g] = g2_send[g]
    q_cols = pl.ds(pl.multiple_of(lax.rem(s, 4) * 128, 128), 128)
    gl_scr[...] = t_dot(h2, rg[:, q_cols]).astype(BF).reshape(G, 2, half, 128)
    g1_send[:, :rows] = t_dot(h1, sg_scr[:, cols]).astype(BF).reshape(G, rows, 128)
    g1_send[:, rows:] = gl_scr[:, s // 4]
    grp_scatter(g1_send, g1_recv, G1)
    g1_recv[g] = g1_send[g]

    wait(lg_buf.at[pl.ds(0, G - 1)], recv.at[GL])
    total = jnp.sum(lg_buf[...], axis=0)
    numer = jnp.sum(jnp.where(lane == 0, total, 0.0), axis=1, keepdims=True)
    denom = jnp.sum(jnp.where(lane == 1, total, 0.0), axis=1, keepdims=True)
    loss_ref[...] = jnp.broadcast_to(numer * S / denom, loss_ref.shape)

    wait(g2_recv.at[pl.ds(0, G - 1)], recv.at[G2])
    f2_buf[s] = jnp.sum(g2_recv[...].astype(F32), axis=0).astype(BF)
    z_bcast(f2_buf, F2)
    wait(g1_recv.at[pl.ds(0, G - 1)], recv.at[G1])
    f1_buf[s] = jnp.sum(g1_recv[...].astype(F32), axis=0).astype(BF)
    z_bcast(f1_buf, F1)

    pltpu.make_async_copy(lo_scr.at[par], lo_ref, here.at[O_LO]).wait()
    pltpu.make_async_copy(ud.at[par], ug_ref, here.at[O_UG]).wait()
    wait(a_buf.at[pl.ds(0, C - 1), 0], send.at[A])
    wait(a2_buf.at[pl.ds(0, C - 1), 0], send.at[A2])
    wait(a2_buf.at[:, 0], send.at[AS2])
    wait(b_buf.at[pl.ds(0, C - 1), 0], send.at[B])
    wait(a_buf.at[:, 0], send.at[AS])
    wait(b_buf.at[:, 0], send.at[BS])
    wait(pe_buf.at[:, 0], send.at[PES])
    for j in range(3):
        wait(pe_buf.at[pl.ds(0, per), 0], send.at[PE + j])
    for q in range(Q):
        wait(pair_recv.at[pl.ds(0, CQ)], send.at[PAIR + q])
    wait(rs_recv.at[pl.ds(0, C - 1)], send.at[RS])
    for buf, i in ((qr_buf, QKV), (at_recv, ATT), (zl_buf, ZL), (za_buf, ZA)):
        wait(buf.at[pl.ds(0, S - 1)], send.at[i])
    wait(h1_buf.at[pl.ds(0, S - 1)], send.at[H1])
    wait(h2_buf.at[0], send.at[H2])
    wait(sl2_buf.at[0], send.at[SL2])
    wait(h256.at[0], send.at[HX])
    wait(nx_buf.at[0], send.at[NX])
    wait(dn_recv, send.at[DN])
    wait(ud_recv, send.at[UD])
    wait(lg_buf.at[pl.ds(0, G - 1)], send.at[GL])
    wait(g1_recv.at[pl.ds(0, G - 1)], send.at[G1])
    wait(g2_recv.at[pl.ds(0, G - 1)], send.at[G2])
    wait(w2r_buf.at[:, 0], send.at[W2S])

    @pl.when(source)
    def _():
        wait(b_buf.at[pl.ds(0, C - 1)], send.at[W2])

    wait(f2_buf.at[pl.ds(0, S - 1)], recv.at[F2])
    for t in range(S):
        gf_ref[:, 128 * t : 128 * (t + 1)] = f2_buf[t].astype(F32)
    wait(f1_buf.at[pl.ds(0, S - 1)], recv.at[F1])
    for t in range(S):
        gm_ref[:, 128 * t : 128 * (t + 1)] = f1_buf[t, :rows].astype(F32)
        gl_ref[half * (t // 4) : half * (t // 4 + 1), 128 * (t % 4) : 128 * (t % 4 + 1)] = f1_buf[t, rows:].astype(F32)
    wait(f1_buf.at[pl.ds(0, S - 1)], send.at[F1])
    wait(f2_buf.at[pl.ds(0, S - 1)], send.at[F2])


def tail(*refs):
    ins, outs, mids = refs[:6], refs[6:12], refs[12:18]
    sem = refs[18]
    for i in range(6):
        pltpu.make_async_copy(ins[i], mids[i], sem.at[i]).start()
    for i in range(6):
        pltpu.make_async_copy(ins[i], mids[i], sem.at[i]).wait()
        if i == 1:
            outs[1][0, 0] = jnp.max(mids[1][...])
        else:
            pltpu.make_async_copy(mids[i], outs[i], sem.at[6 + i]).start()
    for i in (0, 2, 3, 4, 5):
        pltpu.make_async_copy(mids[i], outs[i], sem.at[6 + i]).wait()


def local(history, lengths, next_items, negatives, input_weight, output_weight, pool_features,
          tower_first, tower_middle, tower_last, S, G):
    events = history[0]
    tok = events.shape[0]
    C = G // 2
    R = pool_features.shape[0]
    RH = R // 2
    rows = tower_first.shape[0]
    V = pltpu.VMEM
    vmem = pl.BlockSpec(memory_space=pltpu.VMEM)
    hbm = pl.BlockSpec(memory_space=pltpu.HBM)
    width = G * RH // 4
    scratch = [
        pltpu.SemaphoreType.DMA((N_SEM,)),
        pltpu.SemaphoreType.DMA((N_SEM,)),
        pltpu.SemaphoreType.DMA((N_HERE,)),
        V((2, tok, 512), BF),
        V((2, 1, tok), jnp.int32),
        V((1, negatives.shape[1]), jnp.int32),
        V(input_weight.shape, BF),
        V(output_weight.shape, BF),
        V(pool_features.shape, BF),
        V((C, 2, rows, 128), BF),
        V((C, 2, 4, rows, 128), BF),
        V((C, 2, rows, 512), BF),
        V((2, 2, rows, 1024), BF),
        V((S, tok + tok // 2, 128), BF),
        V((S, tok + tok // 2, 128), BF),
        V((2 * tok, 512), BF),
        V((S * tok, DH), BF),
        V((S * tok, DH), BF),
        V((S * tok, DH), BF),
        V((S // 2, tok, 128), BF),
        V((S, tok, 128), BF),
        V((S, R, 128), BF),
        V((2, 4, R, 128), BF),
        V((2, 4, R, 128), BF),
        V((R, 128), F32),
        V((R, 512), F32),
        V((R, 128), F32),
        V((C, 2, RH, 512), BF),
        V((4, width, 2 * tok), F32),
        V((4, width, 2 * tok), BF),
        V((C, 2, RH, 512), BF),
        V((C, RH, 512), BF),
        V((C, RH, 512), BF),
        V((C, RH, 512), BF),
        V((8, 2 * tok), F32),
        V((8, 2 * tok), F32),
        V((2, tok, 512), F32),
        V((tok, 512), BF),
        V((tok, 512), BF),
        V((2, tok, 512), BF),
        V((S, 8, 128), F32),
        V((G, 8, 128), F32),
        V((S, RH, 512), BF),
        V((R, 512), BF),
        V((R, 1024), BF),
        V((G, 2, rows // 2, 128), BF),
        V((G, rows + rows // 2, 128), BF),
        V((G, rows + rows // 2, 128), BF),
        V((G, rows, 128), BF),
        V((G, rows, 128), BF),
        V((S, rows + rows // 2, 128), BF),
        V((S, rows, 128), BF),
        V((G * RH, 128), F32),
        V((2, tok, 512), F32),
        V((2, tok, 128), F32),
    ]
    shapes = [
        jax.ShapeDtypeStruct((tok, 512), BF),
        jax.ShapeDtypeStruct((8, 128), F32),
        jax.ShapeDtypeStruct((tok, 512), F32),
        jax.ShapeDtypeStruct((rows, 1024), F32),
        jax.ShapeDtypeStruct((rows, 1024), F32),
        jax.ShapeDtypeStruct((rows, 512), F32),
    ]
    results = pl.pallas_call(
        functools.partial(kernel, S, G),
        out_shape=shapes,
        in_specs=[pl.BlockSpec(memory_space=pltpu.SMEM)] + [hbm] * 9,
        out_specs=[hbm, vmem, hbm, vmem, vmem, vmem],
        scratch_shapes=scratch,
        compiler_params=pltpu.CompilerParams(
            collective_id=0, has_side_effects=True, vmem_limit_bytes=56 * 1024 * 1024),
    )(lengths, events, next_items, negatives, input_weight, output_weight, pool_features,
      tower_first, tower_middle, tower_last)
    lo, loss, ug, gf, gm, gl = pl.pallas_call(
        tail,
        out_shape=shapes[:1] + [jax.ShapeDtypeStruct((1, 1), F32)] + shapes[2:],
        in_specs=[hbm] * 6,
        out_specs=[hbm, pl.BlockSpec(memory_space=pltpu.SMEM)] + [hbm] * 4,
        scratch_shapes=[V(x.shape, x.dtype) for x in shapes] + [pltpu.SemaphoreType.DMA((12,))],
        compiler_params=pltpu.CompilerParams(vmem_limit_bytes=56 * 1024 * 1024),
    )(*results)
    return lo[None], loss.reshape(()), ug[None], gf, gm, gl


def solution(mesh):
    placed = (
        P("grp", "seq", None), P("grp"), P("grp", "seq"), P("grp", None), P(), P(),
        P("grp", None), P("grp", None), P("grp", None), P("grp", None),
    )
    return jax.shard_map(
        functools.partial(local, S=mesh.shape["seq"], G=mesh.shape["grp"]),
        mesh=mesh,
        in_specs=placed,
        out_specs=(
            P("grp", "seq", None), P(), P("grp", "seq", None),
            P("grp", None), P("grp", None), P("grp", None),
        ),
        check_vma=False,
    )
```

```python
import functools

import jax
import jax.numpy as jnp
from jax import lax
from jax.experimental import pallas as pl
from jax.experimental.pallas import tpu as pltpu
from jax.sharding import PartitionSpec as P

DH = 64
EPS_NORM = 1e-05
EPS_UNIT = 1e-06
TEMP = 20.0

MESH = pl.DeviceIdType.MESH
BF = jnp.bfloat16
F32 = jnp.float32

(A, A2, B, AS, AS2, BS, QKV, ATT, H1, H2, SL2, NX, NG, UP, US, UT, DN, UDS, UDP, ZA, ZL, GL, GP1, GP2, G1, G2, F1, F2,
 RS, W2, W2S, PE) = range(32)
N_SEM = 32

(I_W3, I_H, I_WIN, I_WOUT, I_X, I_NEG, I_NXT, I_W2R, O_LO, O_UG) = range(10)
I_W1, I_W2 = 10, 11
N_HERE = 15


def silu(x):
    half = 0.5 * x
    return half * (1.0 + jnp.tanh(half))


def silu_slope(z):
    sigma = 0.5 * (1.0 + jnp.tanh(0.5 * z))
    return sigma * (1.0 + z * (1.0 - sigma))


def layer_norm(values):
    center = values - jnp.mean(values, axis=-1, keepdims=True)
    spread = jnp.mean(center * center, axis=-1, keepdims=True)
    return center * lax.rsqrt(spread + EPS_NORM)


def dot(a, b):
    return jnp.dot(a, b, preferred_element_type=F32)


def dot_t(a, b):
    return lax.dot_general(a, b, (((1,), (1,)), ((), ())), preferred_element_type=F32)


def t_dot(a, b):
    return lax.dot_general(a, b, (((0,), (0,)), ((), ())), preferred_element_type=F32)


def wait(ref, sem):
    pltpu.make_async_copy(ref, ref, sem).wait()


def kernel(
    S, G,
    len_ref, hist, nxt, neg, win, wout, xf, w1, w2, w3,
    lo_ref, loss_ref, ug_ref, gf_ref, gm_ref, gl_ref,
    send, recv, here,
    hist_v, nx_buf, neg_buf, win_v, wout_v, xf_v,
    a_buf, a2_buf, b_buf, w2r_buf, qs_buf, qr_buf, gate, k_scr, q_scr, v_scr, at_send, at_recv,
    h1_buf, h2_buf, sl2_buf, pre1, ui, inv, pe_buf, em, st, rs_send, rs_recv, u_buf,
    dn_buf, ud, uds_send, uds_recv, udp_send, udp_recv, lo_scr, zl_buf, lg_buf, za_buf, rg, sg_scr,
    gl_scr, gp1, gp1_recv, gp2, gp2_recv, g1_send, g1_recv, g2_send, g2_recv, f1_buf, f2_buf, cnt, uu, uinv,
):
    C = G // 2
    s = lax.axis_index("seq")
    g = lax.axis_index("grp")
    p = g // 2
    c = g % 2
    par = s % 2
    tok = hist_v.shape[0]
    me = 2 * c + par
    rows = b_buf.shape[2]
    NB = a2_buf.shape[2]
    half = rows // 2
    NEG = neg.shape[1]
    R = xf_v.shape[0]
    RH = R // 2
    length = len_ref[0]
    pair = (s + 1 - 2 * par, g)
    sib = (s, 2 * p + 1 - c)
    diag = (s + 1 - 2 * par, 2 * p + 1 - c)
    cols = pl.ds(pl.multiple_of(s * 128, 128), 128)

    def copy(src, dst, i, dev):
        return pltpu.make_async_remote_copy(
            src_ref=src, dst_ref=dst, send_sem=send.at[i], recv_sem=recv.at[i],
            device_id=dev, device_id_type=MESH)

    def fetch(src, dst, i):
        pltpu.make_async_copy(src, dst, here.at[i]).start()

    def z_bcast(buf, i):
        def step(k, _):
            copy(buf.at[s], buf.at[s], i, (lax.rem(s + k, S), g)).start()
            return 0
        lax.fori_loop(1, S, step, 0)

    def chips(src, dst, i):
        def step(k, _):
            copy(src, dst, i, (s, 2 * lax.rem(p + k, C) + c)).start()
            return 0
        lax.fori_loop(1, C, step, 0)

    def chip_scatter(src, dst, i):
        def step(k, _):
            t = lax.rem(p + k, C)
            copy(src.at[t], dst.at[p], i, (s, 2 * t + c)).start()
            return 0
        lax.fori_loop(1, C, step, 0)
        dst[p] = src[p]

    def quad(buf, i):
        for dev in (sib, pair, diag):
            copy(buf.at[me], buf.at[me], i, dev).start()

    barrier = pltpu.get_barrier_semaphore()

    def greet_grp(k, _):
        pl.semaphore_signal(barrier, inc=1, device_id=(s, lax.rem(g + k, G)), device_id_type=MESH)
        return 0

    def greet_seq(k, _):
        pl.semaphore_signal(barrier, inc=1, device_id=(lax.rem(s + k, S), g), device_id_type=MESH)
        return 0

    lax.fori_loop(1, G, greet_grp, 0)
    lax.fori_loop(1, S, greet_seq, 0)
    pl.semaphore_signal(barrier, inc=1, device_id=diag, device_id_type=MESH)

    fetch(w1.at[:, cols], a_buf.at[p, c], I_W1)
    for j in range(NB):
        block = pl.ds(pl.multiple_of((2 * j + par) * 128, 128), 128)
        fetch(w2.at[:, block], a2_buf.at[p, c, j], I_W2 + j)
    fetch(hist, hist_v, I_H)
    fetch(win, win_v, I_WIN)
    fetch(nxt, nx_buf.at[me], I_NXT)
    fetch(w3, b_buf.at[p, c], I_W3)
    fetch(xf, xf_v, I_X)
    fetch(neg, neg_buf.at[c, :, pl.ds(0, NEG)], I_NEG)
    fetch(wout, wout_v, I_WOUT)
    source = p // 2 == s

    @pl.when(source)
    def _():
        fetch(w2, w2r_buf.at[p % 2, c], I_W2R)

    neg_buf[c, :, NEG:] = jnp.full((1, 128), length, jnp.int32)
    wait(a_buf.at[p, c], here.at[I_W1])
    pl.semaphore_wait(barrier, (G - 1) + (S - 1) + 1)
    chips(a_buf.at[p, c], a_buf.at[p, c], A)

    wait(hist_v, here.at[I_H])
    normed = layer_norm(hist_v[...].astype(F32)).astype(BF)
    wait(win_v, here.at[I_WIN])
    for j in range(4):
        x = silu(dot(normed, win_v[:, 512 + 384 * j : 512 + 384 * (j + 1)])).astype(BF)
        for e in (0, 1):
            o = 192 * e
            qs_buf[2 * j + e, :tok] = x[:, o : o + 128]
            v = x[:, o + 128 : o + 192]
            qs_buf[2 * j + e, tok:] = jnp.concatenate([v[: tok // 2], v[tok // 2 :]], axis=1)

    def qkv_step(k, _):
        t = lax.rem(s + k, S)
        copy(qs_buf.at[t], qr_buf.at[s], QKV, (t, g)).start()
        return 0

    lax.fori_loop(1, S, qkv_step, 0)
    qr_buf[s] = qs_buf[s]
    for j in range(NB):
        wait(a2_buf.at[p, c, j], here.at[I_W2 + j])
    chips(a2_buf.at[p, c], a2_buf.at[p, c], A2)
    wait(nx_buf.at[me], here.at[I_NXT])
    quad(nx_buf, NX)
    wait(neg_buf.at[c, :, pl.ds(0, NEG)], here.at[I_NEG])
    copy(neg_buf.at[c], neg_buf.at[c], NG, sib).start()
    gate[...] = silu(dot(normed, win_v[:, :512])).astype(BF)

    wait(xf_v, here.at[I_X])
    wait(a_buf.at[pl.ds(0, C - 1), 0], recv.at[A])
    copy(a_buf.at[:, c], a_buf.at[:, c], AS, sib).start()
    wait(b_buf.at[p, c], here.at[I_W3])
    chips(b_buf.at[p, c], b_buf.at[p, c], B)
    wait(a_buf.at[:, 0], recv.at[AS])
    z1 = dot(xf_v[...], a_buf[...].reshape(G * rows, 128))
    pre1[...] = z1
    h1_buf[s] = silu(z1).astype(BF)
    z_bcast(h1_buf, H1)

    def local_row(ids):
        return jnp.where((ids // RH) % 4 == me, (ids // (2 * R)) * RH + ids % RH, -1)

    wait(neg_buf.at[0], recv.at[NG])
    n_rows = C * RH
    for e in (0, 1):
        ids = local_row(neg_buf[e, :, :NEG])
        hot = (lax.broadcasted_iota(jnp.int32, (n_rows, NEG), 0) == ids).astype(F32).astype(BF)
        cnt[e] = dot(hot, jnp.ones((NEG, 128), BF))
    def whole(buf):
        return jnp.concatenate([buf[j % 2, j // 2] for j in range(2 * NB)], axis=1)

    wait(a2_buf.at[pl.ds(0, C - 1), 0], recv.at[A2])
    copy(a2_buf.at[:, c], a2_buf.at[:, c], AS2, sib).start()
    wait(qr_buf.at[pl.ds(0, S - 1)], recv.at[QKV])
    for j in range(S):
        x = qr_buf[j]
        q_scr[tok * j : tok * (j + 1)] = x[:tok, :DH]
        k_scr[tok * j : tok * (j + 1)] = x[:tok, DH:]
        v_scr[tok * j : tok * (j + 1)] = jnp.concatenate([x[tok:, :DH], x[tok:, DH:]], axis=0)

    inv_len = 1.0 / jnp.full((1, 1), length, jnp.int32).astype(F32)
    W = 2 * tok

    def attend(b):
        q = q_scr[W * b : W * (b + 1)]
        acc = jnp.zeros((W, DH), F32)
        for kb in range(b + 1):
            hs = dot_t(q, k_scr[W * kb : W * (kb + 1)]) * (0.5 * DH ** (-0.5))
            w = (hs * inv_len) * (1.0 + jnp.tanh(hs))
            if kb == b:
                r = lax.broadcasted_iota(jnp.int32, (W, W), 0)
                cc = lax.broadcasted_iota(jnp.int32, (W, W), 1)
                w = jnp.where(cc <= r, w, 0.0)
            acc = acc + dot(w.astype(BF), v_scr[W * kb : W * (kb + 1)])
        pos = W * b + lax.broadcasted_iota(jnp.int32, (W, 1), 0)
        acc = jnp.where(pos < length, acc, 0.0).astype(BF)
        for i in (0, 1):
            o = acc[tok * i : tok * (i + 1)]
            at_send[2 * b + i] = jnp.concatenate([o[: tok // 2], o[tok // 2 :]], axis=1)

    for b in reversed(range(S // 2)):
        attend(b)
    at_recv[s] = at_send[s]

    wait(h1_buf.at[pl.ds(0, S - 1)], recv.at[H1])
    wait(a2_buf.at[:, 0], recv.at[AS2])
    h1 = jnp.concatenate([h1_buf[j] for j in range(S)], axis=1)
    for j in range(NB):
        z2 = dot(h1, a2_buf[:, :, j].reshape(G * rows, 128))
        h2_buf[par, j] = silu(z2).astype(BF)
        sl2_buf[par, j] = silu_slope(z2).astype(BF)
    copy(h2_buf.at[par], h2_buf.at[par], H2, pair).start()

    def at_step(k, _):
        t = lax.rem(s + k, S)
        copy(at_send.at[t], at_recv.at[s], ATT, (t, g)).start()
        return 0

    lax.fori_loop(1, S, at_step, 0)
    copy(sl2_buf.at[par], sl2_buf.at[par], SL2, pair).start()

    wait(b_buf.at[pl.ds(0, C - 1), 0], recv.at[B])
    copy(b_buf.at[:, c], b_buf.at[:, c], BS, sib).start()

    wait(h2_buf.at[0], recv.at[H2])
    wait(b_buf.at[:, 0], recv.at[BS])
    h2 = whole(h2_buf)
    raw = dot(h2, b_buf[...].reshape(G * rows, 512))
    item_inverse = lax.rsqrt(jnp.sum(raw * raw, axis=-1, keepdims=True) + EPS_UNIT)
    unit_item = raw * item_inverse
    ui[...] = unit_item
    inv[...] = jnp.broadcast_to(item_inverse, inv.shape)
    pe_buf[p] = ui[pl.ds(pl.multiple_of(par * RH, RH), RH)].astype(BF)
    chips(pe_buf.at[p], pe_buf.at[p], PE)

    @pl.when(source)
    def _():
        wait(w2r_buf.at[p % 2, c], here.at[I_W2R])
        chips(w2r_buf.at[p % 2, c], w2r_buf.at[p % 2, c], W2)

    wait(wout_v, here.at[I_WOUT])
    wait(at_recv.at[pl.ds(0, S - 1)], recv.at[ATT])
    tops, bottoms = [], []
    for h in range(S):
        x = at_recv[h]
        tops.append(x[:, :DH])
        bottoms.append(x[:, DH:])
    merged = jnp.concatenate(
        [jnp.concatenate(tops, axis=1), jnp.concatenate(bottoms, axis=1)], axis=0).astype(F32)
    branch = (layer_norm(merged) * gate[...].astype(F32)).astype(BF)
    layer_out = (hist_v[...].astype(F32) + dot(branch, wout_v[...])).astype(BF)
    lo_scr[...] = layer_out
    pltpu.make_async_copy(lo_scr, lo_ref, here.at[O_LO]).start()
    outward = layer_out.astype(F32)
    user_inverse = lax.rsqrt(jnp.sum(outward * outward, axis=-1, keepdims=True) + EPS_UNIT)
    unit_user = outward * user_inverse
    u_buf[me] = unit_user.astype(BF)
    copy(u_buf.at[me], u_buf.at[me], UP, pair).start()
    copy(u_buf.at[me], u_buf.at[me], US, sib).start()
    uu[...] = unit_user
    uinv[...] = jnp.broadcast_to(user_inverse, (tok, 128))

    P4 = 4 * tok
    wait(nx_buf.at[pl.ds(0, 3)], recv.at[NX])
    items = local_row(jnp.concatenate([nx_buf[j] for j in range(4)], axis=1))
    quad_pos = lax.broadcasted_iota(jnp.int32, (1, P4), 1)
    positions = (s // 2) * W + quad_pos % W
    lens = jnp.concatenate([neg_buf[j // 2, :, NEG:] for j in range(4)], axis=1)
    valid = (positions < lens - 1).astype(F32)

    wait(u_buf.at[0], recv.at[UP])
    other = 2 * c + 1 - par
    copy(u_buf.at[other], u_buf.at[other], UT, sib).start()
    wait(pe_buf.at[pl.ds(0, C - 1)], recv.at[PE])
    wait(u_buf.at[0], recv.at[US])
    wait(u_buf.at[0], recv.at[UT])

    Q = 4
    CQ = C // Q
    width = n_rows // Q
    users = u_buf[...].reshape(P4, 512)
    row_id = lax.broadcasted_iota(jnp.int32, (width, P4), 0)
    den = jnp.zeros((1, P4), F32)
    positive = jnp.zeros((1, P4), F32)
    for q in range(Q):
        logit = TEMP * dot_t(pe_buf[CQ * q : CQ * (q + 1)].reshape(width, 512), users)
        own = row_id + width * q == items
        times = jnp.concatenate([cnt[j // 2, width * q : width * (q + 1)] for j in range(4)], axis=1)
        e = jnp.where(own, 0.0, jnp.exp(logit) * times)
        em[q] = e
        den = den + jnp.sum(e, axis=0, keepdims=True)
        positive = positive + jnp.sum(jnp.where(own, logit, 0.0), axis=0, keepdims=True)
    row8 = lax.broadcasted_iota(jnp.int32, (8, P4), 0)
    dn_buf[me] = jnp.where(row8 == 0, den, positive)
    quad(dn_buf, DN)
    wait(dn_buf.at[pl.ds(0, 3)], recv.at[DN])
    sums = dn_buf[0] + dn_buf[1] + dn_buf[2] + dn_buf[3]
    den = sums[0:1]
    positive = sums[1:2]
    positive_exp = jnp.exp(positive)
    den = den + positive_exp
    slope = valid * (positive_exp / den - 1.0)
    scale = valid / den

    for q in range(Q):
        gq = lax.rem(p // CQ + q, Q)
        sm = jnp.where(row_id + width * gq == items, slope, scale * em[gq]).astype(BF)
        st[gq] = sm
        rs_send[pl.ds(CQ * gq, CQ)] = (TEMP * dot(sm, users)).astype(BF).reshape(CQ, RH, 512)

        def rs_step(i, _):
            t = CQ * gq + lax.rem(p + i, CQ)

            @pl.when(t != p)
            def _():
                copy(rs_send.at[t], rs_recv.at[p], RS, (s, 2 * t + c)).start()
            return 0

        lax.fori_loop(0, CQ, rs_step, 0)

    mine = quad_pos // tok == me
    loss_sum = jnp.sum(jnp.where(mine, valid * (jnp.log(den) - positive), 0.0))
    lane = lax.broadcasted_iota(jnp.int32, (8, 128), 1)
    count = jnp.full((8, 128), length - 1, jnp.int32).astype(F32)
    zl_buf[s] = jnp.where(lane == 0, loss_sum, jnp.where(lane == 1, count, 0.0))
    z_bcast(zl_buf, ZL)

    user_dir = t_dot(st[...].reshape(n_rows, P4), pe_buf[...].reshape(n_rows, 512))
    ud[...] = user_dir.reshape(2, 2, tok, 512)
    uds_send[...] = ud[1 - c].astype(BF)
    copy(uds_send, uds_recv, UDS, sib).start()

    @pl.when(source)
    def _():
        wait(w2r_buf.at[0, 0], recv.at[W2])

    @pl.when(jnp.logical_not(source))
    def _():
        wait(w2r_buf.at[:, 0], recv.at[W2])

    copy(w2r_buf.at[:, c], w2r_buf.at[:, c], W2S, sib).start()
    wait(uds_recv, recv.at[UDS])
    udp_send[...] = (ud[c, 1 - par] + uds_recv[1 - par].astype(F32)).astype(BF)
    copy(udp_send, udp_recv, UDP, pair).start()

    wait(rs_recv.at[pl.ds(0, C - 1)], recv.at[RS])
    rs_recv[p] = rs_send[p]
    za_buf[s] = jnp.sum(rs_recv[...].astype(F32), axis=0).astype(BF)
    z_bcast(za_buf, ZA)

    wait(zl_buf.at[pl.ds(0, S - 1)], recv.at[ZL])
    lg_buf[g] = jnp.sum(zl_buf[...], axis=0)

    def lg_step(k, _):
        copy(lg_buf.at[g], lg_buf.at[g], GL, (s, lax.rem(g + k, G))).start()
        return 0

    lax.fori_loop(1, G, lg_step, 0)
    wait(udp_recv, recv.at[UDP])
    user_dir = TEMP * (ud[c, par] + uds_recv[par].astype(F32) + udp_recv[...].astype(F32))
    uun = uu[...]
    uu[...] = uinv[:, :1] * (user_dir - uun * jnp.sum(uun * user_dir, axis=-1, keepdims=True))
    pltpu.make_async_copy(uu, ug_ref, here.at[O_UG]).start()
    wait(w2r_buf.at[:, 0], recv.at[W2S])
    wait(sl2_buf.at[0], recv.at[SL2])
    h1 = jnp.concatenate([h1_buf[j] for j in range(S)], axis=1)
    h2 = whole(h2_buf)
    slope2 = whole(sl2_buf).astype(F32)
    slope1 = silu_slope(pre1[...])

    wait(za_buf.at[pl.ds(0, S - 1)], recv.at[ZA])
    sums = []
    for e in (0, 1):
        part = za_buf[e].astype(F32)
        for t in range(e + 2, S, 2):
            part = part + za_buf[t].astype(F32)
        sums.append(part)
    own_grad = jnp.concatenate(sums, axis=0)
    uin = ui[...]
    raw_grad = (inv[:, :1] * (own_grad - uin * jnp.sum(uin * own_grad, axis=-1, keepdims=True))).astype(BF)
    rg[...] = raw_grad
    sg = (dot_t(raw_grad, b_buf[...].reshape(G * rows, 512)) * slope2).astype(BF)
    sg_scr[...] = sg
    fg = (dot_t(sg, w2r_buf[...].reshape(4 * rows, 1024)) * slope1).astype(BF)
    gp2[...] = t_dot(xf_v[...], fg).astype(BF).reshape(C, 2, rows, 128)
    copy(gp2.at[:, 1 - c], gp2_recv, GP2, sib).start()
    q_cols = pl.ds(pl.multiple_of(lax.rem(s, 4) * 128, 128), 128)
    gl_scr[...] = t_dot(h2, rg[:, q_cols]).astype(BF).reshape(C, 2, 2, half, 128)
    gp1[:, :, :rows] = t_dot(h1, sg_scr[:, cols]).astype(BF).reshape(C, 2, rows, 128)
    gp1[:, :, rows:] = gl_scr[:, :, s // 4]
    copy(gp1.at[:, 1 - c], gp1_recv, GP1, sib).start()
    wait(gp2_recv, recv.at[GP2])
    g2_send[...] = (gp2[:, c].astype(F32) + gp2_recv[...].astype(F32)).astype(BF)
    chip_scatter(g2_send, g2_recv, G2)
    wait(gp1_recv, recv.at[GP1])
    g1_send[...] = (gp1[:, c].astype(F32) + gp1_recv[...].astype(F32)).astype(BF)
    chip_scatter(g1_send, g1_recv, G1)

    wait(lg_buf.at[pl.ds(0, G - 1)], recv.at[GL])
    total = jnp.sum(lg_buf[...], axis=0)
    numer = jnp.sum(jnp.where(lane == 0, total, 0.0), axis=1, keepdims=True)
    denom = jnp.sum(jnp.where(lane == 1, total, 0.0), axis=1, keepdims=True)
    loss_ref[...] = jnp.broadcast_to(numer * S / denom, loss_ref.shape)

    wait(g2_recv.at[pl.ds(0, C - 1)], recv.at[G2])
    f2_buf[s] = jnp.sum(g2_recv[...].astype(F32), axis=0).astype(BF)
    z_bcast(f2_buf, F2)
    wait(g1_recv.at[pl.ds(0, C - 1)], recv.at[G1])
    f1_buf[s] = jnp.sum(g1_recv[...].astype(F32), axis=0).astype(BF)
    z_bcast(f1_buf, F1)

    pltpu.make_async_copy(lo_scr, lo_ref, here.at[O_LO]).wait()
    pltpu.make_async_copy(uu, ug_ref, here.at[O_UG]).wait()
    wait(a_buf.at[pl.ds(0, C - 1), 0], send.at[A])
    wait(a2_buf.at[pl.ds(0, C - 1), 0], send.at[A2])
    wait(a2_buf.at[:, 0], send.at[AS2])
    wait(b_buf.at[pl.ds(0, C - 1), 0], send.at[B])
    wait(a_buf.at[:, 0], send.at[AS])
    wait(b_buf.at[:, 0], send.at[BS])
    wait(pe_buf.at[pl.ds(0, C - 1)], send.at[PE])
    wait(rs_recv.at[pl.ds(0, C - 1)], send.at[RS])
    for buf, i in ((qr_buf, QKV), (at_recv, ATT), (zl_buf, ZL), (za_buf, ZA)):
        wait(buf.at[pl.ds(0, S - 1)], send.at[i])
    wait(h1_buf.at[pl.ds(0, S - 1)], send.at[H1])
    wait(h2_buf.at[0], send.at[H2])
    wait(sl2_buf.at[0], send.at[SL2])
    wait(nx_buf.at[pl.ds(0, 3)], send.at[NX])
    wait(neg_buf.at[0], send.at[NG])
    for i in (UP, US, UT):
        wait(u_buf.at[0], send.at[i])
    wait(dn_buf.at[pl.ds(0, 3)], send.at[DN])
    wait(uds_recv, send.at[UDS])
    wait(udp_recv, send.at[UDP])
    wait(gp1_recv, send.at[GP1])
    wait(gp2_recv, send.at[GP2])
    wait(lg_buf.at[pl.ds(0, G - 1)], send.at[GL])
    wait(g1_recv.at[pl.ds(0, C - 1)], send.at[G1])
    wait(g2_recv.at[pl.ds(0, C - 1)], send.at[G2])
    wait(w2r_buf.at[:, 0], send.at[W2S])

    @pl.when(source)
    def _():
        wait(b_buf.at[pl.ds(0, C - 1)], send.at[W2])

    wait(f2_buf.at[pl.ds(0, S - 1)], recv.at[F2])
    for t in range(S):
        gf_ref[:, 128 * t : 128 * (t + 1)] = f2_buf[t].astype(F32)
    wait(f1_buf.at[pl.ds(0, S - 1)], recv.at[F1])
    for t in range(S):
        gm_ref[:, 128 * t : 128 * (t + 1)] = f1_buf[t, :rows].astype(F32)
        gl_ref[half * (t // 4) : half * (t // 4 + 1), 128 * (t % 4) : 128 * (t % 4 + 1)] = f1_buf[t, rows:].astype(F32)
    wait(f1_buf.at[pl.ds(0, S - 1)], send.at[F1])
    wait(f2_buf.at[pl.ds(0, S - 1)], send.at[F2])


def tail(*refs):
    ins, outs, mids = refs[:6], refs[6:12], refs[12:18]
    sem = refs[18]
    for i in range(6):
        pltpu.make_async_copy(ins[i], mids[i], sem.at[i]).start()
    for i in range(6):
        pltpu.make_async_copy(ins[i], mids[i], sem.at[i]).wait()
        if i == 1:
            outs[1][0, 0] = jnp.max(mids[1][...])
        else:
            pltpu.make_async_copy(mids[i], outs[i], sem.at[6 + i]).start()
    for i in (0, 2, 3, 4, 5):
        pltpu.make_async_copy(mids[i], outs[i], sem.at[6 + i]).wait()


def local(history, lengths, next_items, negatives, input_weight, output_weight, pool_features,
          tower_first, tower_middle, tower_last, S, G):
    events = history[0]
    tok = events.shape[0]
    C = G // 2
    R = pool_features.shape[0]
    RH = R // 2
    rows = tower_first.shape[0]
    V = pltpu.VMEM
    vmem = pl.BlockSpec(memory_space=pltpu.VMEM)
    hbm = pl.BlockSpec(memory_space=pltpu.HBM)
    width = C * RH // 4
    scratch = [
        pltpu.SemaphoreType.DMA((N_SEM,)),
        pltpu.SemaphoreType.DMA((N_SEM,)),
        pltpu.SemaphoreType.DMA((N_HERE,)),
        V((tok, 512), BF),
        V((4, 1, tok), jnp.int32),
        V((2, 1, negatives.shape[1] + 128), jnp.int32),
        V(input_weight.shape, BF),
        V(output_weight.shape, BF),
        V(pool_features.shape, BF),
        V((C, 2, rows, 128), BF),
        V((C, 2, 4, rows, 128), BF),
        V((C, 2, rows, 512), BF),
        V((2, 2, rows, 1024), BF),
        V((S, tok + tok // 2, 128), BF),
        V((S, tok + tok // 2, 128), BF),
        V((tok, 512), BF),
        V((S * tok, DH), BF),
        V((S * tok, DH), BF),
        V((S * tok, DH), BF),
        V((S, tok // 2, 128), BF),
        V((S, tok // 2, 128), BF),
        V((S, R, 128), BF),
        V((2, 4, R, 128), BF),
        V((2, 4, R, 128), BF),
        V((R, 128), F32),
        V((R, 512), F32),
        V((R, 128), F32),
        V((C, RH, 512), BF),
        V((4, width, 4 * tok), F32),
        V((4, width, 4 * tok), BF),
        V((C, RH, 512), BF),
        V((C, RH, 512), BF),
        V((4, tok, 512), BF),
        V((4, 8, 4 * tok), F32),
        V((2, 2, tok, 512), F32),
        V((2, tok, 512), BF),
        V((2, tok, 512), BF),
        V((tok, 512), BF),
        V((tok, 512), BF),
        V((tok, 512), BF),
        V((S, 8, 128), F32),
        V((G, 8, 128), F32),
        V((S, RH, 512), BF),
        V((R, 512), BF),
        V((R, 1024), BF),
        V((C, 2, 2, rows // 2, 128), BF),
        V((C, 2, rows + rows // 2, 128), BF),
        V((C, rows + rows // 2, 128), BF),
        V((C, 2, rows, 128), BF),
        V((C, rows, 128), BF),
        V((C, rows + rows // 2, 128), BF),
        V((C, rows + rows // 2, 128), BF),
        V((C, rows, 128), BF),
        V((C, rows, 128), BF),
        V((S, rows + rows // 2, 128), BF),
        V((S, rows, 128), BF),
        V((2, C * RH, 128), F32),
        V((tok, 512), F32),
        V((tok, 128), F32),
    ]
    shapes = [
        jax.ShapeDtypeStruct((tok, 512), BF),
        jax.ShapeDtypeStruct((8, 128), F32),
        jax.ShapeDtypeStruct((tok, 512), F32),
        jax.ShapeDtypeStruct((rows, 1024), F32),
        jax.ShapeDtypeStruct((rows, 1024), F32),
        jax.ShapeDtypeStruct((rows, 512), F32),
    ]
    results = pl.pallas_call(
        functools.partial(kernel, S, G),
        out_shape=shapes,
        in_specs=[pl.BlockSpec(memory_space=pltpu.SMEM)] + [hbm] * 9,
        out_specs=[hbm, vmem, hbm, vmem, vmem, vmem],
        scratch_shapes=scratch,
        compiler_params=pltpu.CompilerParams(
            collective_id=0, has_side_effects=True, vmem_limit_bytes=56 * 1024 * 1024),
    )(lengths, events, next_items, negatives, input_weight, output_weight, pool_features,
      tower_first, tower_middle, tower_last)
    lo, loss, ug, gf, gm, gl = pl.pallas_call(
        tail,
        out_shape=shapes[:1] + [jax.ShapeDtypeStruct((1, 1), F32)] + shapes[2:],
        in_specs=[hbm] * 6,
        out_specs=[hbm, pl.BlockSpec(memory_space=pltpu.SMEM)] + [hbm] * 4,
        scratch_shapes=[V(x.shape, x.dtype) for x in shapes] + [pltpu.SemaphoreType.DMA((12,))],
        compiler_params=pltpu.CompilerParams(vmem_limit_bytes=56 * 1024 * 1024),
    )(*results)
    return lo[None], loss.reshape(()), ug[None], gf, gm, gl


def solution(mesh):
    placed = (
        P("grp", "seq", None), P("grp"), P("grp", "seq"), P("grp", None), P(), P(),
        P("grp", None), P("grp", None), P("grp", None), P("grp", None),
    )
    return jax.shard_map(
        functools.partial(local, S=mesh.shape["seq"], G=mesh.shape["grp"]),
        mesh=mesh,
        in_specs=placed,
        out_specs=(
            P("grp", "seq", None), P(), P("grp", "seq", None),
            P("grp", None), P("grp", None), P("grp", None),
        ),
        check_vma=False,
    )
```

```python
import functools

import jax
import jax.numpy as jnp
from jax import lax
from jax.experimental import pallas as pl
from jax.experimental.pallas import tpu as pltpu
from jax.sharding import PartitionSpec as P

DH = 64
EPS_NORM = 1e-05
EPS_UNIT = 1e-06
TEMP = 20.0

MESH = pl.DeviceIdType.MESH
BF = jnp.bfloat16
F32 = jnp.float32

(A, A2, B, AS, AS2, BS, QKV, ATT, H1, H2, SL2, NX, NG, UP, US, UT, DN, UDS, UDP, ZL, GL, GP1, GP2, G1, G2, F1, F2,
 W2, PE) = range(29)
RS, ZA = 29, 31
N_SEM = 33

(I_W3, I_H, I_WIN, I_WOUT, I_X, I_NEG, I_NXT, I_W1) = range(8)
I_W2 = 8
N_HERE = 12


def silu(x):
    half = 0.5 * x
    return half * (1.0 + jnp.tanh(half))


def silu_slope(z):
    sigma = 0.5 * (1.0 + jnp.tanh(0.5 * z))
    return sigma * (1.0 + z * (1.0 - sigma))


def layer_norm(values):
    center = values - jnp.mean(values, axis=-1, keepdims=True)
    spread = jnp.mean(center * center, axis=-1, keepdims=True)
    return center * lax.rsqrt(spread + EPS_NORM)


def dot(a, b):
    return jnp.dot(a, b, preferred_element_type=F32)


def dot_t(a, b):
    return lax.dot_general(a, b, (((1,), (1,)), ((), ())), preferred_element_type=F32)


def t_dot(a, b):
    return lax.dot_general(a, b, (((0,), (0,)), ((), ())), preferred_element_type=F32)


def wait(ref, sem):
    pltpu.make_async_copy(ref, ref, sem).wait()


def kernel(
    S, G,
    len_ref, hist, nxt, neg, win, wout, xf, w1, w2, w3,
    lo_ref, loss_ref, ug_ref, gf_ref, gm_ref, gl_ref,
    send, recv, here,
    hist_v, nx_buf, neg_buf, win_v, wout_v, xf_v,
    a_buf, a2_buf, b_buf, w2r_buf, qs_buf, qr_buf, gate, k_scr, q_scr, v_scr, at_send, at_recv,
    h1_buf, h2_buf, sl2_buf, pre1, ui, inv, pe_buf, em, st, rs_send, rs_recv, u_buf,
    dn_buf, ud, uds_send, uds_recv, udp_send, udp_recv, zl_buf, lg_buf, za_buf, rg, sg_scr,
    gl_scr, gp1, gp1_recv, gp2, gp2_recv, g1_send, g1_recv, g2_send, g2_recv, f1_buf, f2_buf, cnt, uu, uinv,
):
    C = G // 2
    s = lax.axis_index("seq")
    g = lax.axis_index("grp")
    p = g // 2
    c = g % 2
    par = s % 2
    tok = hist_v.shape[0]
    me = 2 * c + par
    rows = b_buf.shape[2]
    NB = a2_buf.shape[2]
    half = rows // 2
    NEG = neg.shape[1]
    R = xf_v.shape[0]
    RH = R // 2
    length = len_ref[0]
    pair = (s + 1 - 2 * par, g)
    sib = (s, 2 * p + 1 - c)
    diag = (s + 1 - 2 * par, 2 * p + 1 - c)
    cols = pl.ds(pl.multiple_of(s * 128, 128), 128)

    def copy(src, dst, i, dev):
        return pltpu.make_async_remote_copy(
            src_ref=src, dst_ref=dst, send_sem=send.at[i], recv_sem=recv.at[i],
            device_id=dev, device_id_type=MESH)

    def fetch(src, dst, i):
        pltpu.make_async_copy(src, dst, here.at[i]).start()

    def z_bcast(buf, i):
        def step(k, _):
            copy(buf.at[s], buf.at[s], i, (lax.rem(s + k, S), g)).start()
            return 0
        lax.fori_loop(1, S, step, 0)

    def chips(src, dst, i):
        def step(k, _):
            copy(src, dst, i, (s, 2 * lax.rem(p + k, C) + c)).start()
            return 0
        lax.fori_loop(1, C, step, 0)

    def chip_scatter(src, dst, i):
        def step(k, _):
            t = lax.rem(p + k, C)
            copy(src.at[t], dst.at[p], i, (s, 2 * t + c)).start()
            return 0
        lax.fori_loop(1, C, step, 0)
        dst[p] = src[p]

    def quad(buf, i):
        for dev in (sib, pair, diag):
            copy(buf.at[me], buf.at[me], i, dev).start()

    fetch(w1.at[:, cols], a_buf.at[p, c], I_W1)
    barrier = pltpu.get_barrier_semaphore()

    def greet_grp(k, _):
        pl.semaphore_signal(barrier, inc=1, device_id=(s, lax.rem(g + k, G)), device_id_type=MESH)
        return 0

    def greet_seq(k, _):
        pl.semaphore_signal(barrier, inc=1, device_id=(lax.rem(s + k, S), g), device_id_type=MESH)
        return 0

    lax.fori_loop(1, G, greet_grp, 0)
    lax.fori_loop(1, S, greet_seq, 0)
    pl.semaphore_signal(barrier, inc=1, device_id=diag, device_id_type=MESH)

    for j in range(NB):
        block = pl.ds(pl.multiple_of((2 * j + par) * 128, 128), 128)
        fetch(w2.at[:, block], a2_buf.at[p, c, j], I_W2 + j)
    fetch(hist, hist_v, I_H)
    fetch(win, win_v, I_WIN)
    fetch(nxt, nx_buf.at[me], I_NXT)
    fetch(w3, b_buf.at[p, c], I_W3)
    fetch(xf, xf_v, I_X)
    fetch(neg, neg_buf.at[c, :, pl.ds(0, NEG)], I_NEG)
    fetch(wout, wout_v, I_WOUT)
    neg_buf[c, :, NEG:] = jnp.full((1, 128), length, jnp.int32)
    wait(a_buf.at[p, c], here.at[I_W1])
    pl.semaphore_wait(barrier, (G - 1) + (S - 1) + 1)
    chips(a_buf.at[p, c], a_buf.at[p, c], A)

    wait(hist_v, here.at[I_H])
    normed = layer_norm(hist_v[...].astype(F32)).astype(BF)
    wait(win_v, here.at[I_WIN])
    for j in range(4):
        x = silu(dot(normed, win_v[:, 512 + 384 * j : 512 + 384 * (j + 1)])).astype(BF)
        for e in (0, 1):
            o = 192 * e
            qs_buf[2 * j + e, :tok] = x[:, o : o + 128]
            v = x[:, o + 128 : o + 192]
            qs_buf[2 * j + e, tok:] = jnp.concatenate([v[: tok // 2], v[tok // 2 :]], axis=1)

    def qkv_step(k, _):
        t = lax.rem(s + k, S)
        copy(qs_buf.at[t], qr_buf.at[s], QKV, (t, g)).start()
        return 0

    lax.fori_loop(1, S, qkv_step, 0)
    qr_buf[s] = qs_buf[s]
    for j in range(NB):
        wait(a2_buf.at[p, c, j], here.at[I_W2 + j])
    chips(a2_buf.at[p, c], a2_buf.at[p, c], A2)
    wait(nx_buf.at[me], here.at[I_NXT])
    quad(nx_buf, NX)
    wait(neg_buf.at[c, :, pl.ds(0, NEG)], here.at[I_NEG])
    copy(neg_buf.at[c], neg_buf.at[c], NG, sib).start()
    gate[...] = silu(dot(normed, win_v[:, :512])).astype(BF)

    wait(xf_v, here.at[I_X])
    wait(a_buf.at[pl.ds(0, C - 1), 0], recv.at[A])
    copy(a_buf.at[:, c], a_buf.at[:, c], AS, sib).start()
    wait(b_buf.at[p, c], here.at[I_W3])
    chips(b_buf.at[p, c], b_buf.at[p, c], B)
    wait(a_buf.at[:, 0], recv.at[AS])
    z1 = dot(xf_v[...], a_buf[...].reshape(G * rows, 128))
    pre1[...] = z1
    h1_buf[s] = silu(z1).astype(BF)
    z_bcast(h1_buf, H1)

    def local_row(ids):
        return jnp.where((ids // RH) % 4 == me, (ids // (2 * R)) * RH + ids % RH, -1)

    wait(neg_buf.at[0], recv.at[NG])
    n_rows = C * RH
    for e in (0, 1):
        ids = local_row(neg_buf[e, :, :NEG])
        hot = (lax.broadcasted_iota(jnp.int32, (n_rows, NEG), 0) == ids).astype(F32).astype(BF)
        cnt[e] = dot(hot, jnp.ones((NEG, 128), BF))
    def whole(buf):
        return jnp.concatenate([buf[j % 2, j // 2] for j in range(2 * NB)], axis=1)

    wait(a2_buf.at[pl.ds(0, C - 1), 0], recv.at[A2])
    copy(a2_buf.at[:, c], a2_buf.at[:, c], AS2, sib).start()
    wait(qr_buf.at[pl.ds(0, S - 1)], recv.at[QKV])
    for j in range(S):
        x = qr_buf[j]
        q_scr[tok * j : tok * (j + 1)] = x[:tok, :DH]
        k_scr[tok * j : tok * (j + 1)] = x[:tok, DH:]
        v_scr[tok * j : tok * (j + 1)] = jnp.concatenate([x[tok:, :DH], x[tok:, DH:]], axis=0)

    inv_len = 1.0 / jnp.full((1, 1), length, jnp.int32).astype(F32)
    W = 2 * tok

    def attend(b):
        q = q_scr[W * b : W * (b + 1)]
        acc = jnp.zeros((W, DH), F32)
        for kb in range(b + 1):
            hs = dot_t(q, k_scr[W * kb : W * (kb + 1)]) * (0.5 * DH ** (-0.5))
            w = (hs * inv_len) * (1.0 + jnp.tanh(hs))
            if kb == b:
                r = lax.broadcasted_iota(jnp.int32, (W, W), 0)
                cc = lax.broadcasted_iota(jnp.int32, (W, W), 1)
                w = jnp.where(cc <= r, w, 0.0)
            acc = acc + dot(w.astype(BF), v_scr[W * kb : W * (kb + 1)])
        pos = W * b + lax.broadcasted_iota(jnp.int32, (W, 1), 0)
        acc = jnp.where(pos < length, acc, 0.0).astype(BF)
        for i in (0, 1):
            o = acc[tok * i : tok * (i + 1)]
            at_send[2 * b + i] = jnp.concatenate([o[: tok // 2], o[tok // 2 :]], axis=1)

    for b in reversed(range(S // 2)):
        attend(b)
    at_recv[s] = at_send[s]

    wait(h1_buf.at[pl.ds(0, S - 1)], recv.at[H1])
    wait(a2_buf.at[:, 0], recv.at[AS2])
    h1 = jnp.concatenate([h1_buf[j] for j in range(S)], axis=1)
    for j in range(NB):
        z2 = dot(h1, a2_buf[:, :, j].reshape(G * rows, 128))
        h2_buf[par, j] = silu(z2).astype(BF)
        sl2_buf[par, j] = silu_slope(z2).astype(BF)
    copy(h2_buf.at[par], h2_buf.at[par], H2, pair).start()

    def at_step(k, _):
        t = lax.rem(s + k, S)
        copy(at_send.at[t], at_recv.at[s], ATT, (t, g)).start()
        return 0

    lax.fori_loop(1, S, at_step, 0)
    wait(b_buf.at[pl.ds(0, C - 1), 0], recv.at[B])
    copy(b_buf.at[:, c], b_buf.at[:, c], BS, sib).start()

    wait(h2_buf.at[0], recv.at[H2])
    wait(b_buf.at[:, 0], recv.at[BS])
    h2 = whole(h2_buf)
    raw = dot(h2, b_buf[...].reshape(G * rows, 512))
    item_inverse = lax.rsqrt(jnp.sum(raw * raw, axis=-1, keepdims=True) + EPS_UNIT)
    unit_item = raw * item_inverse
    ui[...] = unit_item
    inv[...] = jnp.broadcast_to(item_inverse, inv.shape)
    pe_buf[p] = ui[pl.ds(pl.multiple_of(par * RH, RH), RH)].astype(BF)
    chips(pe_buf.at[p], pe_buf.at[p], PE)

    wait(wout_v, here.at[I_WOUT])
    wait(at_recv.at[pl.ds(0, S - 1)], recv.at[ATT])
    tops, bottoms = [], []
    for h in range(S):
        x = at_recv[h]
        tops.append(x[:, :DH])
        bottoms.append(x[:, DH:])
    merged = jnp.concatenate(
        [jnp.concatenate(tops, axis=1), jnp.concatenate(bottoms, axis=1)], axis=0).astype(F32)
    branch = (layer_norm(merged) * gate[...].astype(F32)).astype(BF)
    layer_out = (hist_v[...].astype(F32) + dot(branch, wout_v[...])).astype(BF)
    lo_ref[...] = layer_out
    outward = layer_out.astype(F32)
    user_inverse = lax.rsqrt(jnp.sum(outward * outward, axis=-1, keepdims=True) + EPS_UNIT)
    unit_user = outward * user_inverse
    u_buf[me] = unit_user.astype(BF)
    copy(u_buf.at[me], u_buf.at[me], UP, pair).start()
    copy(u_buf.at[me], u_buf.at[me], US, sib).start()
    uu[...] = unit_user
    uinv[...] = jnp.broadcast_to(user_inverse, (tok, 128))

    P4 = 4 * tok
    wait(nx_buf.at[pl.ds(0, 3)], recv.at[NX])
    items = local_row(jnp.concatenate([nx_buf[j] for j in range(4)], axis=1))
    quad_pos = lax.broadcasted_iota(jnp.int32, (1, P4), 1)
    positions = (s // 2) * W + quad_pos % W
    lens = jnp.concatenate([neg_buf[j // 2, :, NEG:] for j in range(4)], axis=1)
    valid = (positions < lens - 1).astype(F32)

    copy(sl2_buf.at[par], sl2_buf.at[par], SL2, pair).start()
    wait(u_buf.at[0], recv.at[UP])
    other = 2 * c + 1 - par
    copy(u_buf.at[other], u_buf.at[other], UT, sib).start()
    wait(pe_buf.at[pl.ds(0, C - 1)], recv.at[PE])
    wait(u_buf.at[0], recv.at[US])
    wait(u_buf.at[0], recv.at[UT])

    Q = 4
    CQ = C // Q
    width = n_rows // Q
    users = u_buf[...].reshape(P4, 512)
    row_id = lax.broadcasted_iota(jnp.int32, (width, P4), 0)
    den = jnp.zeros((1, P4), F32)
    positive = jnp.zeros((1, P4), F32)
    for q in range(Q):
        logit = TEMP * dot_t(pe_buf[CQ * q : CQ * (q + 1)].reshape(width, 512), users)
        own = row_id + width * q == items
        times = jnp.concatenate([cnt[j // 2, width * q : width * (q + 1)] for j in range(4)], axis=1)
        e = jnp.where(own, 0.0, jnp.exp(logit) * times)
        em[q] = e
        den = den + jnp.sum(e, axis=0, keepdims=True)
        positive = positive + jnp.sum(jnp.where(own, logit, 0.0), axis=0, keepdims=True)
    row8 = lax.broadcasted_iota(jnp.int32, (8, P4), 0)
    dn_buf[me] = jnp.where(row8 == 0, den, positive)
    quad(dn_buf, DN)
    wait(dn_buf.at[pl.ds(0, 3)], recv.at[DN])
    sums = dn_buf[0] + dn_buf[1] + dn_buf[2] + dn_buf[3]
    den = sums[0:1]
    positive = sums[1:2]
    positive_exp = jnp.exp(positive)
    den = den + positive_exp
    slope = valid * (positive_exp / den - 1.0)
    scale = valid / den

    for q in range(Q):
        st[q] = jnp.where(row_id + width * q == items, slope, scale * em[q]).astype(BF)
    half_cols = 256

    def pool_half(e):
        part = TEMP * dot(st[...].reshape(n_rows, P4), users[:, half_cols * e : half_cols * (e + 1)])
        rs_send[e] = part.astype(BF).reshape(C, RH, half_cols)

    pool_half(0)
    chip_scatter(rs_send.at[0], rs_recv.at[0], RS)

    per_block = 128 // (2 * rows)
    copy(a2_buf.at[pl.ds(per_block * (s + 1 - 2 * par), per_block)], w2r_buf.at[par], W2, pair).start()
    w2r_buf[par] = a2_buf[pl.ds(per_block * s, per_block)]

    mine = quad_pos // tok == me
    loss_sum = jnp.sum(jnp.where(mine, valid * (jnp.log(den) - positive), 0.0))
    lane = lax.broadcasted_iota(jnp.int32, (8, 128), 1)
    count = jnp.full((8, 128), length - 1, jnp.int32).astype(F32)
    zl_buf[s] = jnp.where(lane == 0, loss_sum, jnp.where(lane == 1, count, 0.0))
    z_bcast(zl_buf, ZL)

    user_dir = t_dot(st[...].reshape(n_rows, P4), pe_buf[...].reshape(n_rows, 512))
    ud[...] = user_dir.reshape(2, 2, tok, 512)
    uds_send[...] = ud[1 - c].astype(BF)
    copy(uds_send, uds_recv, UDS, sib).start()

    pool_half(1)
    wait(rs_recv.at[0, pl.ds(0, C - 1)], send.at[RS])
    chip_scatter(rs_send.at[1], rs_recv.at[1], RS + 1)

    def plane_sum(e):
        wait(rs_recv.at[e, pl.ds(0, C - 1)], recv.at[RS + e])
        za_buf[e, s] = jnp.sum(rs_recv[e].astype(F32), axis=0).astype(BF)
        z_bcast(za_buf.at[e], ZA + e)

    plane_sum(0)
    plane_sum(1)

    wait(uds_recv, recv.at[UDS])
    udp_send[...] = (ud[c, 1 - par] + uds_recv[1 - par].astype(F32)).astype(BF)
    copy(udp_send, udp_recv, UDP, pair).start()
    wait(zl_buf.at[pl.ds(0, S - 1)], recv.at[ZL])
    lg_buf[g] = jnp.sum(zl_buf[...], axis=0)

    def lg_step(k, _):
        copy(lg_buf.at[g], lg_buf.at[g], GL, (s, lax.rem(g + k, G))).start()
        return 0

    lax.fori_loop(1, G, lg_step, 0)
    wait(w2r_buf.at[0], recv.at[W2])
    w2_rows = jnp.concatenate([w2r_buf[j % 2, :, :, j // 2].reshape(128, 128) for j in range(2 * NB)], axis=1)
    wait(sl2_buf.at[0], recv.at[SL2])
    h1 = jnp.concatenate([h1_buf[j] for j in range(S)], axis=1)
    h2 = whole(h2_buf)
    slope2 = whole(sl2_buf).astype(F32)
    slope1 = silu_slope(pre1[...])

    for e in (0, 1):
        wait(za_buf.at[e, pl.ds(0, S - 1)], recv.at[ZA + e])
    halves = []
    for e in (0, 1):
        sums = []
        for o in (0, 1):
            part = za_buf[e, o].astype(F32)
            for t in range(o + 2, S, 2):
                part = part + za_buf[e, t].astype(F32)
            sums.append(part)
        halves.append(jnp.concatenate(sums, axis=0))
    own_grad = jnp.concatenate(halves, axis=1)
    uin = ui[...]
    raw_grad = (inv[:, :1] * (own_grad - uin * jnp.sum(uin * own_grad, axis=-1, keepdims=True))).astype(BF)
    rg[...] = raw_grad
    sg = (dot_t(raw_grad, b_buf[...].reshape(G * rows, 512)) * slope2).astype(BF)
    sg_scr[...] = sg
    fg = (dot_t(sg, w2_rows) * slope1).astype(BF)
    gp2[...] = t_dot(xf_v[...], fg).astype(BF).reshape(C, 2, rows, 128)
    copy(gp2.at[:, 1 - c], gp2_recv, GP2, sib).start()
    q_cols = pl.ds(pl.multiple_of(lax.rem(s, 4) * 128, 128), 128)
    gl_scr[...] = t_dot(h2, rg[:, q_cols]).astype(BF).reshape(C, 2, 2, half, 128)
    gp1[:, :, :rows] = t_dot(h1, sg_scr[:, cols]).astype(BF).reshape(C, 2, rows, 128)
    gp1[:, :, rows:] = gl_scr[:, :, s // 4]
    copy(gp1.at[:, 1 - c], gp1_recv, GP1, sib).start()
    wait(gp2_recv, recv.at[GP2])
    g2_send[...] = (gp2[:, c].astype(F32) + gp2_recv[...].astype(F32)).astype(BF)
    chip_scatter(g2_send, g2_recv, G2)
    wait(gp1_recv, recv.at[GP1])
    g1_send[...] = (gp1[:, c].astype(F32) + gp1_recv[...].astype(F32)).astype(BF)
    chip_scatter(g1_send, g1_recv, G1)

    wait(udp_recv, recv.at[UDP])
    user_dir = TEMP * (ud[c, par] + uds_recv[par].astype(F32) + udp_recv[...].astype(F32))
    uun = uu[...]
    ug_ref[...] = uinv[:, :1] * (user_dir - uun * jnp.sum(uun * user_dir, axis=-1, keepdims=True))
    wait(lg_buf.at[pl.ds(0, G - 1)], recv.at[GL])
    total = jnp.sum(lg_buf[...], axis=0)
    numer = jnp.sum(jnp.where(lane == 0, total, 0.0), axis=1, keepdims=True)
    denom = jnp.sum(jnp.where(lane == 1, total, 0.0), axis=1, keepdims=True)
    loss_ref[...] = jnp.broadcast_to(numer * S / denom, loss_ref.shape)

    wait(g2_recv.at[pl.ds(0, C - 1)], recv.at[G2])
    f2_buf[s] = jnp.sum(g2_recv[...].astype(F32), axis=0).astype(BF)
    z_bcast(f2_buf, F2)
    wait(g1_recv.at[pl.ds(0, C - 1)], recv.at[G1])
    f1_buf[s] = jnp.sum(g1_recv[...].astype(F32), axis=0).astype(BF)
    z_bcast(f1_buf, F1)

    wait(a_buf.at[pl.ds(0, C - 1), 0], send.at[A])
    wait(a2_buf.at[pl.ds(0, C - 1), 0], send.at[A2])
    wait(a2_buf.at[:, 0], send.at[AS2])
    wait(b_buf.at[pl.ds(0, C - 1), 0], send.at[B])
    wait(a_buf.at[:, 0], send.at[AS])
    wait(b_buf.at[:, 0], send.at[BS])
    wait(pe_buf.at[pl.ds(0, C - 1)], send.at[PE])
    wait(rs_recv.at[1, pl.ds(0, C - 1)], send.at[RS + 1])
    for e in (0, 1):
        wait(za_buf.at[e, pl.ds(0, S - 1)], send.at[ZA + e])
    for buf, i in ((qr_buf, QKV), (at_recv, ATT), (zl_buf, ZL)):
        wait(buf.at[pl.ds(0, S - 1)], send.at[i])
    wait(h1_buf.at[pl.ds(0, S - 1)], send.at[H1])
    wait(h2_buf.at[0], send.at[H2])
    wait(sl2_buf.at[0], send.at[SL2])
    wait(nx_buf.at[pl.ds(0, 3)], send.at[NX])
    wait(neg_buf.at[0], send.at[NG])
    for i in (UP, US, UT):
        wait(u_buf.at[0], send.at[i])
    wait(dn_buf.at[pl.ds(0, 3)], send.at[DN])
    wait(uds_recv, send.at[UDS])
    wait(udp_recv, send.at[UDP])
    wait(gp1_recv, send.at[GP1])
    wait(gp2_recv, send.at[GP2])
    wait(lg_buf.at[pl.ds(0, G - 1)], send.at[GL])
    wait(g1_recv.at[pl.ds(0, C - 1)], send.at[G1])
    wait(g2_recv.at[pl.ds(0, C - 1)], send.at[G2])
    wait(w2r_buf.at[0], send.at[W2])

    wait(f2_buf.at[pl.ds(0, S - 1)], recv.at[F2])
    for t in range(S):
        gf_ref[:, 128 * t : 128 * (t + 1)] = f2_buf[t].astype(F32)
    wait(f1_buf.at[pl.ds(0, S - 1)], recv.at[F1])
    for t in range(S):
        gm_ref[:, 128 * t : 128 * (t + 1)] = f1_buf[t, :rows].astype(F32)
        gl_ref[half * (t // 4) : half * (t // 4 + 1), 128 * (t % 4) : 128 * (t % 4 + 1)] = f1_buf[t, rows:].astype(F32)
    wait(f1_buf.at[pl.ds(0, S - 1)], send.at[F1])
    wait(f2_buf.at[pl.ds(0, S - 1)], send.at[F2])


def tail(*refs):
    ins, outs, sem = refs[:6], refs[6:12], refs[12]
    for i in (0, 2, 3, 4, 5):
        pltpu.make_async_copy(ins[i], outs[i], sem.at[i]).start()
    outs[1][0, 0] = jnp.max(ins[1][...])
    for i in (0, 2, 3, 4, 5):
        pltpu.make_async_copy(ins[i], outs[i], sem.at[i]).wait()


def local(history, lengths, next_items, negatives, input_weight, output_weight, pool_features,
          tower_first, tower_middle, tower_last, S, G):
    events = history[0]
    tok = events.shape[0]
    C = G // 2
    R = pool_features.shape[0]
    RH = R // 2
    rows = tower_first.shape[0]
    V = pltpu.VMEM
    vmem = pl.BlockSpec(memory_space=pltpu.VMEM)
    hbm = pl.BlockSpec(memory_space=pltpu.HBM)
    width = C * RH // 4
    scratch = [
        pltpu.SemaphoreType.DMA((N_SEM,)),
        pltpu.SemaphoreType.DMA((N_SEM,)),
        pltpu.SemaphoreType.DMA((N_HERE,)),
        V((tok, 512), BF),
        V((4, 1, tok), jnp.int32),
        V((2, 1, negatives.shape[1] + 128), jnp.int32),
        V(input_weight.shape, BF),
        V(output_weight.shape, BF),
        V(pool_features.shape, BF),
        V((C, 2, rows, 128), BF),
        V((C, 2, 4, rows, 128), BF),
        V((C, 2, rows, 512), BF),
        V((2, 128 // (2 * rows), 2, 4, rows, 128), BF),
        V((S, tok + tok // 2, 128), BF),
        V((S, tok + tok // 2, 128), BF),
        V((tok, 512), BF),
        V((S * tok, DH), BF),
        V((S * tok, DH), BF),
        V((S * tok, DH), BF),
        V((S, tok // 2, 128), BF),
        V((S, tok // 2, 128), BF),
        V((S, R, 128), BF),
        V((2, 4, R, 128), BF),
        V((2, 4, R, 128), BF),
        V((R, 128), F32),
        V((R, 512), F32),
        V((R, 128), F32),
        V((C, RH, 512), BF),
        V((4, width, 4 * tok), F32),
        V((4, width, 4 * tok), BF),
        V((2, C, RH, 256), BF),
        V((2, C, RH, 256), BF),
        V((4, tok, 512), BF),
        V((4, 8, 4 * tok), F32),
        V((2, 2, tok, 512), F32),
        V((2, tok, 512), BF),
        V((2, tok, 512), BF),
        V((tok, 512), BF),
        V((tok, 512), BF),
        V((S, 8, 128), F32),
        V((G, 8, 128), F32),
        V((2, S, RH, 256), BF),
        V((R, 512), BF),
        V((R, 1024), BF),
        V((C, 2, 2, rows // 2, 128), BF),
        V((C, 2, rows + rows // 2, 128), BF),
        V((C, rows + rows // 2, 128), BF),
        V((C, 2, rows, 128), BF),
        V((C, rows, 128), BF),
        V((C, rows + rows // 2, 128), BF),
        V((C, rows + rows // 2, 128), BF),
        V((C, rows, 128), BF),
        V((C, rows, 128), BF),
        V((S, rows + rows // 2, 128), BF),
        V((S, rows, 128), BF),
        V((2, C * RH, 128), F32),
        V((tok, 512), F32),
        V((tok, 128), F32),
    ]
    shapes = [
        jax.ShapeDtypeStruct((tok, 512), BF),
        jax.ShapeDtypeStruct((8, 128), F32),
        jax.ShapeDtypeStruct((tok, 512), F32),
        jax.ShapeDtypeStruct((rows, 1024), F32),
        jax.ShapeDtypeStruct((rows, 1024), F32),
        jax.ShapeDtypeStruct((rows, 512), F32),
    ]
    results = pl.pallas_call(
        functools.partial(kernel, S, G),
        out_shape=[pltpu.VMEM(x.shape, x.dtype) for x in shapes],
        in_specs=[pl.BlockSpec(memory_space=pltpu.SMEM)] + [hbm] * 9,
        out_specs=[vmem] * 6,
        scratch_shapes=scratch,
        compiler_params=pltpu.CompilerParams(
            collective_id=0, has_side_effects=True, vmem_limit_bytes=56 * 1024 * 1024),
    )(lengths, events, next_items, negatives, input_weight, output_weight, pool_features,
      tower_first, tower_middle, tower_last)
    lo, loss, ug, gf, gm, gl = pl.pallas_call(
        tail,
        out_shape=shapes[:1] + [jax.ShapeDtypeStruct((1, 1), F32)] + shapes[2:],
        in_specs=[vmem] * 6,
        out_specs=[hbm, pl.BlockSpec(memory_space=pltpu.SMEM)] + [hbm] * 4,
        scratch_shapes=[pltpu.SemaphoreType.DMA((6,))],
        compiler_params=pltpu.CompilerParams(vmem_limit_bytes=1024 * 1024),
    )(*results)
    return lo[None], loss.reshape(()), ug[None], gf, gm, gl


def solution(mesh):
    placed = (
        P("grp", "seq", None), P("grp"), P("grp", "seq"), P("grp", None), P(), P(),
        P("grp", None), P("grp", None), P("grp", None), P("grp", None),
    )
    return jax.shard_map(
        functools.partial(local, S=mesh.shape["seq"], G=mesh.shape["grp"]),
        mesh=mesh,
        in_specs=placed,
        out_specs=(
            P("grp", "seq", None), P(), P("grp", "seq", None),
            P("grp", None), P("grp", None), P("grp", None),
        ),
        check_vma=False,
    )
```

```python
import functools

import jax
import jax.numpy as jnp
from jax import lax
from jax.experimental import pallas as pl
from jax.experimental.pallas import tpu as pltpu
from jax.sharding import PartitionSpec as P

DH = 64
EPS_NORM = 1e-05
EPS_UNIT = 1e-06
TEMP = 20.0

MESH = pl.DeviceIdType.MESH
BF = jnp.bfloat16
F32 = jnp.float32

(A, A2, B, AS, AS2, BS, QKV, ATT, H1, H2, SL2, NX, NG, UP, US, UT, DN, UDS, UDP, ZL, GL, GP1, G1, G2, F1, F2,
 W2, PE) = range(28)
RS, ZA = 28, 30
N_SEM = 32

PARTS = ((0, 256), (256, 256))

(I_W3, I_H, I_WIN, I_WOUT, I_X, I_NEG, I_NXT, I_W1) = range(8)
I_W2 = 8
N_HERE = 12


def silu(x):
    half = 0.5 * x
    return half * (1.0 + jnp.tanh(half))


def silu_slope(z):
    sigma = 0.5 * (1.0 + jnp.tanh(0.5 * z))
    return sigma * (1.0 + z * (1.0 - sigma))


def layer_norm(values):
    center = values - jnp.mean(values, axis=-1, keepdims=True)
    spread = jnp.mean(center * center, axis=-1, keepdims=True)
    return center * lax.rsqrt(spread + EPS_NORM)


def dot(a, b):
    return jnp.dot(a, b, preferred_element_type=F32)


def dot_t(a, b):
    return lax.dot_general(a, b, (((1,), (1,)), ((), ())), preferred_element_type=F32)


def t_dot(a, b):
    return lax.dot_general(a, b, (((0,), (0,)), ((), ())), preferred_element_type=F32)


def wait(ref, sem):
    pltpu.make_async_copy(ref, ref, sem).wait()


def kernel(
    S, G,
    len_ref, hist, nxt, neg, win, wout, xf, w1, w2, w3,
    lo_ref, loss_ref, ug_ref, gf_ref, gm_ref, gl_ref,
    send, recv, here,
    hist_v, nx_buf, neg_buf, win_v, wout_v, xf_v,
    a_buf, a2_buf, b_buf, w2r_buf, qs_buf, qr_buf, gate, k_scr, q_scr, v_scr, at_send, at_recv,
    h1_buf, h2_buf, sl2_buf, pre1, ui, inv, pe_buf, em, st, u_buf,
    dn_buf, nll, ud, uds_send, uds_recv, udp_send, udp_recv, zl_buf, lg_buf, rg, sg_scr,
    gl_scr, gp1, gp1_recv, g1_send, g1_recv, g2_send, g2_recv, f1_buf, f2_buf, cnt, uu, uinv, *parts,
):
    C = G // 2
    s = lax.axis_index("seq")
    g = lax.axis_index("grp")
    p = g // 2
    c = g % 2
    par = s % 2
    tok = hist_v.shape[0]
    me = 2 * c + par
    rows = b_buf.shape[2]
    NB = a2_buf.shape[2]
    half = rows // 2
    NEG = neg.shape[1]
    R = xf_v.shape[0]
    RH = R // 2
    length = len_ref[0]
    pair = (s + 1 - 2 * par, g)
    sib = (s, 2 * p + 1 - c)
    diag = (s + 1 - 2 * par, 2 * p + 1 - c)
    cols = pl.ds(pl.multiple_of(s * 128, 128), 128)

    def copy(src, dst, i, dev):
        return pltpu.make_async_remote_copy(
            src_ref=src, dst_ref=dst, send_sem=send.at[i], recv_sem=recv.at[i],
            device_id=dev, device_id_type=MESH)

    def fetch(src, dst, i):
        pltpu.make_async_copy(src, dst, here.at[i]).start()

    def z_bcast(buf, i):
        def step(k, _):
            copy(buf.at[s], buf.at[s], i, (lax.rem(s + k, S), g)).start()
            return 0
        lax.fori_loop(1, S, step, 0)

    def chips(src, dst, i):
        def step(k, _):
            copy(src, dst, i, (s, 2 * lax.rem(p + k, C) + c)).start()
            return 0
        lax.fori_loop(1, C, step, 0)

    def chip_scatter(src, dst, i):
        def step(k, _):
            t = lax.rem(p + k, C)
            copy(src.at[t], dst.at[p], i, (s, 2 * t + c)).start()
            return 0
        lax.fori_loop(1, C, step, 0)
        dst[p] = src[p]

    rs_send, rs_recv, za_buf = parts[0:2], parts[2:4], parts[4:6]

    def grp_scatter(src, dst, i):
        def step(k, _):
            t = lax.rem(g + k, G)
            copy(src.at[t], dst.at[g], i, (s, t)).start()
            return 0
        lax.fori_loop(1, G, step, 0)
        dst[g] = src[g]

    def quad(buf, i):
        for dev in (sib, pair, diag):
            copy(buf.at[me], buf.at[me], i, dev).start()

    fetch(w1.at[:, cols], a_buf.at[p, c], I_W1)
    barrier = pltpu.get_barrier_semaphore()

    def greet_grp(k, _):
        pl.semaphore_signal(barrier, inc=1, device_id=(s, lax.rem(g + k, G)), device_id_type=MESH)
        return 0

    def greet_seq(k, _):
        pl.semaphore_signal(barrier, inc=1, device_id=(lax.rem(s + k, S), g), device_id_type=MESH)
        return 0

    lax.fori_loop(1, G, greet_grp, 0)
    lax.fori_loop(1, S, greet_seq, 0)
    pl.semaphore_signal(barrier, inc=1, device_id=diag, device_id_type=MESH)

    for j in range(NB):
        block = pl.ds(pl.multiple_of((2 * j + par) * 128, 128), 128)
        fetch(w2.at[:, block], a2_buf.at[p, c, j], I_W2 + j)
    fetch(hist, hist_v, I_H)
    fetch(win, win_v, I_WIN)
    fetch(nxt, nx_buf.at[me], I_NXT)
    fetch(w3, b_buf.at[p, c], I_W3)
    fetch(xf, xf_v, I_X)
    fetch(neg, neg_buf.at[c, :, pl.ds(0, NEG)], I_NEG)
    fetch(wout, wout_v, I_WOUT)
    neg_buf[c, :, NEG:] = jnp.full((1, 128), length, jnp.int32)
    wait(a_buf.at[p, c], here.at[I_W1])
    pl.semaphore_wait(barrier, (G - 1) + (S - 1) + 1)
    chips(a_buf.at[p, c], a_buf.at[p, c], A)

    wait(hist_v, here.at[I_H])
    normed = layer_norm(hist_v[...].astype(F32)).astype(BF)
    wait(win_v, here.at[I_WIN])
    for j in range(4):
        x = silu(dot(normed, win_v[:, 512 + 384 * j : 512 + 384 * (j + 1)])).astype(BF)
        for e in (0, 1):
            o = 192 * e
            qs_buf[2 * j + e, :tok] = x[:, o : o + 128]
            v = x[:, o + 128 : o + 192]
            qs_buf[2 * j + e, tok:] = jnp.concatenate([v[: tok // 2], v[tok // 2 :]], axis=1)

    def qkv_step(k, _):
        t = lax.rem(s + k, S)
        copy(qs_buf.at[t], qr_buf.at[s], QKV, (t, g)).start()
        return 0

    lax.fori_loop(1, S, qkv_step, 0)
    qr_buf[s] = qs_buf[s]
    for j in range(NB):
        wait(a2_buf.at[p, c, j], here.at[I_W2 + j])
    chips(a2_buf.at[p, c], a2_buf.at[p, c], A2)
    wait(nx_buf.at[me], here.at[I_NXT])
    quad(nx_buf, NX)
    wait(neg_buf.at[c, :, pl.ds(0, NEG)], here.at[I_NEG])
    copy(neg_buf.at[c], neg_buf.at[c], NG, sib).start()
    gate[...] = silu(dot(normed, win_v[:, :512])).astype(BF)

    wait(xf_v, here.at[I_X])
    wait(a_buf.at[pl.ds(0, C - 1), 0], recv.at[A])
    copy(a_buf.at[:, c], a_buf.at[:, c], AS, sib).start()
    wait(b_buf.at[p, c], here.at[I_W3])
    chips(b_buf.at[p, c], b_buf.at[p, c], B)
    wait(a_buf.at[:, 0], recv.at[AS])
    z1 = dot(xf_v[...], a_buf[...].reshape(G * rows, 128))
    pre1[...] = z1
    h1_buf[s] = silu(z1).astype(BF)
    z_bcast(h1_buf, H1)

    def local_row(ids):
        return jnp.where((ids // RH) % 4 == me, (ids // (2 * R)) * RH + ids % RH, -1)

    wait(neg_buf.at[0], recv.at[NG])
    n_rows = C * RH
    for e in (0, 1):
        ids = local_row(neg_buf[e, :, :NEG])
        hot = (lax.broadcasted_iota(jnp.int32, (n_rows, NEG), 0) == ids).astype(F32).astype(BF)
        cnt[e] = dot(hot, jnp.ones((NEG, 128), BF))
    def whole(buf):
        return jnp.concatenate([buf[j % 2, j // 2] for j in range(2 * NB)], axis=1)

    wait(a2_buf.at[pl.ds(0, C - 1), 0], recv.at[A2])
    copy(a2_buf.at[:, c], a2_buf.at[:, c], AS2, sib).start()
    wait(qr_buf.at[pl.ds(0, S - 1)], recv.at[QKV])
    for j in range(S):
        x = qr_buf[j]
        q_scr[tok * j : tok * (j + 1)] = x[:tok, :DH]
        k_scr[tok * j : tok * (j + 1)] = x[:tok, DH:]
        v_scr[tok * j : tok * (j + 1)] = jnp.concatenate([x[tok:, :DH], x[tok:, DH:]], axis=0)

    inv_len = 1.0 / jnp.full((1, 1), length, jnp.int32).astype(F32)
    W = 2 * tok

    def attend(b):
        q = q_scr[W * b : W * (b + 1)]
        acc = jnp.zeros((W, DH), F32)
        for kb in range(b + 1):
            hs = dot_t(q, k_scr[W * kb : W * (kb + 1)]) * (0.5 * DH ** (-0.5))
            w = (hs * inv_len) * (1.0 + jnp.tanh(hs))
            if kb == b:
                r = lax.broadcasted_iota(jnp.int32, (W, W), 0)
                cc = lax.broadcasted_iota(jnp.int32, (W, W), 1)
                w = jnp.where(cc <= r, w, 0.0)
            acc = acc + dot(w.astype(BF), v_scr[W * kb : W * (kb + 1)])
        pos = W * b + lax.broadcasted_iota(jnp.int32, (W, 1), 0)
        acc = jnp.where(pos < length, acc, 0.0).astype(BF)
        for i in (0, 1):
            o = acc[tok * i : tok * (i + 1)]
            at_send[2 * b + i] = jnp.concatenate([o[: tok // 2], o[tok // 2 :]], axis=1)

    for b in reversed(range(S // 2)):
        attend(b)
    at_recv[s] = at_send[s]

    def at_step(k, _):
        t = lax.rem(s + k, S)
        copy(at_send.at[t], at_recv.at[s], ATT, (t, g)).start()
        return 0

    lax.fori_loop(1, S, at_step, 0)
    wait(h1_buf.at[pl.ds(0, S - 1)], recv.at[H1])
    wait(a2_buf.at[:, 0], recv.at[AS2])
    h1 = jnp.concatenate([h1_buf[j] for j in range(S)], axis=1)
    for j in range(NB):
        z2 = dot(h1, a2_buf[:, :, j].reshape(G * rows, 128))
        h2_buf[par, j] = silu(z2).astype(BF)
        sl2_buf[par, j] = silu_slope(z2).astype(BF)
    copy(h2_buf.at[par], h2_buf.at[par], H2, pair).start()

    wait(b_buf.at[pl.ds(0, C - 1), 0], recv.at[B])
    copy(b_buf.at[:, c], b_buf.at[:, c], BS, sib).start()

    wait(h2_buf.at[0], recv.at[H2])
    wait(b_buf.at[:, 0], recv.at[BS])
    h2 = whole(h2_buf)
    raw = dot(h2, b_buf[...].reshape(G * rows, 512))
    item_inverse = lax.rsqrt(jnp.sum(raw * raw, axis=-1, keepdims=True) + EPS_UNIT)
    unit_item = raw * item_inverse
    ui[...] = unit_item
    inv[...] = jnp.broadcast_to(item_inverse, inv.shape)
    pe_buf[p] = ui[pl.ds(pl.multiple_of(par * RH, RH), RH)].astype(BF)
    chips(pe_buf.at[p], pe_buf.at[p], PE)

    wait(wout_v, here.at[I_WOUT])
    wait(at_recv.at[pl.ds(0, S - 1)], recv.at[ATT])
    tops, bottoms = [], []
    for h in range(S):
        x = at_recv[h]
        tops.append(x[:, :DH])
        bottoms.append(x[:, DH:])
    merged = jnp.concatenate(
        [jnp.concatenate(tops, axis=1), jnp.concatenate(bottoms, axis=1)], axis=0).astype(F32)
    branch = (layer_norm(merged) * gate[...].astype(F32)).astype(BF)
    layer_out = (hist_v[...].astype(F32) + dot(branch, wout_v[...])).astype(BF)
    lo_ref[...] = layer_out
    outward = layer_out.astype(F32)
    user_inverse = lax.rsqrt(jnp.sum(outward * outward, axis=-1, keepdims=True) + EPS_UNIT)
    unit_user = outward * user_inverse
    u_buf[me] = unit_user.astype(BF)
    copy(u_buf.at[me], u_buf.at[me], UP, pair).start()
    copy(u_buf.at[me], u_buf.at[me], US, sib).start()
    uu[...] = unit_user
    uinv[...] = jnp.broadcast_to(user_inverse, (tok, 128))

    wait(nx_buf.at[pl.ds(0, 3)], recv.at[NX])
    pair_pos = lax.broadcasted_iota(jnp.int32, (1, W), 1)
    positions = (s // 2) * W + pair_pos

    def items_of(u):
        return local_row(jnp.concatenate([nx_buf[2 * u], nx_buf[2 * u + 1]], axis=1))

    def valid_of(u):
        lens = neg_buf[u, :, NEG:]
        return (positions < jnp.concatenate([lens, lens], axis=1) - 1).astype(F32)

    copy(sl2_buf.at[par], sl2_buf.at[par], SL2, pair).start()
    wait(u_buf.at[0], recv.at[UP])
    other = 2 * c + 1 - par
    copy(u_buf.at[other], u_buf.at[other], UT, sib).start()
    wait(pe_buf.at[pl.ds(0, C - 1)], recv.at[PE])

    Q = 4
    CQ = C // Q
    width = n_rows // Q
    row_id = lax.broadcasted_iota(jnp.int32, (width, W), 0)

    def logits_of(u):
        users = u_buf[pl.ds(2 * u, 2)].reshape(W, 512)
        items = items_of(u)
        den = jnp.zeros((1, W), F32)
        positive = jnp.zeros((1, W), F32)
        for q in range(Q):
            logit = TEMP * dot_t(pe_buf[CQ * q : CQ * (q + 1)].reshape(width, 512), users)
            own = row_id + width * q == items
            times = cnt[u, width * q : width * (q + 1)]
            e = jnp.where(own, 0.0, jnp.exp(logit) * jnp.concatenate([times, times], axis=1))
            em[u, width * q : width * (q + 1)] = e
            den = den + jnp.sum(e, axis=0, keepdims=True)
            positive = positive + jnp.sum(jnp.where(own, logit, 0.0), axis=0, keepdims=True)
        dn_buf[me, u] = jnp.concatenate([den, positive], axis=1)

    logits_of(c)
    wait(u_buf.at[0], recv.at[US])
    wait(u_buf.at[0], recv.at[UT])
    logits_of(1 - c)
    quad(dn_buf, DN)
    wait(dn_buf.at[pl.ds(0, 3)], recv.at[DN])
    for u in (0, 1):
        sums = dn_buf[0, u] + dn_buf[1, u] + dn_buf[2, u] + dn_buf[3, u]
        positive = sums[:, W:]
        positive_exp = jnp.exp(positive)
        den = sums[:, :W] + positive_exp
        valid = valid_of(u)
        items = items_of(u)
        slope = valid * (positive_exp / den - 1.0)
        scale = valid / den
        for q in range(Q):
            block = slice(width * q, width * (q + 1))
            st[u, block] = jnp.where(row_id + width * q == items, slope, scale * em[u, block]).astype(BF)
        nll[u] = valid * (jnp.log(den) - positive)

    def pool_part(e):
        lo, n = PARTS[e]
        part = dot(st[0], u_buf[0:2, :, lo : lo + n].reshape(W, n))
        part = part + dot(st[1], u_buf[2:4, :, lo : lo + n].reshape(W, n))
        rs_send[e][...] = (TEMP * part).astype(BF).reshape(C, RH, n)

    pool_part(0)
    chip_scatter(rs_send[0], rs_recv[0], RS)

    per_block = 128 // (2 * rows)
    copy(a2_buf.at[pl.ds(per_block * (s + 1 - 2 * par), per_block)], w2r_buf.at[par], W2, pair).start()
    w2r_buf[par] = a2_buf[pl.ds(per_block * s, per_block)]

    mine = pair_pos // tok == par
    loss_sum = jnp.sum(jnp.where(mine, nll[c], 0.0))
    lane = lax.broadcasted_iota(jnp.int32, (8, 128), 1)
    count = jnp.full((8, 128), length - 1, jnp.int32).astype(F32)
    zl_buf[s] = jnp.where(lane == 0, loss_sum, jnp.where(lane == 1, count, 0.0))
    z_bcast(zl_buf, ZL)

    rows_here = pe_buf[...].reshape(n_rows, 512)
    for u in (0, 1):
        ud[u] = t_dot(st[u], rows_here).reshape(2, tok, 512)
    uds_send[...] = ud[1 - c].astype(BF)
    copy(uds_send, uds_recv, UDS, sib).start()

    pool_part(1)
    wait(rs_recv[0].at[pl.ds(0, C - 1)], send.at[RS])
    chip_scatter(rs_send[1], rs_recv[1], RS + 1)

    def plane_sum(e):
        wait(rs_recv[e].at[pl.ds(0, C - 1)], recv.at[RS + e])
        za_buf[e][s] = jnp.sum(rs_recv[e][...].astype(F32), axis=0).astype(BF)
        z_bcast(za_buf[e], ZA + e)

    plane_sum(0)
    plane_sum(1)
    wait(uds_recv, recv.at[UDS])
    udp_send[...] = (ud[c, 1 - par] + uds_recv[1 - par].astype(F32)).astype(BF)
    copy(udp_send, udp_recv, UDP, pair).start()

    wait(zl_buf.at[pl.ds(0, S - 1)], recv.at[ZL])
    lg_buf[g] = jnp.sum(zl_buf[...], axis=0)

    def lg_step(k, _):
        copy(lg_buf.at[g], lg_buf.at[g], GL, (s, lax.rem(g + k, G))).start()
        return 0

    lax.fori_loop(1, G, lg_step, 0)
    wait(w2r_buf.at[0], recv.at[W2])
    w2_rows = jnp.concatenate([w2r_buf[j % 2, :, :, j // 2].reshape(128, 128) for j in range(2 * NB)], axis=1)
    wait(sl2_buf.at[0], recv.at[SL2])
    h1 = jnp.concatenate([h1_buf[j] for j in range(S)], axis=1)
    h2 = whole(h2_buf)
    slope2 = whole(sl2_buf).astype(F32)
    slope1 = silu_slope(pre1[...])

    for e in range(2):
        wait(za_buf[e].at[pl.ds(0, S - 1)], recv.at[ZA + e])
    chunks = []
    for e in range(2):
        sums = []
        for o in (0, 1):
            part = za_buf[e][o].astype(F32)
            for t in range(o + 2, S, 2):
                part = part + za_buf[e][t].astype(F32)
            sums.append(part)
        chunks.append(jnp.concatenate(sums, axis=0))
    own_grad = jnp.concatenate(chunks, axis=1)
    uin = ui[...]
    raw_grad = (inv[:, :1] * (own_grad - uin * jnp.sum(uin * own_grad, axis=-1, keepdims=True))).astype(BF)
    rg[...] = raw_grad
    sg = (dot_t(raw_grad, b_buf[...].reshape(G * rows, 512)) * slope2).astype(BF)
    sg_scr[...] = sg
    fg = (dot_t(sg, w2_rows) * slope1).astype(BF)
    g2_send[...] = t_dot(xf_v[...], fg).astype(BF).reshape(G, rows, 128)
    grp_scatter(g2_send, g2_recv, G2)
    q_cols = pl.ds(pl.multiple_of(lax.rem(s, 4) * 128, 128), 128)
    gl_scr[...] = t_dot(h2, rg[:, q_cols]).astype(BF).reshape(C, 2, 2, half, 128)
    gp1[:, :, :rows] = t_dot(h1, sg_scr[:, cols]).astype(BF).reshape(C, 2, rows, 128)
    gp1[:, :, rows:] = gl_scr[:, :, s // 4]
    copy(gp1.at[:, 1 - c], gp1_recv, GP1, sib).start()
    wait(gp1_recv, recv.at[GP1])
    g1_send[...] = (gp1[:, c].astype(F32) + gp1_recv[...].astype(F32)).astype(BF)
    chip_scatter(g1_send, g1_recv, G1)

    wait(udp_recv, recv.at[UDP])
    user_dir = TEMP * (ud[c, par] + uds_recv[par].astype(F32) + udp_recv[...].astype(F32))
    uun = uu[...]
    ug_ref[...] = uinv[:, :1] * (user_dir - uun * jnp.sum(uun * user_dir, axis=-1, keepdims=True))
    wait(lg_buf.at[pl.ds(0, G - 1)], recv.at[GL])
    total = jnp.sum(lg_buf[...], axis=0)
    numer = jnp.sum(jnp.where(lane == 0, total, 0.0), axis=1, keepdims=True)
    denom = jnp.sum(jnp.where(lane == 1, total, 0.0), axis=1, keepdims=True)
    loss_ref[...] = jnp.broadcast_to(numer * S / denom, loss_ref.shape)

    wait(g2_recv.at[pl.ds(0, G - 1)], recv.at[G2])
    f2_buf[s] = jnp.sum(g2_recv[...].astype(F32), axis=0).astype(BF)
    z_bcast(f2_buf, F2)
    wait(g1_recv.at[pl.ds(0, C - 1)], recv.at[G1])
    f1_buf[s] = jnp.sum(g1_recv[...].astype(F32), axis=0).astype(BF)
    z_bcast(f1_buf, F1)

    wait(a_buf.at[pl.ds(0, C - 1), 0], send.at[A])
    wait(a2_buf.at[pl.ds(0, C - 1), 0], send.at[A2])
    wait(a2_buf.at[:, 0], send.at[AS2])
    wait(b_buf.at[pl.ds(0, C - 1), 0], send.at[B])
    wait(a_buf.at[:, 0], send.at[AS])
    wait(b_buf.at[:, 0], send.at[BS])
    wait(pe_buf.at[pl.ds(0, C - 1)], send.at[PE])
    wait(rs_recv[1].at[pl.ds(0, C - 1)], send.at[RS + 1])
    for e in range(2):
        wait(za_buf[e].at[pl.ds(0, S - 1)], send.at[ZA + e])
    for buf, i in ((qr_buf, QKV), (at_recv, ATT), (zl_buf, ZL)):
        wait(buf.at[pl.ds(0, S - 1)], send.at[i])
    wait(h1_buf.at[pl.ds(0, S - 1)], send.at[H1])
    wait(h2_buf.at[0], send.at[H2])
    wait(sl2_buf.at[0], send.at[SL2])
    wait(nx_buf.at[pl.ds(0, 3)], send.at[NX])
    wait(neg_buf.at[0], send.at[NG])
    for i in (UP, US, UT):
        wait(u_buf.at[0], send.at[i])
    wait(dn_buf.at[pl.ds(0, 3)], send.at[DN])
    wait(uds_recv, send.at[UDS])
    wait(udp_recv, send.at[UDP])
    wait(gp1_recv, send.at[GP1])
    wait(lg_buf.at[pl.ds(0, G - 1)], send.at[GL])
    wait(g1_recv.at[pl.ds(0, C - 1)], send.at[G1])
    wait(g2_recv.at[pl.ds(0, G - 1)], send.at[G2])
    wait(w2r_buf.at[0], send.at[W2])

    wait(f2_buf.at[pl.ds(0, S - 1)], recv.at[F2])
    for t in range(S):
        gf_ref[:, 128 * t : 128 * (t + 1)] = f2_buf[t].astype(F32)
    wait(f1_buf.at[pl.ds(0, S - 1)], recv.at[F1])
    for t in range(S):
        gm_ref[:, 128 * t : 128 * (t + 1)] = f1_buf[t, :rows].astype(F32)
        gl_ref[half * (t // 4) : half * (t // 4 + 1), 128 * (t % 4) : 128 * (t % 4 + 1)] = f1_buf[t, rows:].astype(F32)
    wait(f1_buf.at[pl.ds(0, S - 1)], send.at[F1])
    wait(f2_buf.at[pl.ds(0, S - 1)], send.at[F2])


def tail(*refs):
    ins, outs, sem = refs[:6], refs[6:12], refs[12]
    for i in (0, 2, 3, 4, 5):
        pltpu.make_async_copy(ins[i], outs[i], sem.at[i]).start()
    outs[1][0, 0] = jnp.max(ins[1][...])
    for i in (0, 2, 3, 4, 5):
        pltpu.make_async_copy(ins[i], outs[i], sem.at[i]).wait()


def local(history, lengths, next_items, negatives, input_weight, output_weight, pool_features,
          tower_first, tower_middle, tower_last, S, G):
    events = history[0]
    tok = events.shape[0]
    C = G // 2
    R = pool_features.shape[0]
    RH = R // 2
    rows = tower_first.shape[0]
    V = pltpu.VMEM
    vmem = pl.BlockSpec(memory_space=pltpu.VMEM)
    hbm = pl.BlockSpec(memory_space=pltpu.HBM)
    scratch = [
        pltpu.SemaphoreType.DMA((N_SEM,)),
        pltpu.SemaphoreType.DMA((N_SEM,)),
        pltpu.SemaphoreType.DMA((N_HERE,)),
        V((tok, 512), BF),
        V((4, 1, tok), jnp.int32),
        V((2, 1, negatives.shape[1] + 128), jnp.int32),
        V(input_weight.shape, BF),
        V(output_weight.shape, BF),
        V(pool_features.shape, BF),
        V((C, 2, rows, 128), BF),
        V((C, 2, 4, rows, 128), BF),
        V((C, 2, rows, 512), BF),
        V((2, 128 // (2 * rows), 2, 4, rows, 128), BF),
        V((S, tok + tok // 2, 128), BF),
        V((S, tok + tok // 2, 128), BF),
        V((tok, 512), BF),
        V((S * tok, DH), BF),
        V((S * tok, DH), BF),
        V((S * tok, DH), BF),
        V((S, tok // 2, 128), BF),
        V((S, tok // 2, 128), BF),
        V((S, R, 128), BF),
        V((2, 4, R, 128), BF),
        V((2, 4, R, 128), BF),
        V((R, 128), F32),
        V((R, 512), F32),
        V((R, 128), F32),
        V((C, RH, 512), BF),
        V((2, C * RH, 2 * tok), F32),
        V((2, C * RH, 2 * tok), BF),
        V((4, tok, 512), BF),
        V((4, 2, 1, 4 * tok), F32),
        V((2, 1, 2 * tok), F32),
        V((2, 2, tok, 512), F32),
        V((2, tok, 512), BF),
        V((2, tok, 512), BF),
        V((tok, 512), BF),
        V((tok, 512), BF),
        V((S, 8, 128), F32),
        V((G, 8, 128), F32),
        V((R, 512), BF),
        V((R, 1024), BF),
        V((C, 2, 2, rows // 2, 128), BF),
        V((C, 2, rows + rows // 2, 128), BF),
        V((C, rows + rows // 2, 128), BF),
        V((C, rows + rows // 2, 128), BF),
        V((C, rows + rows // 2, 128), BF),
        V((G, rows, 128), BF),
        V((G, rows, 128), BF),
        V((S, rows + rows // 2, 128), BF),
        V((S, rows, 128), BF),
        V((2, C * RH, 128), F32),
        V((tok, 512), F32),
        V((tok, 128), F32),
    ]
    for lead in (C, C, S):
        scratch += [V((lead, RH, n), BF) for _, n in PARTS]
    shapes = [
        jax.ShapeDtypeStruct((tok, 512), BF),
        jax.ShapeDtypeStruct((8, 128), F32),
        jax.ShapeDtypeStruct((tok, 512), F32),
        jax.ShapeDtypeStruct((rows, 1024), F32),
        jax.ShapeDtypeStruct((rows, 1024), F32),
        jax.ShapeDtypeStruct((rows, 512), F32),
    ]
    results = pl.pallas_call(
        functools.partial(kernel, S, G),
        out_shape=[pltpu.VMEM(x.shape, x.dtype) for x in shapes],
        in_specs=[pl.BlockSpec(memory_space=pltpu.SMEM)] + [hbm] * 9,
        out_specs=[vmem] * 6,
        scratch_shapes=scratch,
        compiler_params=pltpu.CompilerParams(
            collective_id=0, has_side_effects=True, vmem_limit_bytes=56 * 1024 * 1024),
    )(lengths, events, next_items, negatives, input_weight, output_weight, pool_features,
      tower_first, tower_middle, tower_last)
    lo, loss, ug, gf, gm, gl = pl.pallas_call(
        tail,
        out_shape=shapes[:1] + [jax.ShapeDtypeStruct((1, 1), F32)] + shapes[2:],
        in_specs=[vmem] * 6,
        out_specs=[hbm, pl.BlockSpec(memory_space=pltpu.SMEM)] + [hbm] * 4,
        scratch_shapes=[pltpu.SemaphoreType.DMA((6,))],
        compiler_params=pltpu.CompilerParams(vmem_limit_bytes=1024 * 1024),
    )(*results)
    return lo[None], loss.reshape(()), ug[None], gf, gm, gl


def solution(mesh):
    placed = (
        P("grp", "seq", None), P("grp"), P("grp", "seq"), P("grp", None), P(), P(),
        P("grp", None), P("grp", None), P("grp", None), P("grp", None),
    )
    return jax.shard_map(
        functools.partial(local, S=mesh.shape["seq"], G=mesh.shape["grp"]),
        mesh=mesh,
        in_specs=placed,
        out_specs=(
            P("grp", "seq", None), P(), P("grp", "seq", None),
            P("grp", None), P("grp", None), P("grp", None),
        ),
        check_vma=False,
    )
```

```python
import functools

import jax
import jax.numpy as jnp
from jax import lax
from jax.experimental import pallas as pl
from jax.experimental.pallas import tpu as pltpu
from jax.sharding import PartitionSpec as P

DH = 64
EPS_NORM = 1e-05
EPS_UNIT = 1e-06
TEMP = 20.0

MESH = pl.DeviceIdType.MESH
BF = jnp.bfloat16
F32 = jnp.float32

(A, A2, B, AS, AS2, BS, QKV, ATT, H1, H2, SL2, NX, NG, UP, US, UT, DN, UDS, UDP, ZL, GL, GP1, G1, G2, F1, F2,
 W2, PE) = range(28)
RS, ZA = 28, 30
N_SEM = 32

PARTS = ((0, 256), (256, 256))

(I_W3, I_H, I_WIN, I_WOUT, I_X, I_NEG, I_NXT, I_W1) = range(8)
I_W2 = 8
N_HERE = 12


def silu(x):
    half = 0.5 * x
    return half * (1.0 + jnp.tanh(half))


def silu_slope(z):
    sigma = 0.5 * (1.0 + jnp.tanh(0.5 * z))
    return sigma * (1.0 + z * (1.0 - sigma))


def layer_norm(values):
    center = values - jnp.mean(values, axis=-1, keepdims=True)
    spread = jnp.mean(center * center, axis=-1, keepdims=True)
    return center * lax.rsqrt(spread + EPS_NORM)


def dot(a, b):
    return jnp.dot(a, b, preferred_element_type=F32)


def dot_t(a, b):
    return lax.dot_general(a, b, (((1,), (1,)), ((), ())), preferred_element_type=F32)


def t_dot(a, b):
    return lax.dot_general(a, b, (((0,), (0,)), ((), ())), preferred_element_type=F32)


def wait(ref, sem):
    pltpu.make_async_copy(ref, ref, sem).wait()


def kernel(
    S, G,
    len_ref, hist, nxt, neg, win, wout, xf, w1, w2, w3,
    lo_ref, loss_ref, ug_ref, gf_ref, gm_ref, gl_ref,
    send, recv, here,
    hist_v, nx_buf, neg_buf, win_v, wout_v, xf_v,
    a_buf, a2_buf, b_buf, w2r_buf, qs_buf, qr_buf, gate, k_scr, q_scr, v_scr, at_send, at_recv,
    h1_buf, h2_buf, sl2_buf, pre1, ui, inv, pe_buf, em, st, u_buf,
    dn_buf, nll, ud, uds_send, uds_recv, udp_send, udp_recv, zl_buf, lg_buf, rg, sg_scr,
    gl_scr, gp1, gp1_recv, g1_send, g1_recv, g2_send, g2_recv, f1_buf, f2_buf, cnt, uu, uinv, *parts,
):
    C = G // 2
    s = lax.axis_index("seq")
    g = lax.axis_index("grp")
    p = g // 2
    c = g % 2
    par = s % 2
    tok = hist_v.shape[0]
    me = 2 * c + par
    rows = b_buf.shape[2]
    NB = a2_buf.shape[2]
    half = rows // 2
    NEG = neg.shape[1]
    R = xf_v.shape[0]
    RH = R // 2
    length = len_ref[0]
    pair = (s + 1 - 2 * par, g)
    sib = (s, 2 * p + 1 - c)
    diag = (s + 1 - 2 * par, 2 * p + 1 - c)
    cols = pl.ds(pl.multiple_of(s * 128, 128), 128)

    def copy(src, dst, i, dev):
        return pltpu.make_async_remote_copy(
            src_ref=src, dst_ref=dst, send_sem=send.at[i], recv_sem=recv.at[i],
            device_id=dev, device_id_type=MESH)

    def fetch(src, dst, i):
        pltpu.make_async_copy(src, dst, here.at[i]).start()

    def z_bcast(buf, i):
        def step(k, _):
            copy(buf.at[s], buf.at[s], i, (lax.rem(s + k, S), g)).start()
            return 0
        lax.fori_loop(1, S, step, 0)

    def chips(src, dst, i):
        def step(k, _):
            copy(src, dst, i, (s, 2 * lax.rem(p + k, C) + c)).start()
            return 0
        lax.fori_loop(1, C, step, 0)

    def chip_scatter(src, dst, i):
        def step(k, _):
            t = lax.rem(p + k, C)
            copy(src.at[t], dst.at[p], i, (s, 2 * t + c)).start()
            return 0
        lax.fori_loop(1, C, step, 0)
        dst[p] = src[p]

    rs_send, rs_recv, za_buf = parts[0:2], parts[2:4], parts[4:6]

    def grp_scatter(src, dst, i):
        def step(k, _):
            t = lax.rem(g + k, G)
            copy(src.at[t], dst.at[g], i, (s, t)).start()
            return 0
        lax.fori_loop(1, G, step, 0)
        dst[g] = src[g]

    def quad(buf, i):
        for dev in (sib, pair, diag):
            copy(buf.at[me], buf.at[me], i, dev).start()

    fetch(w1.at[:, cols], a_buf.at[p, c], I_W1)
    barrier = pltpu.get_barrier_semaphore()

    def greet_grp(k, _):
        pl.semaphore_signal(barrier, inc=1, device_id=(s, lax.rem(g + k, G)), device_id_type=MESH)
        return 0

    def greet_seq(k, _):
        pl.semaphore_signal(barrier, inc=1, device_id=(lax.rem(s + k, S), g), device_id_type=MESH)
        return 0

    lax.fori_loop(1, G, greet_grp, 0)
    lax.fori_loop(1, S, greet_seq, 0)
    pl.semaphore_signal(barrier, inc=1, device_id=diag, device_id_type=MESH)

    for j in range(NB):
        block = pl.ds(pl.multiple_of((2 * j + par) * 128, 128), 128)
        fetch(w2.at[:, block], a2_buf.at[p, c, j], I_W2 + j)
    fetch(hist, hist_v, I_H)
    fetch(win, win_v, I_WIN)
    fetch(nxt, nx_buf.at[me], I_NXT)
    fetch(w3, b_buf.at[p, c], I_W3)
    fetch(xf, xf_v, I_X)
    fetch(neg, neg_buf.at[c, :, pl.ds(0, NEG)], I_NEG)
    fetch(wout, wout_v, I_WOUT)
    neg_buf[c, :, NEG:] = jnp.full((1, 128), length, jnp.int32)
    wait(a_buf.at[p, c], here.at[I_W1])
    pl.semaphore_wait(barrier, (G - 1) + (S - 1) + 1)
    chips(a_buf.at[p, c], a_buf.at[p, c], A)

    wait(hist_v, here.at[I_H])
    normed = layer_norm(hist_v[...].astype(F32)).astype(BF)
    wait(win_v, here.at[I_WIN])
    for j in range(4):
        x = silu(dot(normed, win_v[:, 512 + 384 * j : 512 + 384 * (j + 1)])).astype(BF)
        for e in (0, 1):
            o = 192 * e
            qs_buf[2 * j + e, :tok] = x[:, o : o + 128]
            v = x[:, o + 128 : o + 192]
            qs_buf[2 * j + e, tok:] = jnp.concatenate([v[: tok // 2], v[tok // 2 :]], axis=1)

    def qkv_step(k, _):
        t = lax.rem(s + k, S)
        copy(qs_buf.at[t], qr_buf.at[s], QKV, (t, g)).start()
        return 0

    lax.fori_loop(1, S, qkv_step, 0)
    qr_buf[s] = qs_buf[s]
    for j in range(NB):
        wait(a2_buf.at[p, c, j], here.at[I_W2 + j])
    chips(a2_buf.at[p, c], a2_buf.at[p, c], A2)
    wait(nx_buf.at[me], here.at[I_NXT])
    quad(nx_buf, NX)
    wait(neg_buf.at[c, :, pl.ds(0, NEG)], here.at[I_NEG])
    copy(neg_buf.at[c], neg_buf.at[c], NG, sib).start()
    gate[...] = silu(dot(normed, win_v[:, :512])).astype(BF)

    wait(xf_v, here.at[I_X])
    wait(a_buf.at[pl.ds(0, C - 1), 0], recv.at[A])
    copy(a_buf.at[:, c], a_buf.at[:, c], AS, sib).start()
    wait(b_buf.at[p, c], here.at[I_W3])
    chips(b_buf.at[p, c], b_buf.at[p, c], B)
    wait(a_buf.at[:, 0], recv.at[AS])
    z1 = dot(xf_v[...], a_buf[...].reshape(G * rows, 128))
    pre1[...] = z1
    h1_buf[s] = silu(z1).astype(BF)
    z_bcast(h1_buf, H1)

    def local_row(ids):
        return jnp.where((ids // RH) % 4 == me, (ids // (2 * R)) * RH + ids % RH, -1)

    wait(neg_buf.at[0], recv.at[NG])
    n_rows = C * RH
    for e in (0, 1):
        ids = local_row(neg_buf[e, :, :NEG])
        hot = (lax.broadcasted_iota(jnp.int32, (n_rows, NEG), 0) == ids).astype(F32).astype(BF)
        cnt[e] = dot(hot, jnp.ones((NEG, 128), BF))
    def whole(buf):
        return jnp.concatenate([buf[j % 2, j // 2] for j in range(2 * NB)], axis=1)

    wait(a2_buf.at[pl.ds(0, C - 1), 0], recv.at[A2])
    copy(a2_buf.at[:, c], a2_buf.at[:, c], AS2, sib).start()
    wait(qr_buf.at[pl.ds(0, S - 1)], recv.at[QKV])
    for j in range(S):
        x = qr_buf[j]
        q_scr[tok * j : tok * (j + 1)] = x[:tok, :DH]
        k_scr[tok * j : tok * (j + 1)] = x[:tok, DH:]
        v_scr[tok * j : tok * (j + 1)] = jnp.concatenate([x[tok:, :DH], x[tok:, DH:]], axis=0)

    inv_len = 1.0 / jnp.full((1, 1), length, jnp.int32).astype(F32)
    W = 2 * tok

    def attend(b):
        q = q_scr[W * b : W * (b + 1)]
        acc = jnp.zeros((W, DH), F32)
        for kb in range(b + 1):
            hs = dot_t(q, k_scr[W * kb : W * (kb + 1)]) * (0.5 * DH ** (-0.5))
            w = (hs * inv_len) * (1.0 + jnp.tanh(hs))
            if kb == b:
                r = lax.broadcasted_iota(jnp.int32, (W, W), 0)
                cc = lax.broadcasted_iota(jnp.int32, (W, W), 1)
                w = jnp.where(cc <= r, w, 0.0)
            acc = acc + dot(w.astype(BF), v_scr[W * kb : W * (kb + 1)])
        pos = W * b + lax.broadcasted_iota(jnp.int32, (W, 1), 0)
        acc = jnp.where(pos < length, acc, 0.0).astype(BF)
        for i in (0, 1):
            o = acc[tok * i : tok * (i + 1)]
            at_send[2 * b + i] = jnp.concatenate([o[: tok // 2], o[tok // 2 :]], axis=1)

    for b in reversed(range(S // 2)):
        attend(b)
    at_recv[s] = at_send[s]

    def at_step(k, _):
        t = lax.rem(s + k, S)
        copy(at_send.at[t], at_recv.at[s], ATT, (t, g)).start()
        return 0

    lax.fori_loop(1, S, at_step, 0)
    wait(h1_buf.at[pl.ds(0, S - 1)], recv.at[H1])
    wait(a2_buf.at[:, 0], recv.at[AS2])
    h1 = jnp.concatenate([h1_buf[j] for j in range(S)], axis=1)
    for j in range(NB):
        z2 = dot(h1, a2_buf[:, :, j].reshape(G * rows, 128))
        h2_buf[par, j] = silu(z2).astype(BF)
        sl2_buf[par, j] = silu_slope(z2).astype(BF)
    copy(h2_buf.at[par], h2_buf.at[par], H2, pair).start()

    wait(b_buf.at[pl.ds(0, C - 1), 0], recv.at[B])
    copy(b_buf.at[:, c], b_buf.at[:, c], BS, sib).start()

    wait(h2_buf.at[0], recv.at[H2])
    wait(b_buf.at[:, 0], recv.at[BS])
    h2 = whole(h2_buf)
    raw = dot(h2, b_buf[...].reshape(G * rows, 512))
    item_inverse = lax.rsqrt(jnp.sum(raw * raw, axis=-1, keepdims=True) + EPS_UNIT)
    unit_item = raw * item_inverse
    ui[...] = unit_item
    inv[...] = jnp.broadcast_to(item_inverse, inv.shape)
    pe_buf[p] = ui[pl.ds(pl.multiple_of(par * RH, RH), RH)].astype(BF)
    chips(pe_buf.at[p], pe_buf.at[p], PE)

    wait(wout_v, here.at[I_WOUT])
    wait(at_recv.at[pl.ds(0, S - 1)], recv.at[ATT])
    tops, bottoms = [], []
    for h in range(S):
        x = at_recv[h]
        tops.append(x[:, :DH])
        bottoms.append(x[:, DH:])
    merged = jnp.concatenate(
        [jnp.concatenate(tops, axis=1), jnp.concatenate(bottoms, axis=1)], axis=0).astype(F32)
    branch = (layer_norm(merged) * gate[...].astype(F32)).astype(BF)
    layer_out = (hist_v[...].astype(F32) + dot(branch, wout_v[...])).astype(BF)
    lo_ref[...] = layer_out
    outward = layer_out.astype(F32)
    user_inverse = lax.rsqrt(jnp.sum(outward * outward, axis=-1, keepdims=True) + EPS_UNIT)
    unit_user = outward * user_inverse
    u_buf[me] = unit_user.astype(BF)
    copy(u_buf.at[me], u_buf.at[me], UP, pair).start()
    copy(u_buf.at[me], u_buf.at[me], US, sib).start()
    uu[...] = unit_user
    uinv[...] = jnp.broadcast_to(user_inverse, (tok, 128))

    wait(nx_buf.at[pl.ds(0, 3)], recv.at[NX])
    pair_pos = lax.broadcasted_iota(jnp.int32, (1, W), 1)
    positions = (s // 2) * W + pair_pos

    def items_of(u):
        return local_row(jnp.concatenate([nx_buf[2 * u], nx_buf[2 * u + 1]], axis=1))

    def valid_of(u):
        lens = neg_buf[u, :, NEG:]
        return (positions < jnp.concatenate([lens, lens], axis=1) - 1).astype(F32)

    wait(u_buf.at[0], recv.at[UP])
    other = 2 * c + 1 - par
    copy(u_buf.at[other], u_buf.at[other], UT, sib).start()
    wait(pe_buf.at[pl.ds(0, C - 1)], recv.at[PE])

    Q = 4
    CQ = C // Q
    width = n_rows // Q
    row_id = lax.broadcasted_iota(jnp.int32, (width, W), 0)

    def logits_of(u):
        users = u_buf[pl.ds(2 * u, 2)].reshape(W, 512)
        items = items_of(u)
        den = jnp.zeros((1, W), F32)
        positive = jnp.zeros((1, W), F32)
        for q in range(Q):
            logit = TEMP * dot_t(pe_buf[CQ * q : CQ * (q + 1)].reshape(width, 512), users)
            own = row_id + width * q == items
            times = cnt[u, width * q : width * (q + 1)]
            e = jnp.where(own, 0.0, jnp.exp(logit) * jnp.concatenate([times, times], axis=1))
            em[u, width * q : width * (q + 1)] = e
            den = den + jnp.sum(e, axis=0, keepdims=True)
            positive = positive + jnp.sum(jnp.where(own, logit, 0.0), axis=0, keepdims=True)
        dn_buf[me, u] = jnp.concatenate([den, positive], axis=1)

    logits_of(c)
    wait(u_buf.at[0], recv.at[US])
    wait(u_buf.at[0], recv.at[UT])
    logits_of(1 - c)
    quad(dn_buf, DN)
    wait(dn_buf.at[pl.ds(0, 3)], recv.at[DN])
    for u in (0, 1):
        sums = dn_buf[0, u] + dn_buf[1, u] + dn_buf[2, u] + dn_buf[3, u]
        positive = sums[:, W:]
        positive_exp = jnp.exp(positive)
        den = sums[:, :W] + positive_exp
        valid = valid_of(u)
        items = items_of(u)
        slope = valid * (positive_exp / den - 1.0)
        scale = valid / den
        for q in range(Q):
            block = slice(width * q, width * (q + 1))
            st[u, block] = jnp.where(row_id + width * q == items, slope, scale * em[u, block]).astype(BF)
        nll[u] = valid * (jnp.log(den) - positive)

    def pool_part(e):
        lo, n = PARTS[e]
        part = dot(st[0], u_buf[0:2, :, lo : lo + n].reshape(W, n))
        part = part + dot(st[1], u_buf[2:4, :, lo : lo + n].reshape(W, n))
        rs_send[e][...] = (TEMP * part).astype(BF).reshape(C, RH, n)

    pool_part(0)
    chip_scatter(rs_send[0], rs_recv[0], RS)

    per_block = 128 // (2 * rows)
    copy(a2_buf.at[pl.ds(per_block * (s + 1 - 2 * par), per_block)], w2r_buf.at[par], W2, pair).start()
    w2r_buf[par] = a2_buf[pl.ds(per_block * s, per_block)]
    copy(sl2_buf.at[par], sl2_buf.at[par], SL2, pair).start()

    mine = pair_pos // tok == par
    loss_sum = jnp.sum(jnp.where(mine, nll[c], 0.0))
    lane = lax.broadcasted_iota(jnp.int32, (8, 128), 1)
    count = jnp.full((8, 128), length - 1, jnp.int32).astype(F32)
    zl_buf[s] = jnp.where(lane == 0, loss_sum, jnp.where(lane == 1, count, 0.0))
    z_bcast(zl_buf, ZL)

    rows_here = pe_buf[...].reshape(n_rows, 512)
    for u in (0, 1):
        ud[u] = t_dot(st[u], rows_here).reshape(2, tok, 512)
    uds_send[...] = ud[1 - c].astype(BF)
    copy(uds_send, uds_recv, UDS, sib).start()

    pool_part(1)
    wait(rs_recv[0].at[pl.ds(0, C - 1)], send.at[RS])
    chip_scatter(rs_send[1], rs_recv[1], RS + 1)

    def plane_sum(e):
        wait(rs_recv[e].at[pl.ds(0, C - 1)], recv.at[RS + e])
        za_buf[e][s] = jnp.sum(rs_recv[e][...].astype(F32), axis=0).astype(BF)
        z_bcast(za_buf[e], ZA + e)

    plane_sum(0)
    plane_sum(1)
    wait(zl_buf.at[pl.ds(0, S - 1)], recv.at[ZL])
    lg_buf[g] = jnp.sum(zl_buf[...], axis=0)

    def lg_step(k, _):
        copy(lg_buf.at[g], lg_buf.at[g], GL, (s, lax.rem(g + k, G))).start()
        return 0

    lax.fori_loop(1, G, lg_step, 0)
    wait(w2r_buf.at[0], recv.at[W2])
    w2_rows = jnp.concatenate([w2r_buf[j % 2, :, :, j // 2].reshape(128, 128) for j in range(2 * NB)], axis=1)
    wait(sl2_buf.at[0], recv.at[SL2])
    h1 = jnp.concatenate([h1_buf[j] for j in range(S)], axis=1)
    h2 = whole(h2_buf)
    slope2 = whole(sl2_buf).astype(F32)
    slope1 = silu_slope(pre1[...])

    for e in range(2):
        wait(za_buf[e].at[pl.ds(0, S - 1)], recv.at[ZA + e])
    chunks = []
    for e in range(2):
        sums = []
        for o in (0, 1):
            part = za_buf[e][o].astype(F32)
            for t in range(o + 2, S, 2):
                part = part + za_buf[e][t].astype(F32)
            sums.append(part)
        chunks.append(jnp.concatenate(sums, axis=0))
    own_grad = jnp.concatenate(chunks, axis=1)
    uin = ui[...]
    raw_grad = (inv[:, :1] * (own_grad - uin * jnp.sum(uin * own_grad, axis=-1, keepdims=True))).astype(BF)
    rg[...] = raw_grad
    sg = (dot_t(raw_grad, b_buf[...].reshape(G * rows, 512)) * slope2).astype(BF)
    sg_scr[...] = sg
    fg = (dot_t(sg, w2_rows) * slope1).astype(BF)
    g2_send[...] = t_dot(xf_v[...], fg).astype(BF).reshape(G, rows, 128)
    grp_scatter(g2_send, g2_recv, G2)
    q_cols = pl.ds(pl.multiple_of(lax.rem(s, 4) * 128, 128), 128)
    gl_scr[...] = t_dot(h2, rg[:, q_cols]).astype(BF).reshape(C, 2, 2, half, 128)
    gp1[:, :, :rows] = t_dot(h1, sg_scr[:, cols]).astype(BF).reshape(C, 2, rows, 128)
    gp1[:, :, rows:] = gl_scr[:, :, s // 4]
    copy(gp1.at[:, 1 - c], gp1_recv, GP1, sib).start()
    wait(uds_recv, recv.at[UDS])
    udp_send[...] = (ud[c, 1 - par] + uds_recv[1 - par].astype(F32)).astype(BF)
    copy(udp_send, udp_recv, UDP, pair).start()
    wait(gp1_recv, recv.at[GP1])
    g1_send[...] = (gp1[:, c].astype(F32) + gp1_recv[...].astype(F32)).astype(BF)
    chip_scatter(g1_send, g1_recv, G1)

    wait(lg_buf.at[pl.ds(0, G - 1)], recv.at[GL])
    total = jnp.sum(lg_buf[...], axis=0)
    numer = jnp.sum(jnp.where(lane == 0, total, 0.0), axis=1, keepdims=True)
    denom = jnp.sum(jnp.where(lane == 1, total, 0.0), axis=1, keepdims=True)
    loss_ref[...] = jnp.broadcast_to(numer * S / denom, loss_ref.shape)

    wait(g2_recv.at[pl.ds(0, G - 1)], recv.at[G2])
    f2_buf[s] = jnp.sum(g2_recv[...].astype(F32), axis=0).astype(BF)
    z_bcast(f2_buf, F2)
    wait(g1_recv.at[pl.ds(0, C - 1)], recv.at[G1])
    f1_buf[s] = jnp.sum(g1_recv[...].astype(F32), axis=0).astype(BF)
    z_bcast(f1_buf, F1)

    wait(udp_recv, recv.at[UDP])
    user_dir = TEMP * (ud[c, par] + uds_recv[par].astype(F32) + udp_recv[...].astype(F32))
    uun = uu[...]
    ug_ref[...] = uinv[:, :1] * (user_dir - uun * jnp.sum(uun * user_dir, axis=-1, keepdims=True))
    wait(a_buf.at[pl.ds(0, C - 1), 0], send.at[A])
    wait(a2_buf.at[pl.ds(0, C - 1), 0], send.at[A2])
    wait(a2_buf.at[:, 0], send.at[AS2])
    wait(b_buf.at[pl.ds(0, C - 1), 0], send.at[B])
    wait(a_buf.at[:, 0], send.at[AS])
    wait(b_buf.at[:, 0], send.at[BS])
    wait(pe_buf.at[pl.ds(0, C - 1)], send.at[PE])
    wait(rs_recv[1].at[pl.ds(0, C - 1)], send.at[RS + 1])
    for e in range(2):
        wait(za_buf[e].at[pl.ds(0, S - 1)], send.at[ZA + e])
    for buf, i in ((qr_buf, QKV), (at_recv, ATT), (zl_buf, ZL)):
        wait(buf.at[pl.ds(0, S - 1)], send.at[i])
    wait(h1_buf.at[pl.ds(0, S - 1)], send.at[H1])
    wait(h2_buf.at[0], send.at[H2])
    wait(sl2_buf.at[0], send.at[SL2])
    wait(nx_buf.at[pl.ds(0, 3)], send.at[NX])
    wait(neg_buf.at[0], send.at[NG])
    for i in (UP, US, UT):
        wait(u_buf.at[0], send.at[i])
    wait(dn_buf.at[pl.ds(0, 3)], send.at[DN])
    wait(uds_recv, send.at[UDS])
    wait(udp_recv, send.at[UDP])
    wait(gp1_recv, send.at[GP1])
    wait(lg_buf.at[pl.ds(0, G - 1)], send.at[GL])
    wait(g1_recv.at[pl.ds(0, C - 1)], send.at[G1])
    wait(g2_recv.at[pl.ds(0, G - 1)], send.at[G2])
    wait(w2r_buf.at[0], send.at[W2])

    wait(f2_buf.at[pl.ds(0, S - 1)], recv.at[F2])
    for t in range(S):
        gf_ref[:, 128 * t : 128 * (t + 1)] = f2_buf[t].astype(F32)
    wait(f1_buf.at[pl.ds(0, S - 1)], recv.at[F1])
    for t in range(S):
        gm_ref[:, 128 * t : 128 * (t + 1)] = f1_buf[t, :rows].astype(F32)
        gl_ref[half * (t // 4) : half * (t // 4 + 1), 128 * (t % 4) : 128 * (t % 4 + 1)] = f1_buf[t, rows:].astype(F32)
    wait(f1_buf.at[pl.ds(0, S - 1)], send.at[F1])
    wait(f2_buf.at[pl.ds(0, S - 1)], send.at[F2])


def tail(*refs):
    ins, outs, sem = refs[:6], refs[6:12], refs[12]
    for i in (0, 2, 3, 4, 5):
        pltpu.make_async_copy(ins[i], outs[i], sem.at[i]).start()
    outs[1][0, 0] = jnp.max(ins[1][...])
    for i in (0, 2, 3, 4, 5):
        pltpu.make_async_copy(ins[i], outs[i], sem.at[i]).wait()


def local(history, lengths, next_items, negatives, input_weight, output_weight, pool_features,
          tower_first, tower_middle, tower_last, S, G):
    events = history[0]
    tok = events.shape[0]
    C = G // 2
    R = pool_features.shape[0]
    RH = R // 2
    rows = tower_first.shape[0]
    V = pltpu.VMEM
    vmem = pl.BlockSpec(memory_space=pltpu.VMEM)
    hbm = pl.BlockSpec(memory_space=pltpu.HBM)
    scratch = [
        pltpu.SemaphoreType.DMA((N_SEM,)),
        pltpu.SemaphoreType.DMA((N_SEM,)),
        pltpu.SemaphoreType.DMA((N_HERE,)),
        V((tok, 512), BF),
        V((4, 1, tok), jnp.int32),
        V((2, 1, negatives.shape[1] + 128), jnp.int32),
        V(input_weight.shape, BF),
        V(output_weight.shape, BF),
        V(pool_features.shape, BF),
        V((C, 2, rows, 128), BF),
        V((C, 2, 4, rows, 128), BF),
        V((C, 2, rows, 512), BF),
        V((2, 128 // (2 * rows), 2, 4, rows, 128), BF),
        V((S, tok + tok // 2, 128), BF),
        V((S, tok + tok // 2, 128), BF),
        V((tok, 512), BF),
        V((S * tok, DH), BF),
        V((S * tok, DH), BF),
        V((S * tok, DH), BF),
        V((S, tok // 2, 128), BF),
        V((S, tok // 2, 128), BF),
        V((S, R, 128), BF),
        V((2, 4, R, 128), BF),
        V((2, 4, R, 128), BF),
        V((R, 128), F32),
        V((R, 512), F32),
        V((R, 128), F32),
        V((C, RH, 512), BF),
        V((2, C * RH, 2 * tok), F32),
        V((2, C * RH, 2 * tok), BF),
        V((4, tok, 512), BF),
        V((4, 2, 1, 4 * tok), F32),
        V((2, 1, 2 * tok), F32),
        V((2, 2, tok, 512), F32),
        V((2, tok, 512), BF),
        V((2, tok, 512), BF),
        V((tok, 512), BF),
        V((tok, 512), BF),
        V((S, 8, 128), F32),
        V((G, 8, 128), F32),
        V((R, 512), BF),
        V((R, 1024), BF),
        V((C, 2, 2, rows // 2, 128), BF),
        V((C, 2, rows + rows // 2, 128), BF),
        V((C, rows + rows // 2, 128), BF),
        V((C, rows + rows // 2, 128), BF),
        V((C, rows + rows // 2, 128), BF),
        V((G, rows, 128), BF),
        V((G, rows, 128), BF),
        V((S, rows + rows // 2, 128), BF),
        V((S, rows, 128), BF),
        V((2, C * RH, 128), F32),
        V((tok, 512), F32),
        V((tok, 128), F32),
    ]
    for lead in (C, C, S):
        scratch += [V((lead, RH, n), BF) for _, n in PARTS]
    shapes = [
        jax.ShapeDtypeStruct((tok, 512), BF),
        jax.ShapeDtypeStruct((8, 128), F32),
        jax.ShapeDtypeStruct((tok, 512), F32),
        jax.ShapeDtypeStruct((rows, 1024), F32),
        jax.ShapeDtypeStruct((rows, 1024), F32),
        jax.ShapeDtypeStruct((rows, 512), F32),
    ]
    results = pl.pallas_call(
        functools.partial(kernel, S, G),
        out_shape=[pltpu.VMEM(x.shape, x.dtype) for x in shapes],
        in_specs=[pl.BlockSpec(memory_space=pltpu.SMEM)] + [hbm] * 9,
        out_specs=[vmem] * 6,
        scratch_shapes=scratch,
        compiler_params=pltpu.CompilerParams(
            collective_id=0, has_side_effects=True, vmem_limit_bytes=56 * 1024 * 1024),
    )(lengths, events, next_items, negatives, input_weight, output_weight, pool_features,
      tower_first, tower_middle, tower_last)
    lo, loss, ug, gf, gm, gl = pl.pallas_call(
        tail,
        out_shape=shapes[:1] + [jax.ShapeDtypeStruct((1, 1), F32)] + shapes[2:],
        in_specs=[vmem] * 6,
        out_specs=[hbm, pl.BlockSpec(memory_space=pltpu.SMEM)] + [hbm] * 4,
        scratch_shapes=[pltpu.SemaphoreType.DMA((6,))],
        compiler_params=pltpu.CompilerParams(vmem_limit_bytes=1024 * 1024),
    )(*results)
    return lo[None], loss.reshape(()), ug[None], gf, gm, gl


def solution(mesh):
    placed = (
        P("grp", "seq", None), P("grp"), P("grp", "seq"), P("grp", None), P(), P(),
        P("grp", None), P("grp", None), P("grp", None), P("grp", None),
    )
    return jax.shard_map(
        functools.partial(local, S=mesh.shape["seq"], G=mesh.shape["grp"]),
        mesh=mesh,
        in_specs=placed,
        out_specs=(
            P("grp", "seq", None), P(), P("grp", "seq", None),
            P("grp", None), P("grp", None), P("grp", None),
        ),
        check_vma=False,
    )
```

```python
import functools

import jax
import jax.numpy as jnp
from jax import lax
from jax.experimental import pallas as pl
from jax.experimental.pallas import tpu as pltpu
from jax.sharding import PartitionSpec as P

DH = 64
EPS_NORM = 1e-05
EPS_UNIT = 1e-06
TEMP = 20.0

MESH = pl.DeviceIdType.MESH
BF = jnp.bfloat16
F32 = jnp.float32

(A, A2, B, AS, AS2, BS, QKV, ATT, H1, H2, SL2, NX, NG, UP, US, UT, DN, UDS, UDP, ZL, GL, GP1, G1, G2, F1, F2,
 W2, PE) = range(28)
RS, ZA = 28, 30
N_SEM = 32

PARTS = ((0, 256), (256, 256))

(I_W3, I_H, I_WIN, I_WOUT, I_X, I_NEG, I_NXT, I_W1) = range(8)
I_W2 = 8
N_HERE = 12


def silu(x):
    half = 0.5 * x
    return half * (1.0 + jnp.tanh(half))


def silu_slope(z):
    sigma = 0.5 * (1.0 + jnp.tanh(0.5 * z))
    return sigma * (1.0 + z * (1.0 - sigma))


def layer_norm(values):
    center = values - jnp.mean(values, axis=-1, keepdims=True)
    spread = jnp.mean(center * center, axis=-1, keepdims=True)
    return center * lax.rsqrt(spread + EPS_NORM)


def dot(a, b):
    return jnp.dot(a, b, preferred_element_type=F32)


def dot_t(a, b):
    return lax.dot_general(a, b, (((1,), (1,)), ((), ())), preferred_element_type=F32)


def t_dot(a, b):
    return lax.dot_general(a, b, (((0,), (0,)), ((), ())), preferred_element_type=F32)


def wait(ref, sem):
    pltpu.make_async_copy(ref, ref, sem).wait()


def kernel(
    S, G,
    len_ref, hist, nxt, neg, win, wout, xf, w1, w2, w3,
    lo_ref, loss_ref, ug_ref, gf_ref, gm_ref, gl_ref,
    send, recv, here,
    hist_v, nx_buf, neg_buf, win_v, wout_v, xf_v,
    a_buf, a2_buf, b_buf, w2r_buf, qs_buf, qr_buf, gate, k_scr, q_scr, v_scr, at_send, at_recv,
    h1_buf, h2_buf, sl2_buf, pre1, ui, inv, pe_buf, em, st, u_buf,
    dn_buf, nll, ud, uds_send, uds_recv, udp_send, udp_recv, zl_buf, lg_buf, rg, sg_scr,
    gl_scr, gp1, gp1_recv, g1_send, g1_recv, g2_send, g2_recv, f1_buf, f2_buf, cnt, uu, uinv, *parts,
):
    C = G // 2
    s = lax.axis_index("seq")
    g = lax.axis_index("grp")
    p = g // 2
    c = g % 2
    par = s % 2
    tok = hist_v.shape[0]
    me = 2 * c + par
    rows = b_buf.shape[2]
    NB = a2_buf.shape[2]
    half = rows // 2
    NEG = neg.shape[1]
    R = xf_v.shape[0]
    RH = R // 2
    length = len_ref[0]
    pair = (s + 1 - 2 * par, g)
    sib = (s, 2 * p + 1 - c)
    diag = (s + 1 - 2 * par, 2 * p + 1 - c)
    cols = pl.ds(pl.multiple_of(s * 128, 128), 128)

    def copy(src, dst, i, dev):
        return pltpu.make_async_remote_copy(
            src_ref=src, dst_ref=dst, send_sem=send.at[i], recv_sem=recv.at[i],
            device_id=dev, device_id_type=MESH)

    def fetch(src, dst, i):
        pltpu.make_async_copy(src, dst, here.at[i]).start()

    def z_away(i):
        return lax.rem(s + S // 2 + (1 - 2 * (i % 2)) * ((i + 1) // 2), S)

    def z_bcast(buf, i):
        def step(k, _):
            copy(buf.at[s], buf.at[s], i, (z_away(k), g)).start()
            return 0
        lax.fori_loop(0, S - 1, step, 0)

    def chips(src, dst, i):
        def step(k, _):
            copy(src, dst, i, (s, 2 * lax.rem(p + k, C) + c)).start()
            return 0
        lax.fori_loop(1, C, step, 0)

    def chip_scatter(src, dst, i):
        def step(k, _):
            t = lax.rem(p + k, C)
            copy(src.at[t], dst.at[p], i, (s, 2 * t + c)).start()
            return 0
        lax.fori_loop(1, C, step, 0)
        dst[p] = src[p]

    rs_send, rs_recv, za_buf = parts[0:2], parts[2:4], parts[4:6]

    def grp_scatter(src, dst, i):
        def step(k, _):
            t = lax.rem(g + k, G)
            copy(src.at[t], dst.at[g], i, (s, t)).start()
            return 0
        lax.fori_loop(1, G, step, 0)
        dst[g] = src[g]

    def quad(buf, i):
        for dev in (sib, pair, diag):
            copy(buf.at[me], buf.at[me], i, dev).start()

    fetch(w1.at[:, cols], a_buf.at[p, c], I_W1)
    barrier = pltpu.get_barrier_semaphore()

    def greet_grp(k, _):
        pl.semaphore_signal(barrier, inc=1, device_id=(s, lax.rem(g + k, G)), device_id_type=MESH)
        return 0

    def greet_seq(k, _):
        pl.semaphore_signal(barrier, inc=1, device_id=(lax.rem(s + k, S), g), device_id_type=MESH)
        return 0

    lax.fori_loop(1, G, greet_grp, 0)
    lax.fori_loop(1, S, greet_seq, 0)
    pl.semaphore_signal(barrier, inc=1, device_id=diag, device_id_type=MESH)

    for j in range(NB):
        block = pl.ds(pl.multiple_of((2 * j + par) * 128, 128), 128)
        fetch(w2.at[:, block], a2_buf.at[p, c, j], I_W2 + j)
    fetch(hist, hist_v, I_H)
    fetch(win, win_v, I_WIN)
    fetch(nxt, nx_buf.at[me], I_NXT)
    fetch(w3, b_buf.at[p, c], I_W3)
    fetch(xf, xf_v, I_X)
    fetch(neg, neg_buf.at[c, :, pl.ds(0, NEG)], I_NEG)
    fetch(wout, wout_v, I_WOUT)
    neg_buf[c, :, NEG:] = jnp.full((1, 128), length, jnp.int32)
    wait(a_buf.at[p, c], here.at[I_W1])
    pl.semaphore_wait(barrier, (G - 1) + (S - 1) + 1)
    chips(a_buf.at[p, c], a_buf.at[p, c], A)

    wait(hist_v, here.at[I_H])
    normed = layer_norm(hist_v[...].astype(F32)).astype(BF)
    wait(win_v, here.at[I_WIN])
    for j in range(4):
        x = silu(dot(normed, win_v[:, 512 + 384 * j : 512 + 384 * (j + 1)])).astype(BF)
        for e in (0, 1):
            o = 192 * e
            qs_buf[2 * j + e, :tok] = x[:, o : o + 128]
            v = x[:, o + 128 : o + 192]
            qs_buf[2 * j + e, tok:] = jnp.concatenate([v[: tok // 2], v[tok // 2 :]], axis=1)

    def qkv_step(k, _):
        t = z_away(k)
        copy(qs_buf.at[t], qr_buf.at[s], QKV, (t, g)).start()
        return 0

    lax.fori_loop(0, S - 1, qkv_step, 0)
    qr_buf[s] = qs_buf[s]
    for j in range(NB):
        wait(a2_buf.at[p, c, j], here.at[I_W2 + j])
    chips(a2_buf.at[p, c], a2_buf.at[p, c], A2)
    wait(nx_buf.at[me], here.at[I_NXT])
    quad(nx_buf, NX)
    wait(neg_buf.at[c, :, pl.ds(0, NEG)], here.at[I_NEG])
    copy(neg_buf.at[c], neg_buf.at[c], NG, sib).start()
    gate[...] = silu(dot(normed, win_v[:, :512])).astype(BF)

    wait(xf_v, here.at[I_X])
    wait(a_buf.at[pl.ds(0, C - 1), 0], recv.at[A])
    copy(a_buf.at[:, c], a_buf.at[:, c], AS, sib).start()
    wait(b_buf.at[p, c], here.at[I_W3])
    chips(b_buf.at[p, c], b_buf.at[p, c], B)
    wait(a_buf.at[:, 0], recv.at[AS])
    z1 = dot(xf_v[...], a_buf[...].reshape(G * rows, 128))
    pre1[...] = z1
    h1_buf[s] = silu(z1).astype(BF)
    z_bcast(h1_buf, H1)

    def local_row(ids):
        return jnp.where((ids // RH) % 4 == me, (ids // (2 * R)) * RH + ids % RH, -1)

    wait(neg_buf.at[0], recv.at[NG])
    n_rows = C * RH
    for e in (0, 1):
        ids = local_row(neg_buf[e, :, :NEG])
        hot = (lax.broadcasted_iota(jnp.int32, (n_rows, NEG), 0) == ids).astype(F32).astype(BF)
        cnt[e] = dot(hot, jnp.ones((NEG, 128), BF))
    def whole(buf):
        return jnp.concatenate([buf[j % 2, j // 2] for j in range(2 * NB)], axis=1)

    wait(a2_buf.at[pl.ds(0, C - 1), 0], recv.at[A2])
    copy(a2_buf.at[:, c], a2_buf.at[:, c], AS2, sib).start()
    wait(qr_buf.at[pl.ds(0, S - 1)], recv.at[QKV])
    for j in range(S):
        x = qr_buf[j]
        q_scr[tok * j : tok * (j + 1)] = x[:tok, :DH]
        k_scr[tok * j : tok * (j + 1)] = x[:tok, DH:]
        v_scr[tok * j : tok * (j + 1)] = jnp.concatenate([x[tok:, :DH], x[tok:, DH:]], axis=0)

    inv_len = 1.0 / jnp.full((1, 1), length, jnp.int32).astype(F32)
    W = 2 * tok

    def attend(b):
        q = q_scr[W * b : W * (b + 1)]
        acc = jnp.zeros((W, DH), F32)
        for kb in range(b + 1):
            hs = dot_t(q, k_scr[W * kb : W * (kb + 1)]) * (0.5 * DH ** (-0.5))
            w = (hs * inv_len) * (1.0 + jnp.tanh(hs))
            if kb == b:
                r = lax.broadcasted_iota(jnp.int32, (W, W), 0)
                cc = lax.broadcasted_iota(jnp.int32, (W, W), 1)
                w = jnp.where(cc <= r, w, 0.0)
            acc = acc + dot(w.astype(BF), v_scr[W * kb : W * (kb + 1)])
        pos = W * b + lax.broadcasted_iota(jnp.int32, (W, 1), 0)
        acc = jnp.where(pos < length, acc, 0.0).astype(BF)
        for i in (0, 1):
            o = acc[tok * i : tok * (i + 1)]
            at_send[2 * b + i] = jnp.concatenate([o[: tok // 2], o[tok // 2 :]], axis=1)

    for b in reversed(range(S // 2)):
        attend(b)
    at_recv[s] = at_send[s]

    def at_step(k, _):
        t = z_away(k)
        copy(at_send.at[t], at_recv.at[s], ATT, (t, g)).start()
        return 0

    lax.fori_loop(0, S - 1, at_step, 0)
    wait(h1_buf.at[pl.ds(0, S - 1)], recv.at[H1])
    wait(a2_buf.at[:, 0], recv.at[AS2])
    h1 = jnp.concatenate([h1_buf[j] for j in range(S)], axis=1)
    for j in range(NB):
        z2 = dot(h1, a2_buf[:, :, j].reshape(G * rows, 128))
        h2_buf[par, j] = silu(z2).astype(BF)
        sl2_buf[par, j] = silu_slope(z2).astype(BF)
    copy(h2_buf.at[par], h2_buf.at[par], H2, pair).start()

    wait(b_buf.at[pl.ds(0, C - 1), 0], recv.at[B])
    copy(b_buf.at[:, c], b_buf.at[:, c], BS, sib).start()

    wait(h2_buf.at[0], recv.at[H2])
    wait(b_buf.at[:, 0], recv.at[BS])
    h2 = whole(h2_buf)
    raw = dot(h2, b_buf[...].reshape(G * rows, 512))
    item_inverse = lax.rsqrt(jnp.sum(raw * raw, axis=-1, keepdims=True) + EPS_UNIT)
    unit_item = raw * item_inverse
    ui[...] = unit_item
    inv[...] = jnp.broadcast_to(item_inverse, inv.shape)
    pe_buf[p] = ui[pl.ds(pl.multiple_of(par * RH, RH), RH)].astype(BF)
    chips(pe_buf.at[p], pe_buf.at[p], PE)

    wait(wout_v, here.at[I_WOUT])
    wait(at_recv.at[pl.ds(0, S - 1)], recv.at[ATT])
    tops, bottoms = [], []
    for h in range(S):
        x = at_recv[h]
        tops.append(x[:, :DH])
        bottoms.append(x[:, DH:])
    merged = jnp.concatenate(
        [jnp.concatenate(tops, axis=1), jnp.concatenate(bottoms, axis=1)], axis=0).astype(F32)
    branch = (layer_norm(merged) * gate[...].astype(F32)).astype(BF)
    layer_out = (hist_v[...].astype(F32) + dot(branch, wout_v[...])).astype(BF)
    lo_ref[...] = layer_out
    outward = layer_out.astype(F32)
    user_inverse = lax.rsqrt(jnp.sum(outward * outward, axis=-1, keepdims=True) + EPS_UNIT)
    unit_user = outward * user_inverse
    u_buf[me] = unit_user.astype(BF)
    copy(u_buf.at[me], u_buf.at[me], UP, pair).start()
    copy(u_buf.at[me], u_buf.at[me], US, sib).start()
    uu[...] = unit_user
    uinv[...] = jnp.broadcast_to(user_inverse, (tok, 128))

    wait(nx_buf.at[pl.ds(0, 3)], recv.at[NX])
    pair_pos = lax.broadcasted_iota(jnp.int32, (1, W), 1)
    positions = (s // 2) * W + pair_pos

    def items_of(u):
        return local_row(jnp.concatenate([nx_buf[2 * u], nx_buf[2 * u + 1]], axis=1))

    def valid_of(u):
        lens = neg_buf[u, :, NEG:]
        return (positions < jnp.concatenate([lens, lens], axis=1) - 1).astype(F32)

    wait(u_buf.at[0], recv.at[UP])
    other = 2 * c + 1 - par
    copy(u_buf.at[other], u_buf.at[other], UT, sib).start()
    wait(pe_buf.at[pl.ds(0, C - 1)], recv.at[PE])

    Q = 4
    CQ = C // Q
    width = n_rows // Q
    row_id = lax.broadcasted_iota(jnp.int32, (width, W), 0)

    def logits_of(u):
        users = u_buf[pl.ds(2 * u, 2)].reshape(W, 512)
        items = items_of(u)
        den = jnp.zeros((1, W), F32)
        positive = jnp.zeros((1, W), F32)
        for q in range(Q):
            logit = TEMP * dot_t(pe_buf[CQ * q : CQ * (q + 1)].reshape(width, 512), users)
            own = row_id + width * q == items
            times = cnt[u, width * q : width * (q + 1)]
            e = jnp.where(own, 0.0, jnp.exp(logit) * jnp.concatenate([times, times], axis=1))
            em[u, width * q : width * (q + 1)] = e
            den = den + jnp.sum(e, axis=0, keepdims=True)
            positive = positive + jnp.sum(jnp.where(own, logit, 0.0), axis=0, keepdims=True)
        dn_buf[me, u] = jnp.concatenate([den, positive], axis=1)

    logits_of(c)
    wait(u_buf.at[0], recv.at[US])
    wait(u_buf.at[0], recv.at[UT])
    logits_of(1 - c)
    quad(dn_buf, DN)
    wait(dn_buf.at[pl.ds(0, 3)], recv.at[DN])
    for u in (0, 1):
        sums = dn_buf[0, u] + dn_buf[1, u] + dn_buf[2, u] + dn_buf[3, u]
        positive = sums[:, W:]
        positive_exp = jnp.exp(positive)
        den = sums[:, :W] + positive_exp
        valid = valid_of(u)
        items = items_of(u)
        slope = valid * (positive_exp / den - 1.0)
        scale = valid / den
        for q in range(Q):
            block = slice(width * q, width * (q + 1))
            st[u, block] = jnp.where(row_id + width * q == items, slope, scale * em[u, block]).astype(BF)
        nll[u] = valid * (jnp.log(den) - positive)

    def pool_part(e):
        lo, n = PARTS[e]
        part = dot(st[0], u_buf[0:2, :, lo : lo + n].reshape(W, n))
        part = part + dot(st[1], u_buf[2:4, :, lo : lo + n].reshape(W, n))
        rs_send[e][...] = (TEMP * part).astype(BF).reshape(C, RH, n)

    pool_part(0)
    chip_scatter(rs_send[0], rs_recv[0], RS)

    per_block = 128 // (2 * rows)
    copy(a2_buf.at[pl.ds(per_block * (s + 1 - 2 * par), per_block)], w2r_buf.at[par], W2, pair).start()
    w2r_buf[par] = a2_buf[pl.ds(per_block * s, per_block)]
    copy(sl2_buf.at[par], sl2_buf.at[par], SL2, pair).start()

    mine = pair_pos // tok == par
    loss_sum = jnp.sum(jnp.where(mine, nll[c], 0.0))
    lane = lax.broadcasted_iota(jnp.int32, (8, 128), 1)
    count = jnp.full((8, 128), length - 1, jnp.int32).astype(F32)
    zl_buf[s] = jnp.where(lane == 0, loss_sum, jnp.where(lane == 1, count, 0.0))
    z_bcast(zl_buf, ZL)

    rows_here = pe_buf[...].reshape(n_rows, 512)
    for u in (0, 1):
        ud[u] = t_dot(st[u], rows_here).reshape(2, tok, 512)
    uds_send[...] = ud[1 - c].astype(BF)
    copy(uds_send, uds_recv, UDS, sib).start()

    pool_part(1)
    wait(rs_recv[0].at[pl.ds(0, C - 1)], send.at[RS])
    chip_scatter(rs_send[1], rs_recv[1], RS + 1)

    def plane_sum(e):
        wait(rs_recv[e].at[pl.ds(0, C - 1)], recv.at[RS + e])
        za_buf[e][s] = jnp.sum(rs_recv[e][...].astype(F32), axis=0).astype(BF)
        z_bcast(za_buf[e], ZA + e)

    plane_sum(0)
    plane_sum(1)
    wait(zl_buf.at[pl.ds(0, S - 1)], recv.at[ZL])
    lg_buf[g] = jnp.sum(zl_buf[...], axis=0)

    def lg_step(k, _):
        copy(lg_buf.at[g], lg_buf.at[g], GL, (s, lax.rem(g + k, G))).start()
        return 0

    lax.fori_loop(1, G, lg_step, 0)
    wait(w2r_buf.at[0], recv.at[W2])
    w2_rows = jnp.concatenate([w2r_buf[j % 2, :, :, j // 2].reshape(128, 128) for j in range(2 * NB)], axis=1)
    wait(sl2_buf.at[0], recv.at[SL2])
    h1 = jnp.concatenate([h1_buf[j] for j in range(S)], axis=1)
    h2 = whole(h2_buf)
    slope2 = whole(sl2_buf).astype(F32)
    slope1 = silu_slope(pre1[...])

    for e in range(2):
        wait(za_buf[e].at[pl.ds(0, S - 1)], recv.at[ZA + e])
    chunks = []
    for e in range(2):
        sums = []
        for o in (0, 1):
            part = za_buf[e][o].astype(F32)
            for t in range(o + 2, S, 2):
                part = part + za_buf[e][t].astype(F32)
            sums.append(part)
        chunks.append(jnp.concatenate(sums, axis=0))
    own_grad = jnp.concatenate(chunks, axis=1)
    uin = ui[...]
    raw_grad = (inv[:, :1] * (own_grad - uin * jnp.sum(uin * own_grad, axis=-1, keepdims=True))).astype(BF)
    rg[...] = raw_grad
    sg = (dot_t(raw_grad, b_buf[...].reshape(G * rows, 512)) * slope2).astype(BF)
    sg_scr[...] = sg
    fg = (dot_t(sg, w2_rows) * slope1).astype(BF)
    g2_send[...] = t_dot(xf_v[...], fg).astype(BF).reshape(G, rows, 128)
    grp_scatter(g2_send, g2_recv, G2)
    q_cols = pl.ds(pl.multiple_of(lax.rem(s, 4) * 128, 128), 128)
    gl_scr[...] = t_dot(h2, rg[:, q_cols]).astype(BF).reshape(C, 2, 2, half, 128)
    gp1[:, :, :rows] = t_dot(h1, sg_scr[:, cols]).astype(BF).reshape(C, 2, rows, 128)
    gp1[:, :, rows:] = gl_scr[:, :, s // 4]
    copy(gp1.at[:, 1 - c], gp1_recv, GP1, sib).start()
    wait(uds_recv, recv.at[UDS])
    udp_send[...] = (ud[c, 1 - par] + uds_recv[1 - par].astype(F32)).astype(BF)
    copy(udp_send, udp_recv, UDP, pair).start()
    wait(gp1_recv, recv.at[GP1])
    g1_send[...] = (gp1[:, c].astype(F32) + gp1_recv[...].astype(F32)).astype(BF)
    chip_scatter(g1_send, g1_recv, G1)

    wait(lg_buf.at[pl.ds(0, G - 1)], recv.at[GL])
    total = jnp.sum(lg_buf[...], axis=0)
    numer = jnp.sum(jnp.where(lane == 0, total, 0.0), axis=1, keepdims=True)
    denom = jnp.sum(jnp.where(lane == 1, total, 0.0), axis=1, keepdims=True)
    loss_ref[...] = jnp.broadcast_to(numer * S / denom, loss_ref.shape)

    wait(g2_recv.at[pl.ds(0, G - 1)], recv.at[G2])
    f2_buf[s] = jnp.sum(g2_recv[...].astype(F32), axis=0).astype(BF)
    z_bcast(f2_buf, F2)
    wait(g1_recv.at[pl.ds(0, C - 1)], recv.at[G1])
    f1_buf[s] = jnp.sum(g1_recv[...].astype(F32), axis=0).astype(BF)
    z_bcast(f1_buf, F1)

    wait(udp_recv, recv.at[UDP])
    user_dir = TEMP * (ud[c, par] + uds_recv[par].astype(F32) + udp_recv[...].astype(F32))
    uun = uu[...]
    ug_ref[...] = uinv[:, :1] * (user_dir - uun * jnp.sum(uun * user_dir, axis=-1, keepdims=True))
    wait(a_buf.at[pl.ds(0, C - 1), 0], send.at[A])
    wait(a2_buf.at[pl.ds(0, C - 1), 0], send.at[A2])
    wait(a2_buf.at[:, 0], send.at[AS2])
    wait(b_buf.at[pl.ds(0, C - 1), 0], send.at[B])
    wait(a_buf.at[:, 0], send.at[AS])
    wait(b_buf.at[:, 0], send.at[BS])
    wait(pe_buf.at[pl.ds(0, C - 1)], send.at[PE])
    wait(rs_recv[1].at[pl.ds(0, C - 1)], send.at[RS + 1])
    for e in range(2):
        wait(za_buf[e].at[pl.ds(0, S - 1)], send.at[ZA + e])
    for buf, i in ((qr_buf, QKV), (at_recv, ATT), (zl_buf, ZL)):
        wait(buf.at[pl.ds(0, S - 1)], send.at[i])
    wait(h1_buf.at[pl.ds(0, S - 1)], send.at[H1])
    wait(h2_buf.at[0], send.at[H2])
    wait(sl2_buf.at[0], send.at[SL2])
    wait(nx_buf.at[pl.ds(0, 3)], send.at[NX])
    wait(neg_buf.at[0], send.at[NG])
    for i in (UP, US, UT):
        wait(u_buf.at[0], send.at[i])
    wait(dn_buf.at[pl.ds(0, 3)], send.at[DN])
    wait(uds_recv, send.at[UDS])
    wait(udp_recv, send.at[UDP])
    wait(gp1_recv, send.at[GP1])
    wait(lg_buf.at[pl.ds(0, G - 1)], send.at[GL])
    wait(g1_recv.at[pl.ds(0, C - 1)], send.at[G1])
    wait(g2_recv.at[pl.ds(0, G - 1)], send.at[G2])
    wait(w2r_buf.at[0], send.at[W2])

    wait(f2_buf.at[pl.ds(0, S - 1)], recv.at[F2])
    for t in range(S):
        gf_ref[:, 128 * t : 128 * (t + 1)] = f2_buf[t].astype(F32)
    wait(f1_buf.at[pl.ds(0, S - 1)], recv.at[F1])
    for t in range(S):
        gm_ref[:, 128 * t : 128 * (t + 1)] = f1_buf[t, :rows].astype(F32)
        gl_ref[half * (t // 4) : half * (t // 4 + 1), 128 * (t % 4) : 128 * (t % 4 + 1)] = f1_buf[t, rows:].astype(F32)
    wait(f1_buf.at[pl.ds(0, S - 1)], send.at[F1])
    wait(f2_buf.at[pl.ds(0, S - 1)], send.at[F2])


def tail(*refs):
    ins, outs, sem = refs[:6], refs[6:12], refs[12]
    for i in (0, 2, 3, 4, 5):
        pltpu.make_async_copy(ins[i], outs[i], sem.at[i]).start()
    outs[1][0, 0] = jnp.max(ins[1][...])
    for i in (0, 2, 3, 4, 5):
        pltpu.make_async_copy(ins[i], outs[i], sem.at[i]).wait()


def local(history, lengths, next_items, negatives, input_weight, output_weight, pool_features,
          tower_first, tower_middle, tower_last, S, G):
    events = history[0]
    tok = events.shape[0]
    C = G // 2
    R = pool_features.shape[0]
    RH = R // 2
    rows = tower_first.shape[0]
    V = pltpu.VMEM
    vmem = pl.BlockSpec(memory_space=pltpu.VMEM)
    hbm = pl.BlockSpec(memory_space=pltpu.HBM)
    scratch = [
        pltpu.SemaphoreType.DMA((N_SEM,)),
        pltpu.SemaphoreType.DMA((N_SEM,)),
        pltpu.SemaphoreType.DMA((N_HERE,)),
        V((tok, 512), BF),
        V((4, 1, tok), jnp.int32),
        V((2, 1, negatives.shape[1] + 128), jnp.int32),
        V(input_weight.shape, BF),
        V(output_weight.shape, BF),
        V(pool_features.shape, BF),
        V((C, 2, rows, 128), BF),
        V((C, 2, 4, rows, 128), BF),
        V((C, 2, rows, 512), BF),
        V((2, 128 // (2 * rows), 2, 4, rows, 128), BF),
        V((S, tok + tok // 2, 128), BF),
        V((S, tok + tok // 2, 128), BF),
        V((tok, 512), BF),
        V((S * tok, DH), BF),
        V((S * tok, DH), BF),
        V((S * tok, DH), BF),
        V((S, tok // 2, 128), BF),
        V((S, tok // 2, 128), BF),
        V((S, R, 128), BF),
        V((2, 4, R, 128), BF),
        V((2, 4, R, 128), BF),
        V((R, 128), F32),
        V((R, 512), F32),
        V((R, 128), F32),
        V((C, RH, 512), BF),
        V((2, C * RH, 2 * tok), F32),
        V((2, C * RH, 2 * tok), BF),
        V((4, tok, 512), BF),
        V((4, 2, 1, 4 * tok), F32),
        V((2, 1, 2 * tok), F32),
        V((2, 2, tok, 512), F32),
        V((2, tok, 512), BF),
        V((2, tok, 512), BF),
        V((tok, 512), BF),
        V((tok, 512), BF),
        V((S, 8, 128), F32),
        V((G, 8, 128), F32),
        V((R, 512), BF),
        V((R, 1024), BF),
        V((C, 2, 2, rows // 2, 128), BF),
        V((C, 2, rows + rows // 2, 128), BF),
        V((C, rows + rows // 2, 128), BF),
        V((C, rows + rows // 2, 128), BF),
        V((C, rows + rows // 2, 128), BF),
        V((G, rows, 128), BF),
        V((G, rows, 128), BF),
        V((S, rows + rows // 2, 128), BF),
        V((S, rows, 128), BF),
        V((2, C * RH, 128), F32),
        V((tok, 512), F32),
        V((tok, 128), F32),
    ]
    for lead in (C, C, S):
        scratch += [V((lead, RH, n), BF) for _, n in PARTS]
    shapes = [
        jax.ShapeDtypeStruct((tok, 512), BF),
        jax.ShapeDtypeStruct((8, 128), F32),
        jax.ShapeDtypeStruct((tok, 512), F32),
        jax.ShapeDtypeStruct((rows, 1024), F32),
        jax.ShapeDtypeStruct((rows, 1024), F32),
        jax.ShapeDtypeStruct((rows, 512), F32),
    ]
    results = pl.pallas_call(
        functools.partial(kernel, S, G),
        out_shape=[pltpu.VMEM(x.shape, x.dtype) for x in shapes],
        in_specs=[pl.BlockSpec(memory_space=pltpu.SMEM)] + [hbm] * 9,
        out_specs=[vmem] * 6,
        scratch_shapes=scratch,
        compiler_params=pltpu.CompilerParams(
            collective_id=0, has_side_effects=True, vmem_limit_bytes=56 * 1024 * 1024),
    )(lengths, events, next_items, negatives, input_weight, output_weight, pool_features,
      tower_first, tower_middle, tower_last)
    lo, loss, ug, gf, gm, gl = pl.pallas_call(
        tail,
        out_shape=shapes[:1] + [jax.ShapeDtypeStruct((1, 1), F32)] + shapes[2:],
        in_specs=[vmem] * 6,
        out_specs=[hbm, pl.BlockSpec(memory_space=pltpu.SMEM)] + [hbm] * 4,
        scratch_shapes=[pltpu.SemaphoreType.DMA((6,))],
        compiler_params=pltpu.CompilerParams(vmem_limit_bytes=1024 * 1024),
    )(*results)
    return lo[None], loss.reshape(()), ug[None], gf, gm, gl


def solution(mesh):
    placed = (
        P("grp", "seq", None), P("grp"), P("grp", "seq"), P("grp", None), P(), P(),
        P("grp", None), P("grp", None), P("grp", None), P("grp", None),
    )
    return jax.shard_map(
        functools.partial(local, S=mesh.shape["seq"], G=mesh.shape["grp"]),
        mesh=mesh,
        in_specs=placed,
        out_specs=(
            P("grp", "seq", None), P(), P("grp", "seq", None),
            P("grp", None), P("grp", None), P("grp", None),
        ),
        check_vma=False,
    )
```

```python
import functools

import jax
import jax.numpy as jnp
from jax import lax
from jax.experimental import pallas as pl
from jax.experimental.pallas import tpu as pltpu
from jax.sharding import PartitionSpec as P

DH = 64
EPS_NORM = 1e-05
EPS_UNIT = 1e-06
TEMP = 20.0

MESH = pl.DeviceIdType.MESH
BF = jnp.bfloat16
F32 = jnp.float32

(A, A2, B, AS, AS2, BS, QKV, ATT, H1, H2, SL2, NX, NG, UP, US, UT, DN, UDS, UDP, ZL, GL, GP1, G1, G2, F1, F2,
 W2, PE) = range(28)
RS, ZA = 28, 30
N_SEM = 32

PARTS = ((0, 256), (256, 256))

(I_W3, I_H, I_WIN, I_WOUT, I_X, I_NEG, I_NXT, I_W1) = range(8)
I_W2 = 8
N_HERE = 12


def silu(x):
    half = 0.5 * x
    return half * (1.0 + jnp.tanh(half))


def silu_slope(z):
    sigma = 0.5 * (1.0 + jnp.tanh(0.5 * z))
    return sigma * (1.0 + z * (1.0 - sigma))


def layer_norm(values):
    center = values - jnp.mean(values, axis=-1, keepdims=True)
    spread = jnp.mean(center * center, axis=-1, keepdims=True)
    return center * lax.rsqrt(spread + EPS_NORM)


def dot(a, b):
    return jnp.dot(a, b, preferred_element_type=F32)


def dot_t(a, b):
    return lax.dot_general(a, b, (((1,), (1,)), ((), ())), preferred_element_type=F32)


def t_dot(a, b):
    return lax.dot_general(a, b, (((0,), (0,)), ((), ())), preferred_element_type=F32)


def wait(ref, sem):
    pltpu.make_async_copy(ref, ref, sem).wait()


def kernel(
    S, G,
    len_ref, hist, nxt, neg, win, wout, xf, w1, w2, w3,
    lo_ref, loss_ref, ug_ref, gf_ref, gm_ref, gl_ref,
    send, recv, here,
    hist_v, nx_buf, neg_buf, win_v, wout_v, xf_v,
    a_buf, a2_buf, b_buf, w2r_buf, qs_buf, qr_buf, gate, k_scr, q_scr, v_scr, at_send, at_recv,
    h1_buf, h2_buf, sl2_buf, pre1, ui, inv, pe_buf, em, st, u_buf,
    dn_buf, nll, ud, uds_send, uds_recv, udp_send, udp_recv, zl_buf, lg_buf, rg, sg_scr,
    gl_scr, gp1, gp1_recv, g1_send, g1_recv, g2_send, g2_recv, f1_buf, f2_buf, cnt, uu, uinv, *parts,
):
    C = G // 2
    s = lax.axis_index("seq")
    g = lax.axis_index("grp")
    p = g // 2
    c = g % 2
    par = s % 2
    tok = hist_v.shape[0]
    me = 2 * c + par
    rows = b_buf.shape[2]
    NB = a2_buf.shape[2]
    half = rows // 2
    NEG = neg.shape[1]
    R = xf_v.shape[0]
    RH = R // 2
    length = len_ref[0]
    pair = (s + 1 - 2 * par, g)
    sib = (s, 2 * p + 1 - c)
    diag = (s + 1 - 2 * par, 2 * p + 1 - c)
    cols = pl.ds(pl.multiple_of(s * 128, 128), 128)

    def copy(src, dst, i, dev):
        return pltpu.make_async_remote_copy(
            src_ref=src, dst_ref=dst, send_sem=send.at[i], recv_sem=recv.at[i],
            device_id=dev, device_id_type=MESH)

    def fetch(src, dst, i):
        pltpu.make_async_copy(src, dst, here.at[i]).start()

    def z_away(i):
        return lax.rem(s + S // 2 + (1 - 2 * (i % 2)) * ((i + 1) // 2), S)

    def z_bcast(buf, i):
        def step(k, _):
            copy(buf.at[s], buf.at[s], i, (z_away(k), g)).start()
            return 0
        lax.fori_loop(0, S - 1, step, 0)

    def chips(src, dst, i):
        def step(k, _):
            copy(src, dst, i, (s, 2 * lax.rem(p + k, C) + c)).start()
            return 0
        lax.fori_loop(1, C, step, 0)

    def chip_scatter(src, dst, i):
        def step(k, _):
            t = lax.rem(p + k, C)
            copy(src.at[t], dst.at[p], i, (s, 2 * t + c)).start()
            return 0
        lax.fori_loop(1, C, step, 0)
        dst[p] = src[p]

    rs_send, rs_recv, za_buf = parts[0:2], parts[2:4], parts[4:6]

    def grp_scatter(src, dst, i):
        def step(k, _):
            t = lax.rem(g + k, G)
            copy(src.at[t], dst.at[g], i, (s, t)).start()
            return 0
        lax.fori_loop(1, G, step, 0)
        dst[g] = src[g]

    def quad(buf, i):
        for dev in (sib, pair, diag):
            copy(buf.at[me], buf.at[me], i, dev).start()

    fetch(w1.at[:, cols], a_buf.at[p, c], I_W1)
    barrier = pltpu.get_barrier_semaphore()

    def greet_grp(k, _):
        pl.semaphore_signal(barrier, inc=1, device_id=(s, lax.rem(g + k, G)), device_id_type=MESH)
        return 0

    def greet_seq(k, _):
        pl.semaphore_signal(barrier, inc=1, device_id=(z_away(k), g), device_id_type=MESH)
        return 0

    lax.fori_loop(0, S - 1, greet_seq, 0)
    lax.fori_loop(G // 2, G, greet_grp, 0)
    lax.fori_loop(1, G // 2, greet_grp, 0)
    pl.semaphore_signal(barrier, inc=1, device_id=diag, device_id_type=MESH)

    for j in range(NB):
        block = pl.ds(pl.multiple_of((2 * j + par) * 128, 128), 128)
        fetch(w2.at[:, block], a2_buf.at[p, c, j], I_W2 + j)
    fetch(hist, hist_v, I_H)
    fetch(win, win_v, I_WIN)
    fetch(nxt, nx_buf.at[me], I_NXT)
    fetch(w3, b_buf.at[p, c], I_W3)
    fetch(xf, xf_v, I_X)
    fetch(neg, neg_buf.at[c, :, pl.ds(0, NEG)], I_NEG)
    fetch(wout, wout_v, I_WOUT)
    neg_buf[c, :, NEG:] = jnp.full((1, 128), length, jnp.int32)
    wait(a_buf.at[p, c], here.at[I_W1])
    pl.semaphore_wait(barrier, (G - 1) + (S - 1) + 1)
    chips(a_buf.at[p, c], a_buf.at[p, c], A)

    wait(hist_v, here.at[I_H])
    normed = layer_norm(hist_v[...].astype(F32)).astype(BF)
    wait(win_v, here.at[I_WIN])
    for j in range(4):
        x = silu(dot(normed, win_v[:, 512 + 384 * j : 512 + 384 * (j + 1)])).astype(BF)
        for e in (0, 1):
            o = 192 * e
            qs_buf[2 * j + e, :tok] = x[:, o : o + 128]
            v = x[:, o + 128 : o + 192]
            qs_buf[2 * j + e, tok:] = jnp.concatenate([v[: tok // 2], v[tok // 2 :]], axis=1)

    def qkv_step(k, _):
        t = z_away(k)
        copy(qs_buf.at[t], qr_buf.at[s], QKV, (t, g)).start()
        return 0

    lax.fori_loop(0, S - 1, qkv_step, 0)
    qr_buf[s] = qs_buf[s]
    for j in range(NB):
        wait(a2_buf.at[p, c, j], here.at[I_W2 + j])
    chips(a2_buf.at[p, c], a2_buf.at[p, c], A2)
    wait(nx_buf.at[me], here.at[I_NXT])
    quad(nx_buf, NX)
    wait(neg_buf.at[c, :, pl.ds(0, NEG)], here.at[I_NEG])
    copy(neg_buf.at[c], neg_buf.at[c], NG, sib).start()
    gate[...] = silu(dot(normed, win_v[:, :512])).astype(BF)

    wait(xf_v, here.at[I_X])
    wait(a_buf.at[pl.ds(0, C - 1), 0], recv.at[A])
    copy(a_buf.at[:, c], a_buf.at[:, c], AS, sib).start()
    wait(b_buf.at[p, c], here.at[I_W3])
    chips(b_buf.at[p, c], b_buf.at[p, c], B)
    wait(a_buf.at[:, 0], recv.at[AS])
    z1 = dot(xf_v[...], a_buf[...].reshape(G * rows, 128))
    pre1[...] = z1
    h1_buf[s] = silu(z1).astype(BF)
    z_bcast(h1_buf, H1)

    def local_row(ids):
        return jnp.where((ids // RH) % 4 == me, (ids // (2 * R)) * RH + ids % RH, -1)

    wait(neg_buf.at[0], recv.at[NG])
    n_rows = C * RH
    for e in (0, 1):
        ids = local_row(neg_buf[e, :, :NEG])
        hot = (lax.broadcasted_iota(jnp.int32, (n_rows, NEG), 0) == ids).astype(F32).astype(BF)
        cnt[e] = dot(hot, jnp.ones((NEG, 128), BF))
    def whole(buf):
        return jnp.concatenate([buf[j % 2, j // 2] for j in range(2 * NB)], axis=1)

    wait(a2_buf.at[pl.ds(0, C - 1), 0], recv.at[A2])
    copy(a2_buf.at[:, c], a2_buf.at[:, c], AS2, sib).start()
    wait(qr_buf.at[pl.ds(0, S - 1)], recv.at[QKV])
    for j in range(S):
        x = qr_buf[j]
        q_scr[tok * j : tok * (j + 1)] = x[:tok, :DH]
        k_scr[tok * j : tok * (j + 1)] = x[:tok, DH:]
        v_scr[tok * j : tok * (j + 1)] = jnp.concatenate([x[tok:, :DH], x[tok:, DH:]], axis=0)

    inv_len = 1.0 / jnp.full((1, 1), length, jnp.int32).astype(F32)
    W = 2 * tok

    def attend(b):
        q = q_scr[W * b : W * (b + 1)]
        acc = jnp.zeros((W, DH), F32)
        for kb in range(b + 1):
            hs = dot_t(q, k_scr[W * kb : W * (kb + 1)]) * (0.5 * DH ** (-0.5))
            w = (hs * inv_len) * (1.0 + jnp.tanh(hs))
            if kb == b:
                r = lax.broadcasted_iota(jnp.int32, (W, W), 0)
                cc = lax.broadcasted_iota(jnp.int32, (W, W), 1)
                w = jnp.where(cc <= r, w, 0.0)
            acc = acc + dot(w.astype(BF), v_scr[W * kb : W * (kb + 1)])
        pos = W * b + lax.broadcasted_iota(jnp.int32, (W, 1), 0)
        acc = jnp.where(pos < length, acc, 0.0).astype(BF)
        for i in (0, 1):
            o = acc[tok * i : tok * (i + 1)]
            at_send[2 * b + i] = jnp.concatenate([o[: tok // 2], o[tok // 2 :]], axis=1)

    for b in reversed(range(S // 2)):
        attend(b)
    at_recv[s] = at_send[s]

    def at_step(k, _):
        t = z_away(k)
        copy(at_send.at[t], at_recv.at[s], ATT, (t, g)).start()
        return 0

    lax.fori_loop(0, S - 1, at_step, 0)
    wait(h1_buf.at[pl.ds(0, S - 1)], recv.at[H1])
    wait(a2_buf.at[:, 0], recv.at[AS2])
    h1 = jnp.concatenate([h1_buf[j] for j in range(S)], axis=1)
    for j in range(NB):
        z2 = dot(h1, a2_buf[:, :, j].reshape(G * rows, 128))
        h2_buf[par, j] = silu(z2).astype(BF)
        sl2_buf[par, j] = silu_slope(z2).astype(BF)
    copy(h2_buf.at[par], h2_buf.at[par], H2, pair).start()

    wait(b_buf.at[pl.ds(0, C - 1), 0], recv.at[B])
    copy(b_buf.at[:, c], b_buf.at[:, c], BS, sib).start()

    wait(h2_buf.at[0], recv.at[H2])
    wait(b_buf.at[:, 0], recv.at[BS])
    h2 = whole(h2_buf)
    raw = dot(h2, b_buf[...].reshape(G * rows, 512))
    item_inverse = lax.rsqrt(jnp.sum(raw * raw, axis=-1, keepdims=True) + EPS_UNIT)
    unit_item = raw * item_inverse
    ui[...] = unit_item
    inv[...] = jnp.broadcast_to(item_inverse, inv.shape)
    pe_buf[p] = ui[pl.ds(pl.multiple_of(par * RH, RH), RH)].astype(BF)
    chips(pe_buf.at[p], pe_buf.at[p], PE)

    wait(wout_v, here.at[I_WOUT])
    wait(at_recv.at[pl.ds(0, S - 1)], recv.at[ATT])
    tops, bottoms = [], []
    for h in range(S):
        x = at_recv[h]
        tops.append(x[:, :DH])
        bottoms.append(x[:, DH:])
    merged = jnp.concatenate(
        [jnp.concatenate(tops, axis=1), jnp.concatenate(bottoms, axis=1)], axis=0).astype(F32)
    branch = (layer_norm(merged) * gate[...].astype(F32)).astype(BF)
    layer_out = (hist_v[...].astype(F32) + dot(branch, wout_v[...])).astype(BF)
    lo_ref[...] = layer_out
    outward = layer_out.astype(F32)
    user_inverse = lax.rsqrt(jnp.sum(outward * outward, axis=-1, keepdims=True) + EPS_UNIT)
    unit_user = outward * user_inverse
    u_buf[me] = unit_user.astype(BF)
    copy(u_buf.at[me], u_buf.at[me], UP, pair).start()
    copy(u_buf.at[me], u_buf.at[me], US, sib).start()
    uu[...] = unit_user
    uinv[...] = jnp.broadcast_to(user_inverse, (tok, 128))

    wait(nx_buf.at[pl.ds(0, 3)], recv.at[NX])
    pair_pos = lax.broadcasted_iota(jnp.int32, (1, W), 1)
    positions = (s // 2) * W + pair_pos

    def items_of(u):
        return local_row(jnp.concatenate([nx_buf[2 * u], nx_buf[2 * u + 1]], axis=1))

    def valid_of(u):
        lens = neg_buf[u, :, NEG:]
        return (positions < jnp.concatenate([lens, lens], axis=1) - 1).astype(F32)

    wait(u_buf.at[0], recv.at[UP])
    other = 2 * c + 1 - par
    copy(u_buf.at[other], u_buf.at[other], UT, sib).start()
    wait(pe_buf.at[pl.ds(0, C - 1)], recv.at[PE])

    Q = 4
    CQ = C // Q
    width = n_rows // Q
    row_id = lax.broadcasted_iota(jnp.int32, (width, W), 0)

    def logits_of(u):
        users = u_buf[pl.ds(2 * u, 2)].reshape(W, 512)
        items = items_of(u)
        den = jnp.zeros((1, W), F32)
        positive = jnp.zeros((1, W), F32)
        for q in range(Q):
            logit = TEMP * dot_t(pe_buf[CQ * q : CQ * (q + 1)].reshape(width, 512), users)
            own = row_id + width * q == items
            times = cnt[u, width * q : width * (q + 1)]
            e = jnp.where(own, 0.0, jnp.exp(logit) * jnp.concatenate([times, times], axis=1))
            em[u, width * q : width * (q + 1)] = e
            den = den + jnp.sum(e, axis=0, keepdims=True)
            positive = positive + jnp.sum(jnp.where(own, logit, 0.0), axis=0, keepdims=True)
        dn_buf[me, u] = jnp.concatenate([den, positive], axis=1)

    logits_of(c)
    wait(u_buf.at[0], recv.at[US])
    wait(u_buf.at[0], recv.at[UT])
    logits_of(1 - c)
    quad(dn_buf, DN)
    wait(dn_buf.at[pl.ds(0, 3)], recv.at[DN])
    for u in (0, 1):
        sums = dn_buf[0, u] + dn_buf[1, u] + dn_buf[2, u] + dn_buf[3, u]
        positive = sums[:, W:]
        positive_exp = jnp.exp(positive)
        den = sums[:, :W] + positive_exp
        valid = valid_of(u)
        items = items_of(u)
        slope = valid * (positive_exp / den - 1.0)
        scale = valid / den
        for q in range(Q):
            block = slice(width * q, width * (q + 1))
            st[u, block] = jnp.where(row_id + width * q == items, slope, scale * em[u, block]).astype(BF)
        nll[u] = valid * (jnp.log(den) - positive)

    def pool_part(e):
        lo, n = PARTS[e]
        part = dot(st[0], u_buf[0:2, :, lo : lo + n].reshape(W, n))
        part = part + dot(st[1], u_buf[2:4, :, lo : lo + n].reshape(W, n))
        rs_send[e][...] = (TEMP * part).astype(BF).reshape(C, RH, n)

    pool_part(0)
    chip_scatter(rs_send[0], rs_recv[0], RS)

    per_block = 128 // (2 * rows)
    copy(a2_buf.at[pl.ds(per_block * (s + 1 - 2 * par), per_block)], w2r_buf.at[par], W2, pair).start()
    w2r_buf[par] = a2_buf[pl.ds(per_block * s, per_block)]
    copy(sl2_buf.at[par], sl2_buf.at[par], SL2, pair).start()

    mine = pair_pos // tok == par
    loss_sum = jnp.sum(jnp.where(mine, nll[c], 0.0))
    lane = lax.broadcasted_iota(jnp.int32, (8, 128), 1)
    count = jnp.full((8, 128), length - 1, jnp.int32).astype(F32)
    zl_buf[s] = jnp.where(lane == 0, loss_sum, jnp.where(lane == 1, count, 0.0))
    z_bcast(zl_buf, ZL)

    rows_here = pe_buf[...].reshape(n_rows, 512)
    for u in (0, 1):
        ud[u] = t_dot(st[u], rows_here).reshape(2, tok, 512)
    uds_send[...] = ud[1 - c].astype(BF)
    copy(uds_send, uds_recv, UDS, sib).start()

    pool_part(1)
    wait(rs_recv[0].at[pl.ds(0, C - 1)], send.at[RS])
    chip_scatter(rs_send[1], rs_recv[1], RS + 1)

    def plane_sum(e):
        wait(rs_recv[e].at[pl.ds(0, C - 1)], recv.at[RS + e])
        za_buf[e][s] = jnp.sum(rs_recv[e][...].astype(F32), axis=0).astype(BF)
        z_bcast(za_buf[e], ZA + e)

    plane_sum(0)
    plane_sum(1)
    wait(zl_buf.at[pl.ds(0, S - 1)], recv.at[ZL])
    lg_buf[g] = jnp.sum(zl_buf[...], axis=0)

    def lg_step(k, _):
        copy(lg_buf.at[g], lg_buf.at[g], GL, (s, lax.rem(g + k, G))).start()
        return 0

    lax.fori_loop(1, G, lg_step, 0)
    wait(w2r_buf.at[0], recv.at[W2])
    w2_rows = jnp.concatenate([w2r_buf[j % 2, :, :, j // 2].reshape(128, 128) for j in range(2 * NB)], axis=1)
    wait(sl2_buf.at[0], recv.at[SL2])
    h1 = jnp.concatenate([h1_buf[j] for j in range(S)], axis=1)
    h2 = whole(h2_buf)
    slope2 = whole(sl2_buf).astype(F32)
    slope1 = silu_slope(pre1[...])

    for e in range(2):
        wait(za_buf[e].at[pl.ds(0, S - 1)], recv.at[ZA + e])
    chunks = []
    for e in range(2):
        sums = []
        for o in (0, 1):
            part = za_buf[e][o].astype(F32)
            for t in range(o + 2, S, 2):
                part = part + za_buf[e][t].astype(F32)
            sums.append(part)
        chunks.append(jnp.concatenate(sums, axis=0))
    own_grad = jnp.concatenate(chunks, axis=1)
    uin = ui[...]
    raw_grad = (inv[:, :1] * (own_grad - uin * jnp.sum(uin * own_grad, axis=-1, keepdims=True))).astype(BF)
    rg[...] = raw_grad
    sg = (dot_t(raw_grad, b_buf[...].reshape(G * rows, 512)) * slope2).astype(BF)
    sg_scr[...] = sg
    fg = (dot_t(sg, w2_rows) * slope1).astype(BF)
    g2_send[...] = t_dot(xf_v[...], fg).astype(BF).reshape(G, rows, 128)
    grp_scatter(g2_send, g2_recv, G2)
    q_cols = pl.ds(pl.multiple_of(lax.rem(s, 4) * 128, 128), 128)
    gl_scr[...] = t_dot(h2, rg[:, q_cols]).astype(BF).reshape(C, 2, 2, half, 128)
    gp1[:, :, :rows] = t_dot(h1, sg_scr[:, cols]).astype(BF).reshape(C, 2, rows, 128)
    gp1[:, :, rows:] = gl_scr[:, :, s // 4]
    copy(gp1.at[:, 1 - c], gp1_recv, GP1, sib).start()
    wait(uds_recv, recv.at[UDS])
    udp_send[...] = (ud[c, 1 - par] + uds_recv[1 - par].astype(F32)).astype(BF)
    copy(udp_send, udp_recv, UDP, pair).start()
    wait(gp1_recv, recv.at[GP1])
    g1_send[...] = (gp1[:, c].astype(F32) + gp1_recv[...].astype(F32)).astype(BF)
    chip_scatter(g1_send, g1_recv, G1)

    wait(lg_buf.at[pl.ds(0, G - 1)], recv.at[GL])
    total = jnp.sum(lg_buf[...], axis=0)
    numer = jnp.sum(jnp.where(lane == 0, total, 0.0), axis=1, keepdims=True)
    denom = jnp.sum(jnp.where(lane == 1, total, 0.0), axis=1, keepdims=True)
    loss_ref[...] = jnp.broadcast_to(numer * S / denom, loss_ref.shape)

    wait(g2_recv.at[pl.ds(0, G - 1)], recv.at[G2])
    f2_buf[s] = jnp.sum(g2_recv[...].astype(F32), axis=0).astype(BF)
    z_bcast(f2_buf, F2)
    wait(g1_recv.at[pl.ds(0, C - 1)], recv.at[G1])
    f1_buf[s] = jnp.sum(g1_recv[...].astype(F32), axis=0).astype(BF)
    z_bcast(f1_buf, F1)

    wait(udp_recv, recv.at[UDP])
    user_dir = TEMP * (ud[c, par] + uds_recv[par].astype(F32) + udp_recv[...].astype(F32))
    uun = uu[...]
    ug_ref[...] = uinv[:, :1] * (user_dir - uun * jnp.sum(uun * user_dir, axis=-1, keepdims=True))
    wait(a_buf.at[pl.ds(0, C - 1), 0], send.at[A])
    wait(a2_buf.at[pl.ds(0, C - 1), 0], send.at[A2])
    wait(a2_buf.at[:, 0], send.at[AS2])
    wait(b_buf.at[pl.ds(0, C - 1), 0], send.at[B])
    wait(a_buf.at[:, 0], send.at[AS])
    wait(b_buf.at[:, 0], send.at[BS])
    wait(pe_buf.at[pl.ds(0, C - 1)], send.at[PE])
    wait(rs_recv[1].at[pl.ds(0, C - 1)], send.at[RS + 1])
    for e in range(2):
        wait(za_buf[e].at[pl.ds(0, S - 1)], send.at[ZA + e])
    for buf, i in ((qr_buf, QKV), (at_recv, ATT), (zl_buf, ZL)):
        wait(buf.at[pl.ds(0, S - 1)], send.at[i])
    wait(h1_buf.at[pl.ds(0, S - 1)], send.at[H1])
    wait(h2_buf.at[0], send.at[H2])
    wait(sl2_buf.at[0], send.at[SL2])
    wait(nx_buf.at[pl.ds(0, 3)], send.at[NX])
    wait(neg_buf.at[0], send.at[NG])
    for i in (UP, US, UT):
        wait(u_buf.at[0], send.at[i])
    wait(dn_buf.at[pl.ds(0, 3)], send.at[DN])
    wait(uds_recv, send.at[UDS])
    wait(udp_recv, send.at[UDP])
    wait(gp1_recv, send.at[GP1])
    wait(lg_buf.at[pl.ds(0, G - 1)], send.at[GL])
    wait(g1_recv.at[pl.ds(0, C - 1)], send.at[G1])
    wait(g2_recv.at[pl.ds(0, G - 1)], send.at[G2])
    wait(w2r_buf.at[0], send.at[W2])

    wait(f2_buf.at[pl.ds(0, S - 1)], recv.at[F2])
    for t in range(S):
        gf_ref[:, 128 * t : 128 * (t + 1)] = f2_buf[t].astype(F32)
    wait(f1_buf.at[pl.ds(0, S - 1)], recv.at[F1])
    for t in range(S):
        gm_ref[:, 128 * t : 128 * (t + 1)] = f1_buf[t, :rows].astype(F32)
        gl_ref[half * (t // 4) : half * (t // 4 + 1), 128 * (t % 4) : 128 * (t % 4 + 1)] = f1_buf[t, rows:].astype(F32)
    wait(f1_buf.at[pl.ds(0, S - 1)], send.at[F1])
    wait(f2_buf.at[pl.ds(0, S - 1)], send.at[F2])


def tail(*refs):
    ins, outs, sem = refs[:6], refs[6:12], refs[12]
    for i in (0, 2, 3, 4, 5):
        pltpu.make_async_copy(ins[i], outs[i], sem.at[i]).start()
    outs[1][0, 0] = jnp.max(ins[1][...])
    for i in (0, 2, 3, 4, 5):
        pltpu.make_async_copy(ins[i], outs[i], sem.at[i]).wait()


def local(history, lengths, next_items, negatives, input_weight, output_weight, pool_features,
          tower_first, tower_middle, tower_last, S, G):
    events = history[0]
    tok = events.shape[0]
    C = G // 2
    R = pool_features.shape[0]
    RH = R // 2
    rows = tower_first.shape[0]
    V = pltpu.VMEM
    vmem = pl.BlockSpec(memory_space=pltpu.VMEM)
    hbm = pl.BlockSpec(memory_space=pltpu.HBM)
    scratch = [
        pltpu.SemaphoreType.DMA((N_SEM,)),
        pltpu.SemaphoreType.DMA((N_SEM,)),
        pltpu.SemaphoreType.DMA((N_HERE,)),
        V((tok, 512), BF),
        V((4, 1, tok), jnp.int32),
        V((2, 1, negatives.shape[1] + 128), jnp.int32),
        V(input_weight.shape, BF),
        V(output_weight.shape, BF),
        V(pool_features.shape, BF),
        V((C, 2, rows, 128), BF),
        V((C, 2, 4, rows, 128), BF),
        V((C, 2, rows, 512), BF),
        V((2, 128 // (2 * rows), 2, 4, rows, 128), BF),
        V((S, tok + tok // 2, 128), BF),
        V((S, tok + tok // 2, 128), BF),
        V((tok, 512), BF),
        V((S * tok, DH), BF),
        V((S * tok, DH), BF),
        V((S * tok, DH), BF),
        V((S, tok // 2, 128), BF),
        V((S, tok // 2, 128), BF),
        V((S, R, 128), BF),
        V((2, 4, R, 128), BF),
        V((2, 4, R, 128), BF),
        V((R, 128), F32),
        V((R, 512), F32),
        V((R, 128), F32),
        V((C, RH, 512), BF),
        V((2, C * RH, 2 * tok), F32),
        V((2, C * RH, 2 * tok), BF),
        V((4, tok, 512), BF),
        V((4, 2, 1, 4 * tok), F32),
        V((2, 1, 2 * tok), F32),
        V((2, 2, tok, 512), F32),
        V((2, tok, 512), BF),
        V((2, tok, 512), BF),
        V((tok, 512), BF),
        V((tok, 512), BF),
        V((S, 8, 128), F32),
        V((G, 8, 128), F32),
        V((R, 512), BF),
        V((R, 1024), BF),
        V((C, 2, 2, rows // 2, 128), BF),
        V((C, 2, rows + rows // 2, 128), BF),
        V((C, rows + rows // 2, 128), BF),
        V((C, rows + rows // 2, 128), BF),
        V((C, rows + rows // 2, 128), BF),
        V((G, rows, 128), BF),
        V((G, rows, 128), BF),
        V((S, rows + rows // 2, 128), BF),
        V((S, rows, 128), BF),
        V((2, C * RH, 128), F32),
        V((tok, 512), F32),
        V((tok, 128), F32),
    ]
    for lead in (C, C, S):
        scratch += [V((lead, RH, n), BF) for _, n in PARTS]
    shapes = [
        jax.ShapeDtypeStruct((tok, 512), BF),
        jax.ShapeDtypeStruct((8, 128), F32),
        jax.ShapeDtypeStruct((tok, 512), F32),
        jax.ShapeDtypeStruct((rows, 1024), F32),
        jax.ShapeDtypeStruct((rows, 1024), F32),
        jax.ShapeDtypeStruct((rows, 512), F32),
    ]
    results = pl.pallas_call(
        functools.partial(kernel, S, G),
        out_shape=[pltpu.VMEM(x.shape, x.dtype) for x in shapes],
        in_specs=[pl.BlockSpec(memory_space=pltpu.SMEM)] + [hbm] * 9,
        out_specs=[vmem] * 6,
        scratch_shapes=scratch,
        compiler_params=pltpu.CompilerParams(
            collective_id=0, has_side_effects=True, vmem_limit_bytes=56 * 1024 * 1024),
    )(lengths, events, next_items, negatives, input_weight, output_weight, pool_features,
      tower_first, tower_middle, tower_last)
    lo, loss, ug, gf, gm, gl = pl.pallas_call(
        tail,
        out_shape=shapes[:1] + [jax.ShapeDtypeStruct((1, 1), F32)] + shapes[2:],
        in_specs=[vmem] * 6,
        out_specs=[hbm, pl.BlockSpec(memory_space=pltpu.SMEM)] + [hbm] * 4,
        scratch_shapes=[pltpu.SemaphoreType.DMA((6,))],
        compiler_params=pltpu.CompilerParams(vmem_limit_bytes=1024 * 1024),
    )(*results)
    return lo[None], loss.reshape(()), ug[None], gf, gm, gl


def solution(mesh):
    placed = (
        P("grp", "seq", None), P("grp"), P("grp", "seq"), P("grp", None), P(), P(),
        P("grp", None), P("grp", None), P("grp", None), P("grp", None),
    )
    return jax.shard_map(
        functools.partial(local, S=mesh.shape["seq"], G=mesh.shape["grp"]),
        mesh=mesh,
        in_specs=placed,
        out_specs=(
            P("grp", "seq", None), P(), P("grp", "seq", None),
            P("grp", None), P("grp", None), P("grp", None),
        ),
        check_vma=False,
    )
```

```python
import functools

import jax
import jax.numpy as jnp
from jax import lax
from jax.experimental import pallas as pl
from jax.experimental.pallas import tpu as pltpu
from jax.sharding import PartitionSpec as P

DH = 64
EPS_NORM = 1e-05
EPS_UNIT = 1e-06
TEMP = 20.0

MESH = pl.DeviceIdType.MESH
BF = jnp.bfloat16
F32 = jnp.float32

(A, A2, B, AS, AS2, BS, QKV, ATT, H1, H2, SL2, NX, NG, UP, US, UT, DN, UDS, UDP, ZL, GL, GP1, G1, G2, F1, F2,
 W2, PE) = range(28)
RS, ZA = 28, 30
N_SEM = 32

PARTS = ((0, 256), (256, 256))

(I_W3, I_H, I_WIN, I_WOUT, I_X, I_NEG, I_NXT, I_W1) = range(8)
I_W2 = 8
N_HERE = 12


def silu(x):
    half = 0.5 * x
    return half * (1.0 + jnp.tanh(half))


def silu_slope(z):
    sigma = 0.5 * (1.0 + jnp.tanh(0.5 * z))
    return sigma * (1.0 + z * (1.0 - sigma))


def layer_norm(values):
    center = values - jnp.mean(values, axis=-1, keepdims=True)
    spread = jnp.mean(center * center, axis=-1, keepdims=True)
    return center * lax.rsqrt(spread + EPS_NORM)


def dot(a, b):
    return jnp.dot(a, b, preferred_element_type=F32)


def dot_t(a, b):
    return lax.dot_general(a, b, (((1,), (1,)), ((), ())), preferred_element_type=F32)


def t_dot(a, b):
    return lax.dot_general(a, b, (((0,), (0,)), ((), ())), preferred_element_type=F32)


def wait(ref, sem):
    pltpu.make_async_copy(ref, ref, sem).wait()


def kernel(
    S, G,
    len_ref, hist, nxt, neg, win, wout, xf, w1, w2, w3,
    lo_ref, loss_ref, ug_ref, gf_ref, gm_ref, gl_ref,
    send, recv, here,
    hist_v, nx_buf, neg_buf, win_v, wout_v, xf_v,
    a_buf, a2_buf, b_buf, w2r_buf, qs_buf, qr_buf, gate, k_scr, q_scr, v_scr, at_send, at_recv,
    h1_buf, h2_buf, sl2_buf, pre1, ui, inv, pe_buf, em, st, u_buf,
    dn_buf, nll, ud, uds_send, uds_recv, udp_send, udp_recv, zl_buf, lg_buf, rg, sg_scr,
    gl_scr, gp1, gp1_recv, g1_send, g1_recv, g2_send, g2_recv, f1_buf, f2_buf, cnt, uu, uinv, *parts,
):
    C = G // 2
    s = lax.axis_index("seq")
    g = lax.axis_index("grp")
    p = g // 2
    c = g % 2
    par = s % 2
    tok = hist_v.shape[0]
    me = 2 * c + par
    rows = b_buf.shape[2]
    NB = a2_buf.shape[2]
    half = rows // 2
    NEG = neg.shape[1]
    R = xf_v.shape[0]
    RH = R // 2
    length = len_ref[0]
    pair = (s + 1 - 2 * par, g)
    sib = (s, 2 * p + 1 - c)
    diag = (s + 1 - 2 * par, 2 * p + 1 - c)
    cols = pl.ds(pl.multiple_of(s * 128, 128), 128)

    def copy(src, dst, i, dev):
        return pltpu.make_async_remote_copy(
            src_ref=src, dst_ref=dst, send_sem=send.at[i], recv_sem=recv.at[i],
            device_id=dev, device_id_type=MESH)

    def fetch(src, dst, i):
        pltpu.make_async_copy(src, dst, here.at[i]).start()

    def z_away(i):
        return lax.rem(s + S // 2 + (1 - 2 * (i % 2)) * ((i + 1) // 2), S)

    def z_bcast(buf, i):
        def step(k, _):
            copy(buf.at[s], buf.at[s], i, (z_away(k), g)).start()
            return 0
        lax.fori_loop(0, S - 1, step, 0)

    def chip_away(k):
        return (p // 4 + 2 + k // 4) % 4 * 4 + (p + 2 + k) % 4

    def each_chip(step):
        lax.fori_loop(0, 10, step, 0)
        lax.fori_loop(11, 16, step, 0)

    def chips(src, dst, i):
        def step(k, _):
            copy(src, dst, i, (s, 2 * chip_away(k) + c)).start()
            return 0
        each_chip(step)

    def chip_scatter(src, dst, i):
        def step(k, _):
            t = chip_away(k)
            copy(src.at[t], dst.at[p], i, (s, 2 * t + c)).start()
            return 0
        each_chip(step)
        dst[p] = src[p]

    rs_send, rs_recv, za_buf = parts[0:2], parts[2:4], parts[4:6]

    def grp_scatter(src, dst, i):
        def step(k, _):
            t = lax.rem(g + k, G)
            copy(src.at[t], dst.at[g], i, (s, t)).start()
            return 0
        lax.fori_loop(1, G, step, 0)
        dst[g] = src[g]

    def quad(buf, i):
        for dev in (sib, pair, diag):
            copy(buf.at[me], buf.at[me], i, dev).start()

    fetch(w1.at[:, cols], a_buf.at[p, c], I_W1)
    barrier = pltpu.get_barrier_semaphore()

    def greet_grp(k, _):
        pl.semaphore_signal(barrier, inc=1, device_id=(s, lax.rem(g + k, G)), device_id_type=MESH)
        return 0

    def greet_seq(k, _):
        pl.semaphore_signal(barrier, inc=1, device_id=(lax.rem(s + k, S), g), device_id_type=MESH)
        return 0

    lax.fori_loop(1, G, greet_grp, 0)
    lax.fori_loop(1, S, greet_seq, 0)
    pl.semaphore_signal(barrier, inc=1, device_id=diag, device_id_type=MESH)

    for j in range(NB):
        block = pl.ds(pl.multiple_of((2 * j + par) * 128, 128), 128)
        fetch(w2.at[:, block], a2_buf.at[p, c, j], I_W2 + j)
    fetch(hist, hist_v, I_H)
    fetch(win, win_v, I_WIN)
    fetch(nxt, nx_buf.at[me], I_NXT)
    fetch(w3, b_buf.at[p, c], I_W3)
    fetch(xf, xf_v, I_X)
    fetch(neg, neg_buf.at[c, :, pl.ds(0, NEG)], I_NEG)
    fetch(wout, wout_v, I_WOUT)
    neg_buf[c, :, NEG:] = jnp.full((1, 128), length, jnp.int32)
    wait(a_buf.at[p, c], here.at[I_W1])
    pl.semaphore_wait(barrier, (G - 1) + (S - 1) + 1)
    chips(a_buf.at[p, c], a_buf.at[p, c], A)

    wait(hist_v, here.at[I_H])
    normed = layer_norm(hist_v[...].astype(F32)).astype(BF)
    wait(win_v, here.at[I_WIN])
    for j in range(4):
        x = silu(dot(normed, win_v[:, 512 + 384 * j : 512 + 384 * (j + 1)])).astype(BF)
        for e in (0, 1):
            o = 192 * e
            qs_buf[2 * j + e, :tok] = x[:, o : o + 128]
            v = x[:, o + 128 : o + 192]
            qs_buf[2 * j + e, tok:] = jnp.concatenate([v[: tok // 2], v[tok // 2 :]], axis=1)

    def qkv_step(k, _):
        t = z_away(k)
        copy(qs_buf.at[t], qr_buf.at[s], QKV, (t, g)).start()
        return 0

    lax.fori_loop(0, S - 1, qkv_step, 0)
    qr_buf[s] = qs_buf[s]
    for j in range(NB):
        wait(a2_buf.at[p, c, j], here.at[I_W2 + j])
    chips(a2_buf.at[p, c], a2_buf.at[p, c], A2)
    wait(nx_buf.at[me], here.at[I_NXT])
    quad(nx_buf, NX)
    wait(neg_buf.at[c, :, pl.ds(0, NEG)], here.at[I_NEG])
    copy(neg_buf.at[c], neg_buf.at[c], NG, sib).start()
    gate[...] = silu(dot(normed, win_v[:, :512])).astype(BF)

    wait(xf_v, here.at[I_X])
    wait(a_buf.at[pl.ds(0, C - 1), 0], recv.at[A])
    copy(a_buf.at[:, c], a_buf.at[:, c], AS, sib).start()
    wait(b_buf.at[p, c], here.at[I_W3])
    chips(b_buf.at[p, c], b_buf.at[p, c], B)
    wait(a_buf.at[:, 0], recv.at[AS])
    z1 = dot(xf_v[...], a_buf[...].reshape(G * rows, 128))
    pre1[...] = z1
    h1_buf[s] = silu(z1).astype(BF)
    z_bcast(h1_buf, H1)

    def local_row(ids):
        return jnp.where((ids // RH) % 4 == me, (ids // (2 * R)) * RH + ids % RH, -1)

    wait(neg_buf.at[0], recv.at[NG])
    n_rows = C * RH
    for e in (0, 1):
        ids = local_row(neg_buf[e, :, :NEG])
        hot = (lax.broadcasted_iota(jnp.int32, (n_rows, NEG), 0) == ids).astype(F32).astype(BF)
        cnt[e] = dot(hot, jnp.ones((NEG, 128), BF))
    def whole(buf):
        return jnp.concatenate([buf[j % 2, j // 2] for j in range(2 * NB)], axis=1)

    wait(a2_buf.at[pl.ds(0, C - 1), 0], recv.at[A2])
    copy(a2_buf.at[:, c], a2_buf.at[:, c], AS2, sib).start()
    wait(qr_buf.at[pl.ds(0, S - 1)], recv.at[QKV])
    for j in range(S):
        x = qr_buf[j]
        q_scr[tok * j : tok * (j + 1)] = x[:tok, :DH]
        k_scr[tok * j : tok * (j + 1)] = x[:tok, DH:]
        v_scr[tok * j : tok * (j + 1)] = jnp.concatenate([x[tok:, :DH], x[tok:, DH:]], axis=0)

    inv_len = 1.0 / jnp.full((1, 1), length, jnp.int32).astype(F32)
    W = 2 * tok

    def attend(b):
        q = q_scr[W * b : W * (b + 1)]
        acc = jnp.zeros((W, DH), F32)
        for kb in range(b + 1):
            hs = dot_t(q, k_scr[W * kb : W * (kb + 1)]) * (0.5 * DH ** (-0.5))
            w = (hs * inv_len) * (1.0 + jnp.tanh(hs))
            if kb == b:
                r = lax.broadcasted_iota(jnp.int32, (W, W), 0)
                cc = lax.broadcasted_iota(jnp.int32, (W, W), 1)
                w = jnp.where(cc <= r, w, 0.0)
            acc = acc + dot(w.astype(BF), v_scr[W * kb : W * (kb + 1)])
        pos = W * b + lax.broadcasted_iota(jnp.int32, (W, 1), 0)
        acc = jnp.where(pos < length, acc, 0.0).astype(BF)
        for i in (0, 1):
            o = acc[tok * i : tok * (i + 1)]
            at_send[2 * b + i] = jnp.concatenate([o[: tok // 2], o[tok // 2 :]], axis=1)

    for b in reversed(range(S // 2)):
        attend(b)
    at_recv[s] = at_send[s]

    def at_step(k, _):
        t = z_away(k)
        copy(at_send.at[t], at_recv.at[s], ATT, (t, g)).start()
        return 0

    lax.fori_loop(0, S - 1, at_step, 0)
    wait(h1_buf.at[pl.ds(0, S - 1)], recv.at[H1])
    wait(a2_buf.at[:, 0], recv.at[AS2])
    h1 = jnp.concatenate([h1_buf[j] for j in range(S)], axis=1)
    for j in range(NB):
        z2 = dot(h1, a2_buf[:, :, j].reshape(G * rows, 128))
        h2_buf[par, j] = silu(z2).astype(BF)
        sl2_buf[par, j] = silu_slope(z2).astype(BF)
    copy(h2_buf.at[par], h2_buf.at[par], H2, pair).start()

    wait(b_buf.at[pl.ds(0, C - 1), 0], recv.at[B])
    copy(b_buf.at[:, c], b_buf.at[:, c], BS, sib).start()

    wait(h2_buf.at[0], recv.at[H2])
    wait(b_buf.at[:, 0], recv.at[BS])
    h2 = whole(h2_buf)
    raw = dot(h2, b_buf[...].reshape(G * rows, 512))
    item_inverse = lax.rsqrt(jnp.sum(raw * raw, axis=-1, keepdims=True) + EPS_UNIT)
    unit_item = raw * item_inverse
    ui[...] = unit_item
    inv[...] = jnp.broadcast_to(item_inverse, inv.shape)
    pe_buf[p] = ui[pl.ds(pl.multiple_of(par * RH, RH), RH)].astype(BF)
    chips(pe_buf.at[p], pe_buf.at[p], PE)

    wait(wout_v, here.at[I_WOUT])
    wait(at_recv.at[pl.ds(0, S - 1)], recv.at[ATT])
    tops, bottoms = [], []
    for h in range(S):
        x = at_recv[h]
        tops.append(x[:, :DH])
        bottoms.append(x[:, DH:])
    merged = jnp.concatenate(
        [jnp.concatenate(tops, axis=1), jnp.concatenate(bottoms, axis=1)], axis=0).astype(F32)
    branch = (layer_norm(merged) * gate[...].astype(F32)).astype(BF)
    layer_out = (hist_v[...].astype(F32) + dot(branch, wout_v[...])).astype(BF)
    lo_ref[...] = layer_out
    outward = layer_out.astype(F32)
    user_inverse = lax.rsqrt(jnp.sum(outward * outward, axis=-1, keepdims=True) + EPS_UNIT)
    unit_user = outward * user_inverse
    u_buf[me] = unit_user.astype(BF)
    copy(u_buf.at[me], u_buf.at[me], UP, pair).start()
    copy(u_buf.at[me], u_buf.at[me], US, sib).start()
    uu[...] = unit_user
    uinv[...] = jnp.broadcast_to(user_inverse, (tok, 128))

    wait(nx_buf.at[pl.ds(0, 3)], recv.at[NX])
    pair_pos = lax.broadcasted_iota(jnp.int32, (1, W), 1)
    positions = (s // 2) * W + pair_pos

    def items_of(u):
        return local_row(jnp.concatenate([nx_buf[2 * u], nx_buf[2 * u + 1]], axis=1))

    def valid_of(u):
        lens = neg_buf[u, :, NEG:]
        return (positions < jnp.concatenate([lens, lens], axis=1) - 1).astype(F32)

    wait(u_buf.at[0], recv.at[UP])
    other = 2 * c + 1 - par
    copy(u_buf.at[other], u_buf.at[other], UT, sib).start()
    wait(pe_buf.at[pl.ds(0, C - 1)], recv.at[PE])

    Q = 4
    CQ = C // Q
    width = n_rows // Q
    row_id = lax.broadcasted_iota(jnp.int32, (width, W), 0)

    def logits_of(u):
        users = u_buf[pl.ds(2 * u, 2)].reshape(W, 512)
        items = items_of(u)
        den = jnp.zeros((1, W), F32)
        positive = jnp.zeros((1, W), F32)
        for q in range(Q):
            logit = TEMP * dot_t(pe_buf[CQ * q : CQ * (q + 1)].reshape(width, 512), users)
            own = row_id + width * q == items
            times = cnt[u, width * q : width * (q + 1)]
            e = jnp.where(own, 0.0, jnp.exp(logit) * jnp.concatenate([times, times], axis=1))
            em[u, width * q : width * (q + 1)] = e
            den = den + jnp.sum(e, axis=0, keepdims=True)
            positive = positive + jnp.sum(jnp.where(own, logit, 0.0), axis=0, keepdims=True)
        dn_buf[me, u] = jnp.concatenate([den, positive], axis=1)

    logits_of(c)
    wait(u_buf.at[0], recv.at[US])
    wait(u_buf.at[0], recv.at[UT])
    logits_of(1 - c)
    quad(dn_buf, DN)
    wait(dn_buf.at[pl.ds(0, 3)], recv.at[DN])
    for u in (0, 1):
        sums = dn_buf[0, u] + dn_buf[1, u] + dn_buf[2, u] + dn_buf[3, u]
        positive = sums[:, W:]
        positive_exp = jnp.exp(positive)
        den = sums[:, :W] + positive_exp
        valid = valid_of(u)
        items = items_of(u)
        slope = valid * (positive_exp / den - 1.0)
        scale = valid / den
        for q in range(Q):
            block = slice(width * q, width * (q + 1))
            st[u, block] = jnp.where(row_id + width * q == items, slope, scale * em[u, block]).astype(BF)
        nll[u] = valid * (jnp.log(den) - positive)

    def pool_part(e):
        lo, n = PARTS[e]
        part = dot(st[0], u_buf[0:2, :, lo : lo + n].reshape(W, n))
        part = part + dot(st[1], u_buf[2:4, :, lo : lo + n].reshape(W, n))
        rs_send[e][...] = (TEMP * part).astype(BF).reshape(C, RH, n)

    pool_part(0)
    chip_scatter(rs_send[0], rs_recv[0], RS)

    per_block = 128 // (2 * rows)
    copy(a2_buf.at[pl.ds(per_block * (s + 1 - 2 * par), per_block)], w2r_buf.at[par], W2, pair).start()
    w2r_buf[par] = a2_buf[pl.ds(per_block * s, per_block)]
    copy(sl2_buf.at[par], sl2_buf.at[par], SL2, pair).start()

    mine = pair_pos // tok == par
    loss_sum = jnp.sum(jnp.where(mine, nll[c], 0.0))
    lane = lax.broadcasted_iota(jnp.int32, (8, 128), 1)
    count = jnp.full((8, 128), length - 1, jnp.int32).astype(F32)
    zl_buf[s] = jnp.where(lane == 0, loss_sum, jnp.where(lane == 1, count, 0.0))
    z_bcast(zl_buf, ZL)

    rows_here = pe_buf[...].reshape(n_rows, 512)
    for u in (0, 1):
        ud[u] = t_dot(st[u], rows_here).reshape(2, tok, 512)
    uds_send[...] = ud[1 - c].astype(BF)
    copy(uds_send, uds_recv, UDS, sib).start()

    pool_part(1)
    wait(rs_recv[0].at[pl.ds(0, C - 1)], send.at[RS])
    chip_scatter(rs_send[1], rs_recv[1], RS + 1)

    def plane_sum(e):
        wait(rs_recv[e].at[pl.ds(0, C - 1)], recv.at[RS + e])
        za_buf[e][s] = jnp.sum(rs_recv[e][...].astype(F32), axis=0).astype(BF)
        z_bcast(za_buf[e], ZA + e)

    plane_sum(0)
    plane_sum(1)
    wait(zl_buf.at[pl.ds(0, S - 1)], recv.at[ZL])
    lg_buf[g] = jnp.sum(zl_buf[...], axis=0)

    def lg_step(k, _):
        copy(lg_buf.at[g], lg_buf.at[g], GL, (s, lax.rem(g + k, G))).start()
        return 0

    lax.fori_loop(1, G, lg_step, 0)
    wait(w2r_buf.at[0], recv.at[W2])
    w2_rows = jnp.concatenate([w2r_buf[j % 2, :, :, j // 2].reshape(128, 128) for j in range(2 * NB)], axis=1)
    wait(sl2_buf.at[0], recv.at[SL2])
    h1 = jnp.concatenate([h1_buf[j] for j in range(S)], axis=1)
    h2 = whole(h2_buf)
    slope2 = whole(sl2_buf).astype(F32)
    slope1 = silu_slope(pre1[...])

    for e in range(2):
        wait(za_buf[e].at[pl.ds(0, S - 1)], recv.at[ZA + e])
    chunks = []
    for e in range(2):
        sums = []
        for o in (0, 1):
            part = za_buf[e][o].astype(F32)
            for t in range(o + 2, S, 2):
                part = part + za_buf[e][t].astype(F32)
            sums.append(part)
        chunks.append(jnp.concatenate(sums, axis=0))
    own_grad = jnp.concatenate(chunks, axis=1)
    uin = ui[...]
    raw_grad = (inv[:, :1] * (own_grad - uin * jnp.sum(uin * own_grad, axis=-1, keepdims=True))).astype(BF)
    rg[...] = raw_grad
    sg = (dot_t(raw_grad, b_buf[...].reshape(G * rows, 512)) * slope2).astype(BF)
    sg_scr[...] = sg
    fg = (dot_t(sg, w2_rows) * slope1).astype(BF)
    g2_send[...] = t_dot(xf_v[...], fg).astype(BF).reshape(G, rows, 128)
    grp_scatter(g2_send, g2_recv, G2)
    q_cols = pl.ds(pl.multiple_of(lax.rem(s, 4) * 128, 128), 128)
    gl_scr[...] = t_dot(h2, rg[:, q_cols]).astype(BF).reshape(C, 2, 2, half, 128)
    gp1[:, :, :rows] = t_dot(h1, sg_scr[:, cols]).astype(BF).reshape(C, 2, rows, 128)
    gp1[:, :, rows:] = gl_scr[:, :, s // 4]
    copy(gp1.at[:, 1 - c], gp1_recv, GP1, sib).start()
    wait(uds_recv, recv.at[UDS])
    udp_send[...] = (ud[c, 1 - par] + uds_recv[1 - par].astype(F32)).astype(BF)
    copy(udp_send, udp_recv, UDP, pair).start()
    wait(gp1_recv, recv.at[GP1])
    g1_send[...] = (gp1[:, c].astype(F32) + gp1_recv[...].astype(F32)).astype(BF)
    chip_scatter(g1_send, g1_recv, G1)

    wait(lg_buf.at[pl.ds(0, G - 1)], recv.at[GL])
    total = jnp.sum(lg_buf[...], axis=0)
    numer = jnp.sum(jnp.where(lane == 0, total, 0.0), axis=1, keepdims=True)
    denom = jnp.sum(jnp.where(lane == 1, total, 0.0), axis=1, keepdims=True)
    loss_ref[...] = jnp.broadcast_to(numer * S / denom, loss_ref.shape)

    wait(g2_recv.at[pl.ds(0, G - 1)], recv.at[G2])
    f2_buf[s] = jnp.sum(g2_recv[...].astype(F32), axis=0).astype(BF)
    z_bcast(f2_buf, F2)
    wait(g1_recv.at[pl.ds(0, C - 1)], recv.at[G1])
    f1_buf[s] = jnp.sum(g1_recv[...].astype(F32), axis=0).astype(BF)
    z_bcast(f1_buf, F1)

    wait(udp_recv, recv.at[UDP])
    user_dir = TEMP * (ud[c, par] + uds_recv[par].astype(F32) + udp_recv[...].astype(F32))
    uun = uu[...]
    ug_ref[...] = uinv[:, :1] * (user_dir - uun * jnp.sum(uun * user_dir, axis=-1, keepdims=True))
    wait(a_buf.at[pl.ds(0, C - 1), 0], send.at[A])
    wait(a2_buf.at[pl.ds(0, C - 1), 0], send.at[A2])
    wait(a2_buf.at[:, 0], send.at[AS2])
    wait(b_buf.at[pl.ds(0, C - 1), 0], send.at[B])
    wait(a_buf.at[:, 0], send.at[AS])
    wait(b_buf.at[:, 0], send.at[BS])
    wait(pe_buf.at[pl.ds(0, C - 1)], send.at[PE])
    wait(rs_recv[1].at[pl.ds(0, C - 1)], send.at[RS + 1])
    for e in range(2):
        wait(za_buf[e].at[pl.ds(0, S - 1)], send.at[ZA + e])
    for buf, i in ((qr_buf, QKV), (at_recv, ATT), (zl_buf, ZL)):
        wait(buf.at[pl.ds(0, S - 1)], send.at[i])
    wait(h1_buf.at[pl.ds(0, S - 1)], send.at[H1])
    wait(h2_buf.at[0], send.at[H2])
    wait(sl2_buf.at[0], send.at[SL2])
    wait(nx_buf.at[pl.ds(0, 3)], send.at[NX])
    wait(neg_buf.at[0], send.at[NG])
    for i in (UP, US, UT):
        wait(u_buf.at[0], send.at[i])
    wait(dn_buf.at[pl.ds(0, 3)], send.at[DN])
    wait(uds_recv, send.at[UDS])
    wait(udp_recv, send.at[UDP])
    wait(gp1_recv, send.at[GP1])
    wait(lg_buf.at[pl.ds(0, G - 1)], send.at[GL])
    wait(g1_recv.at[pl.ds(0, C - 1)], send.at[G1])
    wait(g2_recv.at[pl.ds(0, G - 1)], send.at[G2])
    wait(w2r_buf.at[0], send.at[W2])

    wait(f2_buf.at[pl.ds(0, S - 1)], recv.at[F2])
    for t in range(S):
        gf_ref[:, 128 * t : 128 * (t + 1)] = f2_buf[t].astype(F32)
    wait(f1_buf.at[pl.ds(0, S - 1)], recv.at[F1])
    for t in range(S):
        gm_ref[:, 128 * t : 128 * (t + 1)] = f1_buf[t, :rows].astype(F32)
        gl_ref[half * (t // 4) : half * (t // 4 + 1), 128 * (t % 4) : 128 * (t % 4 + 1)] = f1_buf[t, rows:].astype(F32)
    wait(f1_buf.at[pl.ds(0, S - 1)], send.at[F1])
    wait(f2_buf.at[pl.ds(0, S - 1)], send.at[F2])


def tail(*refs):
    ins, outs, sem = refs[:6], refs[6:12], refs[12]
    for i in (0, 2, 3, 4, 5):
        pltpu.make_async_copy(ins[i], outs[i], sem.at[i]).start()
    outs[1][0, 0] = jnp.max(ins[1][...])
    for i in (0, 2, 3, 4, 5):
        pltpu.make_async_copy(ins[i], outs[i], sem.at[i]).wait()


def local(history, lengths, next_items, negatives, input_weight, output_weight, pool_features,
          tower_first, tower_middle, tower_last, S, G):
    events = history[0]
    tok = events.shape[0]
    C = G // 2
    R = pool_features.shape[0]
    RH = R // 2
    rows = tower_first.shape[0]
    V = pltpu.VMEM
    vmem = pl.BlockSpec(memory_space=pltpu.VMEM)
    hbm = pl.BlockSpec(memory_space=pltpu.HBM)
    scratch = [
        pltpu.SemaphoreType.DMA((N_SEM,)),
        pltpu.SemaphoreType.DMA((N_SEM,)),
        pltpu.SemaphoreType.DMA((N_HERE,)),
        V((tok, 512), BF),
        V((4, 1, tok), jnp.int32),
        V((2, 1, negatives.shape[1] + 128), jnp.int32),
        V(input_weight.shape, BF),
        V(output_weight.shape, BF),
        V(pool_features.shape, BF),
        V((C, 2, rows, 128), BF),
        V((C, 2, 4, rows, 128), BF),
        V((C, 2, rows, 512), BF),
        V((2, 128 // (2 * rows), 2, 4, rows, 128), BF),
        V((S, tok + tok // 2, 128), BF),
        V((S, tok + tok // 2, 128), BF),
        V((tok, 512), BF),
        V((S * tok, DH), BF),
        V((S * tok, DH), BF),
        V((S * tok, DH), BF),
        V((S, tok // 2, 128), BF),
        V((S, tok // 2, 128), BF),
        V((S, R, 128), BF),
        V((2, 4, R, 128), BF),
        V((2, 4, R, 128), BF),
        V((R, 128), F32),
        V((R, 512), F32),
        V((R, 128), F32),
        V((C, RH, 512), BF),
        V((2, C * RH, 2 * tok), F32),
        V((2, C * RH, 2 * tok), BF),
        V((4, tok, 512), BF),
        V((4, 2, 1, 4 * tok), F32),
        V((2, 1, 2 * tok), F32),
        V((2, 2, tok, 512), F32),
        V((2, tok, 512), BF),
        V((2, tok, 512), BF),
        V((tok, 512), BF),
        V((tok, 512), BF),
        V((S, 8, 128), F32),
        V((G, 8, 128), F32),
        V((R, 512), BF),
        V((R, 1024), BF),
        V((C, 2, 2, rows // 2, 128), BF),
        V((C, 2, rows + rows // 2, 128), BF),
        V((C, rows + rows // 2, 128), BF),
        V((C, rows + rows // 2, 128), BF),
        V((C, rows + rows // 2, 128), BF),
        V((G, rows, 128), BF),
        V((G, rows, 128), BF),
        V((S, rows + rows // 2, 128), BF),
        V((S, rows, 128), BF),
        V((2, C * RH, 128), F32),
        V((tok, 512), F32),
        V((tok, 128), F32),
    ]
    for lead in (C, C, S):
        scratch += [V((lead, RH, n), BF) for _, n in PARTS]
    shapes = [
        jax.ShapeDtypeStruct((tok, 512), BF),
        jax.ShapeDtypeStruct((8, 128), F32),
        jax.ShapeDtypeStruct((tok, 512), F32),
        jax.ShapeDtypeStruct((rows, 1024), F32),
        jax.ShapeDtypeStruct((rows, 1024), F32),
        jax.ShapeDtypeStruct((rows, 512), F32),
    ]
    results = pl.pallas_call(
        functools.partial(kernel, S, G),
        out_shape=[pltpu.VMEM(x.shape, x.dtype) for x in shapes],
        in_specs=[pl.BlockSpec(memory_space=pltpu.SMEM)] + [hbm] * 9,
        out_specs=[vmem] * 6,
        scratch_shapes=scratch,
        compiler_params=pltpu.CompilerParams(
            collective_id=0, has_side_effects=True, vmem_limit_bytes=56 * 1024 * 1024),
    )(lengths, events, next_items, negatives, input_weight, output_weight, pool_features,
      tower_first, tower_middle, tower_last)
    lo, loss, ug, gf, gm, gl = pl.pallas_call(
        tail,
        out_shape=shapes[:1] + [jax.ShapeDtypeStruct((1, 1), F32)] + shapes[2:],
        in_specs=[vmem] * 6,
        out_specs=[hbm, pl.BlockSpec(memory_space=pltpu.SMEM)] + [hbm] * 4,
        scratch_shapes=[pltpu.SemaphoreType.DMA((6,))],
        compiler_params=pltpu.CompilerParams(vmem_limit_bytes=1024 * 1024),
    )(*results)
    return lo[None], loss.reshape(()), ug[None], gf, gm, gl


def solution(mesh):
    placed = (
        P("grp", "seq", None), P("grp"), P("grp", "seq"), P("grp", None), P(), P(),
        P("grp", None), P("grp", None), P("grp", None), P("grp", None),
    )
    return jax.shard_map(
        functools.partial(local, S=mesh.shape["seq"], G=mesh.shape["grp"]),
        mesh=mesh,
        in_specs=placed,
        out_specs=(
            P("grp", "seq", None), P(), P("grp", "seq", None),
            P("grp", None), P("grp", None), P("grp", None),
        ),
        check_vma=False,
    )
```
